32 devices in a mesh: dp: 8 (over y, x, core), rows: 4 (over z).
Axes of the slice: x: 2, y: 2, z: 4, core: 2. Of those that a mesh axis runs over, the one named last changes fastest.
Arguments:
- features: bfloat16 [8, 36, 48, 2048], P('dp', 'rows'), may hold values from -6 to 6
- extent: int32 [8, 2], P('dp'), may hold values from 18 to 48, as said below
- pointwise_weight: bfloat16 [2048, 256], P('dp', 'rows'), may hold values from -0.125 to 0.125
- pooling_weight: bfloat16 [2048, 256], P('dp', 'rows'), may hold values from -0.125 to 0.125
- dilated_weight: bfloat16 [55296, 256], P('dp', 'rows'), may hold values from -0.046875 to 0.046875
- projection_weight: bfloat16 [1280, 256], P('dp', 'rows'), may hold values from -0.15625 to 0.15625
- norm_gain: float32 [6, 256], replicated, may hold values from 0.5 to 1.5
- norm_bias: float32 [6, 256], replicated, may hold values from -3 to 3
- cotangent: bfloat16 [8, 36, 48, 256], P('dp', 'rows'), may hold values from -6 to 6
Outputs:
- output: bfloat16 [8, 36, 48, 256], P('dp', 'rows')
- feature_input_gradient: bfloat16 [8, 36, 48, 2048], P('dp', 'rows')
- pointwise_gradient: float32 [2048, 256], P('dp', 'rows')
- pooling_gradient: float32 [2048, 256], P('dp', 'rows')
- dilated_gradient: float32 [55296, 256], P('dp', 'rows')
- projection_gradient: float32 [1280, 256], P('dp', 'rows')
- norm_gain_gradient: float32 [6, 256], replicated
- norm_bias_gradient: float32 [6, 256], replicated
The draws below stay inside these ranges and needn't reach their ends.
Inputs may be any that keep to these rules, and one draw needn't show every extreme that they name: `extent`: column 0 lies between 18 and 36, column 1 between 24 and 48; the first image fills its whole frame and the last has exactly 18 rows and 24 columns.
All inputs are finite; a program needn't handle non-finite values.
Results may differ from the reference program's by a relative error of at most 0.015.
Values may be sent and summed in bfloat16 or wider, within the bound.
No kernel may reach another device: no remote copies, remote signals or barrier semaphores. Data moves between devices by JAX's collectives and lax.ppermute only.
A program may use at most 384 MiB of HBM per device.

```python
import jax
import jax.numpy as jnp
from jax import lax

FEATURE_WIDTH = 2048
BRANCH_WIDTH = 256
W = 48
IMGS = 8
H = 36


def draw_extent(key, part):
    row_key, col_key = jax.random.split(jax.random.fold_in(key, 7))
    rows_drawn = jax.random.randint(row_key, (IMGS,), H // 2, H + 1)
    cols_drawn = jax.random.randint(col_key, (IMGS,), W // 2, W + 1)
    image_ids = jnp.arange(IMGS, dtype=jnp.int32)
    rows_drawn = jnp.where(image_ids == 0, H, jnp.where(image_ids == IMGS - 1, H // 2, rows_drawn))
    cols_drawn = jnp.where(image_ids == 0, W, jnp.where(image_ids == IMGS - 1, W // 2, cols_drawn))
    return jnp.stack([rows_drawn, cols_drawn], axis=1).astype(jnp.int32)


def strengthened(drawn, rng, source, target, parts, factor):
    owner, partner = [(jnp.arange(drawn.shape[axis_at]) // (drawn.shape[axis_at] // parts)).reshape([-1 if axis == axis_at else 1 for axis in range(drawn.ndim)]) for axis_at in (source, target)]
    chosen = jax.random.permutation(rng, parts)[partner]
    strong = (owner == chosen) | (owner == (partner + parts // 2) % parts)
    return jnp.where(strong, factor * drawn, drawn)


def block_levels(key, shape, shards, smallest, top_value):
    def one(position, shards_of):
        heights = jax.random.uniform(jax.random.fold_in(jax.random.fold_in(key, 6), position), (shards_of,), jnp.float32, smallest / len(shards), top_value / len(shards))
        return jnp.repeat(jnp.exp(heights), shape[position] // shards_of).reshape((-1,) + (1,) * (len(shape) - position - 1))

    gain = one(*shards[0])
    for cut in shards[1:]:
        gain = gain * one(*cut)
    return gain


def normal_values(own_key, shape, width, reach, pieces=(), kind=jnp.bfloat16):
    array = jax.random.normal(own_key, shape, jnp.float32) * width
    if len(pieces) > 0:
        array = block_levels(own_key, shape, pieces, -0.22, 0.18) * array
    return jnp.clip(array, min=-reach, max=reach).astype(kind)


def bell_draw_with(stream_key, shape, scale, limit, cuts, heavy, held_as=jnp.bfloat16):
    drawn = scale * jax.random.normal(stream_key, shape, jnp.float32)
    if cuts:
        drawn = drawn * block_levels(stream_key, shape, cuts, -0.22, 0.18)
    return jnp.clip(strengthened(drawn, jax.random.fold_in(stream_key, 3), *heavy), -limit, limit).astype(held_as)


def setup_inputs(seed: int = 0) -> dict:
    keys = jax.random.split(jax.random.key(seed), 10)
    return {
        "features": bell_draw_with(keys[0], (IMGS, H, W, FEATURE_WIDTH), 1.0, 6.0, ((0, 8), (1, 4)), (0, 3, 8, 2.0)),
        "extent": draw_extent(jax.random.fold_in(keys[9], 71), 0),
        "pointwise_weight": normal_values(keys[2], (FEATURE_WIDTH, BRANCH_WIDTH), FEATURE_WIDTH ** -0.5, 0.125, ((0, 8), (1, 4))),
        "pooling_weight": normal_values(keys[3], (FEATURE_WIDTH, BRANCH_WIDTH), FEATURE_WIDTH ** -0.5, 0.125, ((0, 8), (1, 4))),
        "dilated_weight": normal_values(keys[4], (27 * FEATURE_WIDTH, BRANCH_WIDTH), (9 * FEATURE_WIDTH) ** -0.5, 0.046875, ((0, 8), (1, 4))),
        "projection_weight": normal_values(keys[5], (5 * BRANCH_WIDTH, BRANCH_WIDTH), (5 * BRANCH_WIDTH) ** -0.5, 0.15625, ((0, 8), (1, 4))),
        "norm_gain": jnp.clip(1.0 + 0.1 * jax.random.normal(keys[6], (6, BRANCH_WIDTH), jnp.float32), 0.5, 1.5),
        "norm_bias": normal_values(keys[7], (6, BRANCH_WIDTH), 0.5, 3.0, (), jnp.float32),
        "cotangent": normal_values(keys[8], (IMGS, H, W, BRANCH_WIDTH), 1.0, 6.0, ((0, 8), (1, 4))),
    }


@jax.custom_vjp
def low(v):
    return lax.optimization_barrier(v.astype(jnp.bfloat16)).astype(jnp.float32)

@jax.custom_vjp
def low_back(v):
    return v

def low_keep(v):
    return (low(v), None)

def low_pass(kept, grad):
    return (grad,)

def back_keep(v):
    return (v, None)

def back_low(kept, grad):
    return (low(grad),)
low.defvjp(low_keep, low_pass)
low_back.defvjp(back_keep, back_low)
epsilon = 1e-05
dilations = (6, 12, 18)
highest = lax.Precision.HIGHEST

def batch_norm(values, validity_mask, pixel_total, scale_gain, shift_bias):
    reduce_axes = tuple(range(values.ndim - 1))
    weight = validity_mask[..., None]
    average = lax.optimization_barrier(jnp.sum(values * weight, axis=reduce_axes)) / pixel_total
    spread = lax.optimization_barrier(jnp.sum(weight * (values - average) ** 2, axis=reduce_axes)) / pixel_total
    normed = (values - average) * lax.rsqrt(spread + epsilon)
    return weight * jax.nn.silu(scale_gain * normed + shift_bias)

def image_convs(masked_image, pointwise_weight, dilated_weight):
    single = masked_image[None]
    results = [jnp.einsum('ihwc,ca->ihwa', single, pointwise_weight, precision=highest)[0]]
    for branch_index, dilation in enumerate(dilations):
        kernel_tensor = dilated_weight[branch_index * 9 * FEATURE_WIDTH:(branch_index + 1) * 9 * FEATURE_WIDTH].reshape(3, 3, FEATURE_WIDTH, BRANCH_WIDTH)
        convolved = lax.conv_general_dilated(single, kernel_tensor, (1, 1), ((dilation, dilation), (dilation, dilation)), rhs_dilation=(dilation, dilation), dimension_numbers=('NHWC', 'HWIO', 'NHWC'), precision=highest)
        results.append(convolved[0])
    return jnp.stack(results)

def forward_pass(features, pointwise_weight, pooling_weight, dilated_weight, projection_weight, norm_gain, norm_bias, validity_mask, image_region_sizes):
    masked = features * validity_mask[..., None]
    pixel_total = jnp.sum(validity_mask)
    per_image = jax.checkpoint(lambda masked_image: image_convs(masked_image, pointwise_weight, dilated_weight))
    all_convs = lax.map(per_image, masked)
    branches = [low_back(all_convs[:, branch_index]) for branch_index in range(4)]
    pooled = lax.optimization_barrier(jnp.sum(masked, axis=(1, 2))) / image_region_sizes[:, None]
    pool_pre = low_back(jnp.dot(low(pooled), pooling_weight, precision=highest))
    branch_acts = [batch_norm(branches[branch_index], validity_mask, pixel_total, norm_gain[branch_index], norm_bias[branch_index]) for branch_index in range(4)]
    image_ones = jnp.ones((IMGS,), jnp.float32)
    pool_act = batch_norm(pool_pre, image_ones, jnp.sum(image_ones), norm_gain[4], norm_bias[4])
    concat = low(jnp.concatenate(branch_acts + [pool_act[:, None, None, :] * validity_mask[..., None]], axis=-1))
    projected = low_back(jnp.einsum('ihwk,ka->ihwa', concat, projection_weight, precision=highest))
    return batch_norm(projected, validity_mask, pixel_total, norm_gain[5], norm_bias[5])

def reference(features, extent, pointwise_weight, pooling_weight, dilated_weight, projection_weight, norm_gain, norm_bias, cotangent):
    row_ids = jnp.arange(H, dtype=jnp.int32)
    col_ids = jnp.arange(W, dtype=jnp.int32)
    validity_mask = ((row_ids[None, :, None] < extent[:, 0][:, None, None]) & (col_ids[None, None, :] < extent[:, 1][:, None, None])).astype(jnp.float32)
    image_region_sizes = (extent[:, 0] * extent[:, 1]).astype(jnp.float32)

    def wrapped_function(incoming_features, incoming_pointwise, incoming_pooling, incoming_dilated, incoming_projection, incoming_gain, incoming_bias):
        return forward_pass(incoming_features, incoming_pointwise, incoming_pooling, incoming_dilated, incoming_projection, incoming_gain, incoming_bias, validity_mask, image_region_sizes)
    output, backward_rule = jax.vjp(wrapped_function, features.astype(jnp.float32), pointwise_weight.astype(jnp.float32), pooling_weight.astype(jnp.float32), dilated_weight.astype(jnp.float32), projection_weight.astype(jnp.float32), norm_gain, norm_bias)
    gradients = backward_rule(cotangent.astype(jnp.float32))
    return (output.astype(jnp.bfloat16), gradients[0].astype(jnp.bfloat16), gradients[1], gradients[2], gradients[3], gradients[4], gradients[5], gradients[6])
```

```python
import jax
import jax.numpy as jnp
from jax import lax
from jax.experimental import pallas as pl
from jax.experimental.pallas import tpu as pltpu
from jax.sharding import PartitionSpec as P

epsilon = 1e-05
dilations = (6, 12, 18)
LANES = 128
BLOCK_ROWS = 6
AXES = ("dp", "rows")
FULL, SHORT, PER_CHIP = 14, 13, 27
NT = (((1,), (1,)), ((), ()))
TN = (((0,), (0,)), ((), ()))
NN = (((1,), (0,)), ((), ()))


def dot(first, second, dims):
    return lax.dot_general(first, second, dims, preferred_element_type=jnp.float32)


def silu_slope(values):
    sigma = jax.nn.sigmoid(values)
    return sigma * (1.0 + values * (1.0 - sigma))


class Place:
    def __init__(self):
        self.nd, self.nr = lax.axis_size("dp"), lax.axis_size("rows")
        self.nzl = self.nr // 2
        d, z = lax.axis_index("dp"), lax.axis_index("rows")
        self.d, self.z = d, z
        self.m, self.c = d // 2, d % 2
        self.zh, self.zl = z // self.nzl, z % self.nzl
        self.part = self.c * self.nzl + self.zl
        self.image = 2 * self.m + self.zh

    def send(self, x, target):
        nzl = self.nzl
        pairs = []
        for flat in range(self.nd * self.nr):
            d, z = divmod(flat, self.nr)
            m, c, zh, zl = target(d // 2, d % 2, z // nzl, z % nzl)
            pairs.append((flat, (2 * m + c) * self.nr + zh * nzl + zl))
        return lax.ppermute(x, AXES, pairs)

    def swap(self, x, m=0, c=0, zh=0, zl=0):
        return self.send(x, lambda a, b, e, f: (a ^ m, b ^ c, e ^ zh, f ^ zl))


def by_xor(items, index):
    items = list(items)
    bit = 1
    while bit < len(items):
        flip = (index & bit) != 0
        items = [jnp.where(flip, items[k ^ bit], items[k]) for k in range(len(items))]
        bit *= 2
    return items


def tree(items):
    items = list(items)
    while len(items) > 1:
        items = [items[i] + items[i + 1] for i in range(0, len(items), 2)]
    return items[0]


def exchange_stages(place):
    return (
        [dict(c=1)],
        [dict(m=k) for k in range(1, place.nd // 2)],
        [dict(zh=k // place.nzl, zl=k % place.nzl) for k in range(1, place.nr)],
    )


def total(place, x):
    for stage in exchange_stages(place):
        x = tree([x] + [place.swap(x, **s) for s in stage])
    return x


def moments(place, sums, squares, count, extra=None):
    width = sums.shape[1]
    k = sums.shape[0]
    rows = [sums, squares, jnp.full((1, width), count, jnp.float32)]
    if extra is not None:
        rows.append(extra)
    x = jnp.concatenate(rows, axis=0)
    for stage in exchange_stages(place):
        xs = [x] + [place.swap(x, **s) for s in stage]
        whole = tree(xs)
        n = whole[2 * k : 2 * k + 1]
        mean = whole[:k] / jnp.maximum(n, 1.0)
        between = []
        for y in xs:
            own = y[2 * k : 2 * k + 1]
            gap = y[:k] / jnp.maximum(own, 1.0) - mean
            between.append(own * gap * gap)
        x = jnp.concatenate([whole[:k], whole[k : 2 * k] + tree(between), whole[2 * k :]], axis=0)
    n = x[2 * k : 2 * k + 1]
    return x[:k] / n, x[k : 2 * k] / n, n, x[2 * k + 1 :]


def local_moments(values, mask, count):
    sums = jnp.sum(values * mask, axis=0, keepdims=True)
    centred = (values - sums / jnp.maximum(count, 1.0)) * mask
    return sums, jnp.sum(centred * centred, axis=0, keepdims=True)


def line_pieces(place, dilated, pointwise, pooling):
    tiles = lambda w: jnp.transpose(w.T.reshape(w.shape[1], w.shape[0] // LANES, LANES), (1, 0, 2))
    dil, one, pool = tiles(dilated), tiles(pointwise), tiles(pooling)
    same = [jnp.concatenate([dil[r::4][:FULL], one[r : r + 1], pool[r : r + 1]], axis=0) for r in range(2)]
    other = [dil[2 + r :: 4][:SHORT] for r in range(2)]
    same, other = by_xor(same, place.zl), by_xor(other, place.zl)
    halves = []
    for kh in range(2):
        got = []
        for kc, source in ((0, same), (1, other)):
            for kl in range(2):
                piece = source[kl]
                if (kc, kh, kl) != (0, 0, 0):
                    piece = place.swap(piece, c=kc, zh=kh, zl=kl)
                got.append(piece)
        halves.append(jnp.concatenate(got, axis=0))
    return halves


def plane_gather(place, halves):
    own, far = halves
    own_x, own_y = place.swap(own, m=1), place.swap(own, m=2)
    far_x, far_y = place.swap(far, m=1), place.swap(far, m=2)
    own_d, far_d = place.swap(own_x, m=2), place.swap(far_y, m=1)
    return [[own, far], [own_x, far_x], [own_y, far_y], [own_d, far_d]]


def add_low(first, *others):
    out = first.astype(jnp.float32)
    for o in others:
        out = out + o.astype(jnp.float32)
    return out.astype(jnp.bfloat16)


def plane_scatter(place, pieces):
    own_d, far_d = place.swap(pieces[3][0], m=2), place.swap(pieces[3][1], m=1)
    own_y, far_x = place.swap(pieces[2][0], m=2), place.swap(pieces[1][1], m=1)
    own_x = place.swap(add_low(pieces[1][0], own_d), m=1)
    far_y = place.swap(add_low(pieces[2][1], far_d), m=2)
    return [add_low(pieces[0][0], own_x, own_y), add_low(pieces[0][1], far_x, far_y)]


def line_back(place, halves):
    sums = {}
    for kc in range(2):
        for kl in range(2):
            start = kl * (FULL + 2) if kc == 0 else 2 * (FULL + 2) + kl * SHORT
            size = FULL + 2 if kc == 0 else SHORT
            got = None
            for kh in range(2):
                piece = halves[kh][start : start + size]
                if (kc, kh, kl) != (0, 0, 0):
                    piece = place.swap(piece, c=kc, zh=kh, zl=kl)
                piece = piece.astype(jnp.float32)
                got = piece if got is None else got + piece
            sums[kc, kl] = got
    same = by_xor([sums[0, 0], sums[0, 1]], place.zl)
    other = by_xor([sums[1, 0], sums[1, 1]], place.zl)
    gap = jnp.zeros((FULL - SHORT,) + other[0].shape[1:], jnp.float32)
    dil = jnp.stack([s[:FULL] for s in same] + [jnp.concatenate([o, gap], axis=0) for o in other], axis=1)
    dil = dil.reshape((4 * FULL,) + dil.shape[2:])[: 2 * PER_CHIP]
    rows = lambda t: jnp.transpose(t, (1, 0, 2)).reshape(t.shape[1], t.shape[0] * LANES).T
    one = jnp.stack([s[FULL] for s in same])
    pool = jnp.stack([s[FULL + 1] for s in same])
    return rows(dil), rows(one), rows(pool)


def gathered_tiles(place, dilated, pointwise, pooling):
    whole = []
    for w in (dilated, pointwise, pooling):
        w = lax.all_gather(w, "rows", axis=1, tiled=True)
        w = lax.all_gather(w, "dp", axis=0, tiled=True)
        channels = pointwise.shape[0] * place.nd
        taps = w.shape[0] // channels
        w = w.reshape(taps, channels // (LANES * place.nr), place.nr, LANES, w.shape[1])
        w = lax.dynamic_index_in_dim(w, place.part, 2, keepdims=False)
        whole.append(jnp.transpose(w.reshape(taps, channels // place.nr, w.shape[-1]), (0, 2, 1)))
    return jnp.concatenate(whole, axis=0)


def scattered_tiles(place, gradients):
    outs = []
    taps, columns, width = gradients.shape
    for g in (gradients[: taps - 2], gradients[taps - 2 : taps - 1], gradients[taps - 1 :]):
        g = jnp.transpose(g, (0, 2, 1)).reshape(g.shape[0], width // LANES, 1, LANES, columns)
        spread = jnp.zeros((g.shape[0], width // LANES, place.nr, LANES, columns), g.dtype)
        g = lax.dynamic_update_slice_in_dim(spread, g, place.part, 2).reshape(-1, columns)
        g = lax.psum_scatter(g, "dp", scatter_dimension=0, tiled=True)
        outs.append(lax.psum_scatter(g, "rows", scatter_dimension=1, tiled=True).astype(jnp.float32))
    return outs


class Shape:
    def __init__(self, band_rows, columns, nr, width, out, pieces):
        self.band_rows, self.columns, self.nr, self.width, self.out = band_rows, columns, nr, width, out
        self.rows = band_rows * nr
        self.band, self.pixels = band_rows * columns, band_rows * columns * nr
        self.block = BLOCK_ROWS * columns
        self.blocks = self.rows // BLOCK_ROWS
        self.pieces = pieces
        self.n_weights = 8 if pieces else 1


ANY = pl.BlockSpec(memory_space=pl.ANY)
SMEM = pl.BlockSpec(memory_space=pltpu.SMEM)
VMEM = pl.BlockSpec(memory_space=pltpu.VMEM)
PARAMS = pltpu.CompilerParams(vmem_limit_bytes=58 * 2**20)


def start_bands(shape, refs, scratch, sem, part):
    for k, ref in enumerate(refs):
        pltpu.make_async_copy(ref, scratch.at[pl.ds((part ^ k) * shape.band, shape.band), :], sem.at[k]).start()


def wait_bands(shape, refs, scratch, sem):
    for k, ref in enumerate(refs):
        pltpu.make_async_copy(ref, scratch.at[pl.ds(k * shape.band, shape.band), :], sem.at[k]).wait()


def piece_of(t, kl, c):
    same = jnp.where(c == 0, t < FULL, t >= SHORT)
    return jnp.where(same, (FULL + 2) * kl + t - SHORT * c, 2 * (FULL + 2) + SHORT * kl + t - FULL * (1 - c))


def for_tiles(shape, info, first_tap, n_taps, visit):
    m, c, zh, zl = info[0], info[1], info[2], info[3]

    def column(kh, kl):
        return ((zh ^ kh) * 2 + (zl ^ kl)) * (shape.out // shape.nr)

    if first_tap < 27:

        def body(v, carry):
            chip = v // PER_CHIP
            t = v - chip * PER_CHIP
            for rel in range(4):

                @pl.when((chip ^ m) == rel)
                def _():
                    for kl in range(2):
                        slot = piece_of(t, kl, c)
                        for kh in range(2):
                            visit(rel, kh, slot, v // 4 - first_tap, (v % 4) * LANES, column(kh, kl))

            return carry

        lax.fori_loop(4 * first_tap, 4 * min(first_tap + n_taps, 27), body, 0)
    for tap in range(max(first_tap, 27), first_tap + n_taps):
        for rel in range(4):
            for kl in range(2):
                for kh in range(2):
                    lane = pl.multiple_of((rel ^ m) * LANES, LANES)
                    visit(rel, kh, (FULL + 2) * kl + FULL + tap - 27, tap - first_tap, lane, column(kh, kl))


def start_weights(shape, refs, scratch, sem, info, first_tap, n_taps):
    if not shape.pieces:
        pltpu.make_async_copy(refs[0].at[pl.ds(first_tap, n_taps)], scratch, sem).start()
        return
    part = shape.out // shape.nr

    def visit(rel, kh, slot, tap, lane, column):
        place = scratch.at[tap, pl.ds(pl.multiple_of(column, part), part), pl.ds(pl.multiple_of(lane, LANES), LANES)]
        pltpu.make_async_copy(refs[2 * rel + kh].at[slot], place, sem).start()

    for_tiles(shape, info, first_tap, n_taps, visit)


def wait_weights(scratch, sem):
    pltpu.make_async_copy(scratch, scratch, sem).wait()


def shifted(values, by, columns):
    if by == 0:
        return values
    pixels = values.shape[0]
    source = lax.broadcasted_iota(jnp.int32, (pixels, 1), 0) % columns - by
    return jnp.where((source >= 0) & (source < columns), pltpu.roll(values, by % pixels, 0), 0.0)


def put_halves(shape, c, blk, value, keep, sent):
    half = shape.blocks // 2
    at = pl.ds((blk % half) * shape.block, shape.block)

    @pl.when(c == blk // half)
    def _():
        keep[at, :] = value

    @pl.when(c != blk // half)
    def _():
        sent[at, :] = value.astype(sent.dtype)


def half_shapes(shape):
    half = shape.pixels // 2
    return [jax.ShapeDtypeStruct((half, shape.out), jnp.float32), jax.ShapeDtypeStruct((half, shape.out), jnp.bfloat16)]


def dilated_kernel(shape, branch, info, *refs):
    dilation = dilations[branch]
    bands, weights = refs[: shape.nr], refs[shape.nr : shape.nr + shape.n_weights]
    keep, sent, x, w, y, band_sem, w_sem = refs[shape.nr + shape.n_weights :]
    start_bands(shape, bands, x, band_sem, info[4])
    start_weights(shape, weights, w, w_sem, info, 9 * branch, 9)
    wait_bands(shape, bands, x, band_sem)
    wait_weights(w, w_sem)
    move = dilation * shape.columns
    for s in range(3):
        y[s] = dot(x[...], w[3 + s], NT)
        y[s, move:, :] += dot(x[: shape.pixels - move, :], w[s], NT)
        y[s, : shape.pixels - move, :] += dot(x[move:, :], w[6 + s], NT)
    for blk in range(shape.blocks):
        at = slice(blk * shape.block, (blk + 1) * shape.block)
        z = y[1, at, :] + shifted(y[0, at, :], dilation, shape.columns) + shifted(y[2, at, :], -dilation, shape.columns)
        put_halves(shape, info[1], blk, z, keep, sent)


def dilated_sums(shape, branch, info, bands, weights):
    macs = shape.pixels * shape.width * shape.out * 7
    return pl.pallas_call(
        lambda *refs: dilated_kernel(shape, branch, *refs),
        out_shape=half_shapes(shape),
        in_specs=[SMEM] + [ANY] * (shape.nr + shape.n_weights),
        out_specs=[VMEM] * 2,
        scratch_shapes=[
            pltpu.VMEM((shape.pixels, shape.width), jnp.bfloat16),
            pltpu.VMEM((9, shape.out, shape.width), jnp.bfloat16),
            pltpu.VMEM((3, shape.pixels, shape.out), jnp.float32),
            pltpu.SemaphoreType.DMA((shape.nr,)),
            pltpu.SemaphoreType.DMA,
        ],
        compiler_params=PARAMS,
        cost_estimate=pl.CostEstimate(flops=2 * macs, bytes_accessed=2**23, transcendentals=0),
        name=f"branch{branch}",
    )(info, *bands, *weights)


def one_kernel(shape, info, area, *refs):
    bands, weights = refs[: shape.nr], refs[shape.nr : shape.nr + shape.n_weights]
    keep, sent, pooled, lifted, x, w, band_sem, w_sem = refs[shape.nr + shape.n_weights :]
    start_bands(shape, bands, x, band_sem, info[4])
    start_weights(shape, weights, w, w_sem, info, 27, 2)
    wait_bands(shape, bands, x, band_sem)
    wait_weights(w, w_sem)
    sums = jnp.zeros((1, shape.width), jnp.float32)
    for blk in range(shape.blocks):
        at = slice(blk * shape.block, (blk + 1) * shape.block)
        values = x[at, :]
        sums = sums + jnp.sum(values.astype(jnp.float32), axis=0, keepdims=True)
        put_halves(shape, info[1], blk, dot(values, w[0], NT), keep, sent)
    low = jnp.broadcast_to(sums / area[0], pooled.shape).astype(jnp.bfloat16)
    first = lax.broadcasted_iota(jnp.int32, pooled.shape, 0) == 0
    pooled[...] = jnp.where(first, low.astype(jnp.float32), 0.0).astype(jnp.bfloat16)
    lifted[...] = dot(pooled[...], w[1], NT)


def one_sums(shape, info, area, bands, weights):
    return pl.pallas_call(
        lambda *refs: one_kernel(shape, *refs),
        out_shape=half_shapes(shape)
        + [jax.ShapeDtypeStruct((16, shape.width), jnp.bfloat16), jax.ShapeDtypeStruct((16, shape.out), jnp.float32)],
        in_specs=[SMEM, SMEM] + [ANY] * (shape.nr + shape.n_weights),
        out_specs=[VMEM] * 4,
        scratch_shapes=[
            pltpu.VMEM((shape.pixels, shape.width), jnp.bfloat16),
            pltpu.VMEM((2, shape.out, shape.width), jnp.bfloat16),
            pltpu.SemaphoreType.DMA((shape.nr,)),
            pltpu.SemaphoreType.DMA,
        ],
        compiler_params=PARAMS,
        cost_estimate=pl.CostEstimate(
            flops=2 * shape.pixels * shape.width * shape.out, bytes_accessed=2**22, transcendentals=0
        ),
        name="one_by_one",
    )(info, area, *bands, *weights)


def moved_deltas(shape, delta, moved, branch):
    for blk in range(shape.blocks):
        at = slice(blk * shape.block, (blk + 1) * shape.block)
        values = delta[at, (branch + 1) * shape.out : (branch + 2) * shape.out].astype(jnp.float32)
        for s in range(3):
            moved[s, at, :] = shifted(values, (s - 1) * dilations[branch], shape.columns).astype(jnp.bfloat16)


def weight_kernel(shape, info, *refs):
    nr = shape.nr
    bands, deltas, pool_delta, pooled = refs[:nr], refs[nr : 2 * nr], refs[2 * nr], refs[2 * nr + 1]
    outs = refs[2 * nr + 2 : 2 * nr + 2 + shape.n_weights]
    x, delta, moved, grads, band_sem, delta_sem = refs[2 * nr + 2 + shape.n_weights :]
    start_bands(shape, deltas, delta, delta_sem, info[4])
    start_bands(shape, bands, x, band_sem, info[4])
    wait_bands(shape, deltas, delta, delta_sem)
    wait_bands(shape, bands, x, band_sem)
    part = shape.out // nr

    def put(first_tap, n_taps):
        if not shape.pieces:
            outs[0][first_tap : first_tap + n_taps] = grads[:n_taps]
            return

        def visit(rel, kh, slot, tap, lane, column):
            rows, lanes = pl.ds(pl.multiple_of(column, part), part), pl.ds(pl.multiple_of(lane, LANES), LANES)
            outs[2 * rel + kh][slot] = grads[tap, rows, lanes]

        for_tiles(shape, info, first_tap, n_taps, visit)

    for branch in range(3):
        moved_deltas(shape, delta, moved, branch)
        move = dilations[branch] * shape.columns
        for s in range(3):
            grads[s] = dot(moved[s, move:, :], x[: shape.pixels - move, :], TN).astype(jnp.bfloat16)
            grads[3 + s] = dot(moved[s], x[...], TN).astype(jnp.bfloat16)
            grads[6 + s] = dot(moved[s, : shape.pixels - move, :], x[move:, :], TN).astype(jnp.bfloat16)
        put(9 * branch, 9)
    grads[0] = dot(delta[:, : shape.out], x[...], TN).astype(jnp.bfloat16)
    grads[1] = dot(pool_delta[...], pooled[...], TN).astype(jnp.bfloat16)
    put(27, 2)


def weight_gradients(shape, info, bands, deltas, pool_delta, pooled):
    if shape.pieces:
        slots = 2 * (FULL + 2) + 2 * SHORT
        out_shape = [jax.ShapeDtypeStruct((slots, shape.out // shape.nr, LANES), jnp.bfloat16)] * 8
    else:
        out_shape = [jax.ShapeDtypeStruct((29, shape.out, shape.width), jnp.bfloat16)]
    return pl.pallas_call(
        lambda *refs: weight_kernel(shape, *refs),
        out_shape=out_shape,
        in_specs=[SMEM] + [ANY] * (2 * shape.nr) + [VMEM] * 2,
        out_specs=[VMEM] * len(out_shape),
        scratch_shapes=[
            pltpu.VMEM((shape.pixels, shape.width), jnp.bfloat16),
            pltpu.VMEM((shape.pixels, 4 * shape.out), jnp.bfloat16),
            pltpu.VMEM((3, shape.pixels, shape.out), jnp.bfloat16),
            pltpu.VMEM((9, shape.out, shape.width), jnp.bfloat16),
            pltpu.SemaphoreType.DMA((shape.nr,)),
            pltpu.SemaphoreType.DMA((shape.nr,)),
        ],
        compiler_params=PARAMS,
        cost_estimate=pl.CostEstimate(
            flops=44 * shape.pixels * shape.width * shape.out, bytes_accessed=2**24, transcendentals=0
        ),
        name="weight_gradients",
    )(info, *bands, *deltas, pool_delta, pooled)


def input_kernel(shape, info, area, *refs):
    nr, n = shape.nr, shape.n_weights
    deltas, pool_delta, mask, weights = refs[:nr], refs[nr], refs[nr + 1], refs[nr + 2 : nr + 2 + n]
    outs = refs[nr + 2 + n : 2 * nr + 2 + n]
    delta, moved, w, acc, delta_sem, w_sem = refs[2 * nr + 2 + n :]
    start_bands(shape, deltas, delta, delta_sem, info[4])
    start_weights(shape, weights, w, w_sem, info, 0, 29)
    wait_bands(shape, deltas, delta, delta_sem)
    wait_weights(w, w_sem)
    pool = dot(pool_delta[...], w[28], NN)[0:1] / area[0]
    acc[...] = dot(delta[:, : shape.out], w[27], NN) + pool
    for branch in range(3):
        moved_deltas(shape, delta, moved, branch)
        move = dilations[branch] * shape.columns
        for s in range(3):
            acc[...] += dot(moved[s], w[9 * branch + 3 + s], NN)
            acc[: shape.pixels - move, :] += dot(moved[s, move:, :], w[9 * branch + s], NN)
            acc[move:, :] += dot(moved[s, : shape.pixels - move, :], w[9 * branch + 6 + s], NN)
    for k in range(nr):
        at = pl.ds(pl.multiple_of((info[4] ^ k) * shape.band, shape.band), shape.band)
        outs[k][...] = (acc[at, :] * mask[at, :]).astype(jnp.bfloat16)


def input_gradient(shape, info, area, deltas, pool_delta, mask, weights):
    return pl.pallas_call(
        lambda *refs: input_kernel(shape, *refs),
        out_shape=[jax.ShapeDtypeStruct((shape.band, shape.width), jnp.bfloat16)] * shape.nr,
        in_specs=[SMEM, SMEM] + [ANY] * shape.nr + [VMEM] * 2 + [ANY] * shape.n_weights,
        out_specs=[VMEM] * shape.nr,
        scratch_shapes=[
            pltpu.VMEM((shape.pixels, 4 * shape.out), jnp.bfloat16),
            pltpu.VMEM((3, shape.pixels, shape.out), jnp.bfloat16),
            pltpu.VMEM((29, shape.out, shape.width), jnp.bfloat16),
            pltpu.VMEM((shape.pixels, shape.width), jnp.float32),
            pltpu.SemaphoreType.DMA((shape.nr,)),
            pltpu.SemaphoreType.DMA,
        ],
        compiler_params=PARAMS,
        cost_estimate=pl.CostEstimate(
            flops=44 * shape.pixels * shape.width * shape.out, bytes_accessed=2**24, transcendentals=0
        ),
        name="input_gradient",
    )(info, area, *deltas, pool_delta, mask, *weights)


def valid_pixels(extent, first_row, rows, columns):
    r = first_row + lax.broadcasted_iota(jnp.int32, (rows, columns), 0)
    w = lax.broadcasted_iota(jnp.int32, (rows, columns), 1)
    return ((r < extent[0]) & (w < extent[1])).astype(jnp.float32).reshape(rows * columns, 1)


def to_logical(place, x):
    return place.send(x, lambda m, c, zh, zl: (m, zh, c, zl))


def on_device(
    features, extent, pointwise_weight, pooling_weight, dilated_weight, projection_weight, norm_gain, norm_bias, cotangent
):
    place = Place()
    nr, nzl = place.nr, place.nzl
    _, band_rows, columns, channels = features.shape
    width, out = channels // nr, norm_gain.shape[1]
    band = band_rows * columns
    pieces = nr == 4 and place.nd == 8 and dilated_weight.shape[0] == 2 * PER_CHIP * LANES
    shape = Shape(band_rows, columns, nr, width, out, pieces)
    images = place.nd

    if pieces:
        weights = [w for pair in plane_gather(place, line_pieces(place, dilated_weight, pointwise_weight, pooling_weight)) for w in pair]
    else:
        weights = [gathered_tiles(place, dilated_weight, pointwise_weight, pooling_weight)]
    projection = lax.all_gather(projection_weight, "rows", axis=1, tiled=True)
    projection = lax.all_gather(projection, "dp", axis=0, tiled=True)

    partner = place.swap(extent, c=1)
    extent_here = jnp.where(place.zh == place.c, extent, partner)[0]
    area = (extent_here[0] * extent_here[1]).astype(jnp.float32)
    mask = valid_pixels(extent_here, place.part * band_rows, band_rows, columns)
    whole_mask = valid_pixels(extent_here, 0, shape.rows, columns)
    own_mask = valid_pixels(extent[0], place.z * band_rows, band_rows, columns)
    info = jnp.stack([place.m, place.c, place.zh, place.zl, place.part]).astype(jnp.int32)
    areas = area.reshape(1)

    masked = (features.reshape(band, channels) * own_mask.astype(jnp.bfloat16)).reshape(band, channels // (LANES * nr), nr, LANES)
    parts = by_xor([masked[:, :, q].reshape(band, width) for q in range(nr)], place.z)
    bands = []
    for k in range(nr):
        k0, k1 = divmod(k, nzl)
        bands.append(place.send(parts[k], lambda m, c, zh, zl: (m, zh ^ k0, c, zl ^ k1)))
    upstream_low = to_logical(place, cotangent.reshape(band, out))

    def reduce(keep, sent):
        half = keep + place.swap(sent, c=1).astype(jnp.float32)
        rows = half.reshape(nzl, band, out)
        mine = lax.dynamic_index_in_dim(rows, place.zl, 0, keepdims=False)
        for k in range(1, nzl):
            other = lax.dynamic_index_in_dim(rows, place.zl ^ k, 0, keepdims=False).astype(jnp.bfloat16)
            mine = mine + place.swap(other, zl=k).astype(jnp.float32)
        return mine

    keep, sent, pooled, lifted = one_sums(shape, info, areas, bands, weights)
    z = [reduce(keep, sent)]
    for branch in range(3):
        z.append(reduce(*dilated_sums(shape, branch, info, bands, weights)))

    local_count = jnp.sum(mask)
    stats = [local_moments(v, mask, local_count) for v in z]
    table = (lax.broadcasted_iota(jnp.int32, (images, 1), 0) == place.image).astype(jnp.float32) * lifted[0:1]
    average, spread, count, pool_pre = moments(
        place,
        jnp.concatenate([s for s, _ in stats], axis=0),
        jnp.concatenate([q for _, q in stats], axis=0),
        local_count,
        table,
    )
    inv_std = lax.rsqrt(spread + epsilon)
    normed = [(z[k] - average[k : k + 1]) * inv_std[k : k + 1] for k in range(4)]
    pre_act = [norm_gain[k : k + 1] * normed[k] + norm_bias[k : k + 1] for k in range(4)]

    pool_average = jnp.mean(pool_pre, axis=0, keepdims=True)
    pool_centred = pool_pre - pool_average
    pool_inv = lax.rsqrt(jnp.mean(pool_centred * pool_centred, axis=0, keepdims=True) + epsilon)
    pool_normed = pool_centred * pool_inv
    pool_lift = norm_gain[4:5] * pool_normed + norm_bias[4:5]
    here = lambda rows: lax.dynamic_slice_in_dim(rows, place.image, 1, axis=0)
    pool_act = here(jax.nn.silu(pool_lift))

    concat = jnp.concatenate([jax.nn.silu(u) * mask for u in pre_act] + [pool_act * mask], axis=1).astype(jnp.bfloat16)
    proj_pre = dot(concat, projection, NN)
    proj_sums, proj_squares = local_moments(proj_pre, mask, local_count)
    proj_average, proj_spread, _, _ = moments(place, proj_sums, proj_squares, local_count)
    proj_inv = lax.rsqrt(proj_spread + epsilon)
    proj_normed = (proj_pre - proj_average) * proj_inv
    proj_lift = norm_gain[5:6] * proj_normed + norm_bias[5:6]
    output = to_logical(place, (jax.nn.silu(proj_lift) * mask).astype(jnp.bfloat16))

    upstream = upstream_low.astype(jnp.float32) * mask * silu_slope(proj_lift)
    sums = jnp.concatenate(
        [jnp.sum(upstream * proj_normed, axis=0, keepdims=True), jnp.sum(upstream, axis=0, keepdims=True)], axis=0
    )
    proj_totals = total(place, sums)
    proj_gain_grad, proj_bias_grad = proj_totals[0:1], proj_totals[1:2]
    gain = norm_gain[5:6]
    proj_delta = (
        mask
        * proj_inv
        * (gain * upstream - gain * proj_bias_grad / count - proj_normed * gain * proj_gain_grad / count)
    ).astype(jnp.bfloat16)
    concat_grad = dot(proj_delta, projection, NT)
    projection_partial = dot(concat, proj_delta, TN).astype(jnp.bfloat16)
    branch_up = [
        concat_grad[:, k * out : (k + 1) * out] * mask * silu_slope(pre_act[k]) for k in range(4)
    ]
    pool_part = jnp.sum(concat_grad[:, 4 * out :] * mask, axis=0, keepdims=True)
    table = (lax.broadcasted_iota(jnp.int32, (images, 1), 0) == place.image).astype(jnp.float32) * pool_part
    totals = total(
        place,
        jnp.concatenate(
            [jnp.sum(branch_up[k] * normed[k], axis=0, keepdims=True) for k in range(4)]
            + [jnp.sum(branch_up[k], axis=0, keepdims=True) for k in range(4)]
            + [table],
            axis=0,
        ),
    )
    branch_gain_grad, branch_bias_grad = totals[:4], totals[4:8]
    pool_up = totals[8:] * silu_slope(pool_lift)
    pool_gain_grad = jnp.sum(pool_up * pool_normed, axis=0, keepdims=True)
    pool_bias_grad = jnp.sum(pool_up, axis=0, keepdims=True)
    pool_delta = here(
        pool_inv
        * (
            norm_gain[4:5] * pool_up
            - norm_gain[4:5] * pool_bias_grad / images
            - pool_normed * norm_gain[4:5] * pool_gain_grad / images
        )
    )
    pool_delta = jnp.pad(pool_delta, ((0, 15), (0, 0))).astype(jnp.bfloat16)
    deltas = []
    for k in range(4):
        gain = norm_gain[k : k + 1]
        deltas.append(
            mask
            * inv_std[k : k + 1]
            * (
                gain * branch_up[k]
                - gain * branch_bias_grad[k : k + 1] / count
                - normed[k] * gain * branch_gain_grad[k : k + 1] / count
            )
        )
    delta = jnp.concatenate(deltas, axis=1).astype(jnp.bfloat16)
    near = [delta] + [place.swap(delta, zl=k) for k in range(1, nzl)]
    spread_deltas = near + [place.swap(v, c=1) for v in near]

    grads = weight_gradients(shape, info, bands, spread_deltas, pool_delta, pooled)
    inputs = input_gradient(shape, info, areas, spread_deltas, pool_delta, whole_mask, weights)

    returned = []
    for k in range(nr):
        k0, k1 = divmod(k, nzl)
        returned.append(place.send(inputs[k], lambda m, c, zh, zl: (m, zh, c ^ k0, zl ^ k1)))
    returned = by_xor(returned, place.z)
    feature_gradient = jnp.stack([r.reshape(band, channels // (LANES * nr), LANES) for r in returned], axis=2)

    if pieces:
        pairs = [[grads[2 * rel], grads[2 * rel + 1]] for rel in range(4)]
        dilated_gradient, pointwise_gradient, pooling_gradient = line_back(place, plane_scatter(place, pairs))
    else:
        dilated_gradient, pointwise_gradient, pooling_gradient = scattered_tiles(place, grads[0])
    projection_gradient = lax.psum_scatter(projection_partial, "dp", scatter_dimension=0, tiled=True)
    projection_gradient = lax.psum_scatter(projection_gradient, "rows", scatter_dimension=1, tiled=True)

    return (
        output.reshape(cotangent.shape),
        feature_gradient.reshape(features.shape),
        pointwise_gradient,
        pooling_gradient,
        dilated_gradient,
        projection_gradient.astype(jnp.float32),
        jnp.concatenate([branch_gain_grad, pool_gain_grad, proj_gain_grad], axis=0),
        jnp.concatenate([branch_bias_grad, pool_bias_grad, proj_bias_grad], axis=0),
    )


def solution(mesh):
    banded = P("dp", "rows", None, None)
    blocks = P("dp", "rows")
    return jax.shard_map(
        on_device,
        mesh=mesh,
        in_specs=(banded, P("dp", None), blocks, blocks, blocks, blocks, P(), P(), banded),
        out_specs=(banded, banded, blocks, blocks, blocks, blocks, P(), P()),
        check_vma=False,
    )
```

```python
import jax
import jax.numpy as jnp
from jax import lax
from jax.experimental import pallas as pl
from jax.experimental.pallas import tpu as pltpu
from jax.sharding import PartitionSpec as P

epsilon = 1e-05
dilations = (6, 12, 18)
LANES = 128
BLOCK_ROWS = 6
AXES = ("dp", "rows")
FULL, SHORT, PER_CHIP = 14, 13, 27
SLOTS = FULL + 2 + SHORT
CUT = 15
NT = (((1,), (1,)), ((), ()))
TN = (((0,), (0,)), ((), ()))
NN = (((1,), (0,)), ((), ()))


def dot(first, second, dims):
    return lax.dot_general(first, second, dims, preferred_element_type=jnp.float32)


def after(x, *first):
    return lax.optimization_barrier((x, first))[0]


def silu_slope(values):
    sigma = jax.nn.sigmoid(values)
    return sigma * (1.0 + values * (1.0 - sigma))


class Place:
    def __init__(self):
        self.nd, self.nr = lax.axis_size("dp"), lax.axis_size("rows")
        self.nzl = self.nr // 2
        d, z = lax.axis_index("dp"), lax.axis_index("rows")
        self.d, self.z = d, z
        self.m, self.c = d // 2, d % 2
        self.zh, self.zl = z // self.nzl, z % self.nzl
        self.part = self.c * self.nzl + self.zl
        self.image = 2 * self.m + self.zh

    def swap(self, x, m=0, c=0, zh=0, zl=0):
        nzl = self.nzl
        pairs = []
        for flat in range(self.nd * self.nr):
            d, z = divmod(flat, self.nr)
            pairs.append((flat, (d ^ (2 * m + c)) * self.nr + (z ^ (zh * nzl + zl))))
        return lax.ppermute(x, AXES, pairs)


def by_xor(items, index):
    items = list(items)
    bit = 1
    while bit < len(items):
        flip = (index & bit) != 0
        pick = lambda a, b: jnp.where(flip, a, b)
        items = [jax.tree.map(pick, items[k ^ bit], items[k]) for k in range(len(items))]
        bit *= 2
    return items


def tree(items):
    items = list(items)
    while len(items) > 1:
        items = [items[i] + items[i + 1] for i in range(0, len(items), 2)]
    return items[0]


def exchange_stages(place):
    return (
        [dict(c=1)],
        [dict(m=k) for k in range(1, place.nd // 2)],
        [dict(zh=k // place.nzl, zl=k % place.nzl) for k in range(1, place.nr)],
    )


def total(place, x):
    for stage in exchange_stages(place):
        x = tree([x] + [place.swap(x, **s) for s in stage])
    return x


def moments(place, sums, squares, count, extra=None):
    width = sums.shape[1]
    k = sums.shape[0]
    rows = [sums, squares, jnp.full((1, width), count, jnp.float32)]
    if extra is not None:
        rows.append(extra)
    x = jnp.concatenate(rows, axis=0)
    for stage in exchange_stages(place):
        xs = [x] + [place.swap(x, **s) for s in stage]
        whole = tree(xs)
        n = whole[2 * k : 2 * k + 1]
        mean = whole[:k] / jnp.maximum(n, 1.0)
        between = []
        for y in xs:
            own = y[2 * k : 2 * k + 1]
            gap = y[:k] / jnp.maximum(own, 1.0) - mean
            between.append(own * gap * gap)
        x = jnp.concatenate([whole[:k], whole[k : 2 * k] + tree(between), whole[2 * k :]], axis=0)
    n = x[2 * k : 2 * k + 1]
    return x[:k] / n, x[k : 2 * k] / n, n, x[2 * k + 1 :]


def local_moments(values, mask, count):
    sums = jnp.sum(values * mask, axis=0, keepdims=True)
    centred = (values - sums / jnp.maximum(count, 1.0)) * mask
    return sums, jnp.sum(centred * centred, axis=0, keepdims=True)


def line_pieces(place, dilated, pointwise, pooling):
    tiles = lambda w: jnp.transpose(w.T.reshape(w.shape[1], w.shape[0] // LANES, LANES), (1, 0, 2))
    dil, one, pool = tiles(dilated), tiles(pointwise), tiles(pooling)
    other = [dil[2 + r :: 4][:SHORT] for r in range(2)]
    got = place.swap(jnp.concatenate(other, axis=0), c=1)
    same = [jnp.concatenate([dil[r::4][:FULL], one[r : r + 1], pool[r : r + 1]], axis=0) for r in range(2)]
    whole = [jnp.concatenate([same[r], got[r * SHORT : (r + 1) * SHORT]], axis=0) for r in range(2)]
    return by_xor(whole, place.zl)


def plane_direct(place, half):
    return place.swap(half, m=1), place.swap(half, m=2)


def plane_diagonal(place, by_x, by_y):
    return place.swap(by_x[:CUT], m=2), place.swap(by_y[CUT:], m=1)


def add_low(first, *others):
    out = first.astype(jnp.float32)
    for o in others:
        out = out + o.astype(jnp.float32)
    return out.astype(jnp.bfloat16)


def plane_scatter(place, pieces):
    first_d, second_d = place.swap(pieces[3][0], m=2), place.swap(pieces[3][1], m=1)
    to_x = jnp.stack([add_low(pieces[1][0], first_d), pieces[1][1]])
    to_y = jnp.stack([pieces[2][0], add_low(pieces[2][1], second_d)])
    by_x, by_y = place.swap(to_x, m=1), place.swap(to_y, m=2)
    return [add_low(pieces[0][q], by_x[q], by_y[q]) for q in range(2)]


def line_back(place, quarters):
    by_kl = by_xor(quarters, place.zl)
    by_part = by_xor([by_kl[0], place.swap(by_kl[1], zl=1)], place.zl)
    same = [p[: FULL + 2] for p in by_part]
    got = place.swap(jnp.concatenate([p[FULL + 2 :] for p in by_part], axis=0), c=1)
    other = [got[r * SHORT : (r + 1) * SHORT] for r in range(2)]
    gap = jnp.zeros((FULL - SHORT,) + other[0].shape[1:], other[0].dtype)
    dil = jnp.stack([s[:FULL] for s in same] + [jnp.concatenate([o, gap], axis=0) for o in other], axis=1)
    dil = dil.reshape((4 * FULL,) + dil.shape[2:])[: 2 * PER_CHIP]
    rows = lambda t: jnp.transpose(t, (1, 0, 2)).reshape(t.shape[1], t.shape[0] * LANES).astype(jnp.float32).T
    one = jnp.stack([s[FULL] for s in same])
    pool = jnp.stack([s[FULL + 1] for s in same])
    return rows(dil), rows(one), rows(pool)


def gathered_tiles(place, dilated, pointwise, pooling):
    whole = []
    for w in (dilated, pointwise, pooling):
        w = lax.all_gather(w, "rows", axis=1, tiled=True)
        w = lax.all_gather(w, "dp", axis=0, tiled=True)
        channels = pointwise.shape[0] * place.nd
        taps = w.shape[0] // channels
        w = w.reshape(taps, channels // (LANES * place.nr), place.nr, LANES, w.shape[1])
        w = lax.dynamic_index_in_dim(w, place.part, 2, keepdims=False)
        whole.append(jnp.transpose(w.reshape(taps, channels // place.nr, w.shape[-1]), (0, 2, 1)))
    return jnp.concatenate(whole, axis=0)


def scattered_tiles(place, gradients):
    outs = []
    taps, half, width = gradients.shape
    for g in (gradients[: taps - 2], gradients[taps - 2 : taps - 1], gradients[taps - 1 :]):
        g = jnp.transpose(g, (0, 2, 1)).reshape(g.shape[0], width // LANES, 1, LANES, half)
        spread = jnp.zeros((g.shape[0], width // LANES, place.nr, LANES, 2 * half), g.dtype)
        g = lax.dynamic_update_slice(spread, g, (0, 0, place.part, 0, place.zh * half)).reshape(-1, 2 * half)
        g = lax.psum_scatter(g, "dp", scatter_dimension=0, tiled=True)
        outs.append(lax.psum_scatter(g, "rows", scatter_dimension=1, tiled=True).astype(jnp.float32))
    return outs


def doubling(place):
    steps = []
    for name, index, size in (("zl", place.zl, place.nzl), ("zh", place.zh, 2), ("c", place.c, 2), ("m", place.m, place.nd // 2)):
        bit = 1
        while bit < size:
            steps.append(({name: bit}, (index & bit) != 0))
            bit *= 2
    return steps


def joined(place, x, step):
    swap, upper = step
    return jnp.stack(by_xor([x, place.swap(x, **swap)], upper.astype(jnp.int32)))


def halved(place, x, step):
    swap, upper = step
    mine = by_xor([x[0], x[1]], upper.astype(jnp.int32))
    return add_low(mine[0], place.swap(mine[1], **swap))


class Shape:
    def __init__(self, band_rows, columns, nr, width, out, pieces):
        self.band_rows, self.columns, self.nr, self.width, self.out = band_rows, columns, nr, width, out
        self.rows = band_rows * nr
        self.band, self.pixels = band_rows * columns, band_rows * columns * nr
        self.block = BLOCK_ROWS * columns
        self.blocks = self.rows // BLOCK_ROWS
        self.pieces = pieces
        self.quarter = out // 4

    def regions(self, dilation):
        cuts = sorted({0, min(dilation, self.rows), max(self.rows - dilation, 0), self.rows})
        for lo, hi in zip(cuts, cuts[1:]):
            yield lo, hi, [r for r in range(3) if 0 <= lo + (r - 1) * dilation and hi + (r - 1) * dilation <= self.rows]


ANY = pl.BlockSpec(memory_space=pl.ANY)
SMEM = pl.BlockSpec(memory_space=pltpu.SMEM)
VMEM = pl.BlockSpec(memory_space=pltpu.VMEM)
PARAMS = pltpu.CompilerParams(vmem_limit_bytes=58 * 2**20)


LIGHT = pl.CostEstimate(flops=0, bytes_accessed=0, transcendentals=0)


def lanes_at(start, size=LANES):
    return pl.ds(pl.multiple_of(start, LANES), size)


def start_bands(shape, refs, scratch, sem, part):
    for k, ref in enumerate(refs):
        pltpu.make_async_copy(ref, scratch.at[pl.ds((part ^ k) * shape.band, shape.band), :], sem.at[k]).start()


def start_cuts(shape, refs, scratch, sem, part):
    for k, cuts in enumerate(refs):
        first = 0
        for ref in cuts:
            place = scratch.at[pl.ds((part ^ k) * shape.band + first, ref.shape[0]), :]
            pltpu.make_async_copy(ref, place, sem.at[k]).start()
            first += ref.shape[0]


def wait_bands(shape, refs, scratch, sem):
    for k, ref in enumerate(refs):
        pltpu.make_async_copy(ref, scratch.at[pl.ds(k * shape.band, shape.band), :], sem.at[k]).wait()


def split_features(shape, features, mask, c):
    tiles, n = shape.width // LANES, shape.nr // 2

    def kernel(info, x, mask_ref, *outs):
        valid = mask_ref[...].astype(jnp.bfloat16)
        for k, out in enumerate(outs):
            for q in range(n):
                for i in range(tiles):
                    at = (i * shape.nr + (info[0] ^ k) * n + q) * LANES
                    out[q, :, i * LANES : (i + 1) * LANES] = x[:, lanes_at(at)] * valid

    return pl.pallas_call(
        kernel,
        out_shape=[jax.ShapeDtypeStruct((n, shape.band, shape.width), jnp.bfloat16)] * 2,
        in_specs=[SMEM, VMEM, VMEM],
        out_specs=[VMEM] * 2,
        compiler_params=PARAMS,
        cost_estimate=LIGHT,
        name="split_features",
    )(c.reshape(1), features, mask)


def join_features(shape, own, other, c, zl):
    tiles, n = shape.width // LANES, shape.nr // 2

    def kernel(info, *refs):
        for k, part in enumerate(refs[: 2 * n]):
            core, q = info[0] ^ (k // n), info[1] ^ (k % n)
            for i in range(tiles):
                at = (i * shape.nr + core * n + q) * LANES
                refs[2 * n][:, lanes_at(at)] = part[:, i * LANES : (i + 1) * LANES]

    return pl.pallas_call(
        kernel,
        out_shape=jax.ShapeDtypeStruct((shape.band, shape.width * shape.nr), jnp.bfloat16),
        in_specs=[SMEM] + [VMEM] * shape.nr,
        out_specs=VMEM,
        compiler_params=PARAMS,
        cost_estimate=LIGHT,
        name="join_features",
    )(jnp.stack([c, zl]).astype(jnp.int32), *own, *other)


def packed_half(shape, zl, pieces):
    size = shape.quarter

    def kernel(info, *refs):
        for kl, ref in enumerate(refs[:2]):
            refs[2][:, pl.ds(pl.multiple_of((info[0] ^ kl) * size, size), size), :] = ref[...]

    return pl.pallas_call(
        kernel,
        out_shape=jax.ShapeDtypeStruct((SLOTS, 2 * size, LANES), jnp.bfloat16),
        in_specs=[SMEM] + [VMEM] * 2,
        out_specs=VMEM,
        compiler_params=PARAMS,
        cost_estimate=LIGHT,
        name="packed_half",
    )(zl.reshape(1), *pieces)


def chip_slot(t, c):
    return jnp.where(jnp.where(c == 0, t < FULL, t >= SHORT), t - SHORT * c, FULL + 2 + t - FULL * (1 - c))


def assembled_weights(shape, info, own, by_x, by_y, diagonal):
    def kernel(info, *refs):
        ins, out, sem = refs[:5], refs[5], refs[6]
        m, c = info[0], info[1]

        def copy(ref, slot, tap, lane):
            pltpu.make_async_copy(ref.at[slot], out.at[tap, :, lanes_at(lane)], sem).start()

        def place(rel, slot, tap, lane):
            if rel < 3:
                copy(ins[rel], slot, tap, lane)
            else:

                @pl.when(slot < CUT)
                def _():
                    copy(ins[3], slot, tap, lane)

                @pl.when(slot >= CUT)
                def _():
                    copy(ins[4], slot - CUT, tap, lane)

        for rel in range(4):
            chip = m ^ rel

            def body(t, carry):
                v = chip * PER_CHIP + t
                place(rel, chip_slot(t, c), v // 4, (v % 4) * LANES)
                return carry

            lax.fori_loop(0, PER_CHIP, body, 0)
            for extra in range(2):
                place(rel, FULL + extra, 27 + extra, chip * LANES)
        pltpu.make_async_copy(out, out, sem).wait()

    return pl.pallas_call(
        kernel,
        out_shape=jax.ShapeDtypeStruct((29, shape.out // 2, shape.width), jnp.bfloat16),
        in_specs=[SMEM] + [ANY] * 5,
        out_specs=VMEM,
        scratch_shapes=[pltpu.SemaphoreType.DMA],
        compiler_params=PARAMS,
        cost_estimate=LIGHT,
        name="assembled_weights",
    )(info, own, by_x, by_y, *diagonal)


def shifted(values, by, columns):
    if by == 0:
        return values
    pixels = values.shape[0]
    source = lax.broadcasted_iota(jnp.int32, (pixels, 1), 0) % columns - by
    return jnp.where((source >= 0) & (source < columns), pltpu.roll(values, by % pixels, 0), 0.0)


def put_halves(shape, c, blk, value, keep, sent, lane):
    half = shape.blocks // 2
    rows, lanes = pl.ds((blk % half) * shape.block, shape.block), slice(lane, lane + shape.out)

    @pl.when(c == blk // half)
    def _():
        keep[rows, lanes] = value

    @pl.when(c != blk // half)
    def _():
        sent[rows, lanes] = value.astype(sent.dtype)


def half_shapes(shape, n):
    half = shape.pixels // 2
    return [
        jax.ShapeDtypeStruct((half, n * shape.out), jnp.float32),
        jax.ShapeDtypeStruct((half, n * shape.out), jnp.bfloat16),
    ]


def start_taps(weights, scratch, sem, taps, zh):
    half = weights[0].shape[1]
    for n, tap in enumerate(taps):
        for kh, ref in enumerate(weights):
            columns = pl.ds(pl.multiple_of((zh ^ kh) * half, half), half)
            pltpu.make_async_copy(ref.at[tap], scratch.at[n, columns], sem.at[n]).start()


def wait_taps(scratch, sem, some):
    for n in some:
        pltpu.make_async_copy(scratch.at[n], scratch.at[n], sem.at[n]).wait()


def dilated_products(shape, branch, x, w, first, y):
    dilation, columns = dilations[branch], shape.columns
    for s in range(3):
        for lo, hi, rs in shape.regions(dilation):
            pixels = jnp.concatenate(
                [x[(lo + (r - 1) * dilation) * columns : (hi + (r - 1) * dilation) * columns, :] for r in rs], axis=1
            )
            taps = jnp.concatenate([w[first + 3 * s + r] for r in rs], axis=1)
            y[s, lo * columns : hi * columns, :] = dot(pixels, taps, NT)


def put_dilated(shape, branch, y, c, keep, sent, lane):
    dilation, columns = dilations[branch], shape.columns
    for blk in range(shape.blocks):
        at = slice(blk * shape.block, (blk + 1) * shape.block)
        z = y[1, at, :] + shifted(y[0, at, :], dilation, columns) + shifted(y[2, at, :], -dilation, columns)
        put_halves(shape, c, blk, z, keep, sent, lane)


def taps_of(branch):
    return [9 * branch + 3 * r + s for s in range(3) for r in range(3)]


def far_sums(shape, info, bands, weights):
    nr = shape.nr

    def kernel(info, *refs):
        ins, weights = refs[:nr], refs[nr : nr + 2]
        keep, sent, x, w, y, band_sem, w_sem = refs[nr + 2 :]
        start_bands(shape, ins, x, band_sem, info[5])
        start_taps(weights, w, w_sem, taps_of(2) + taps_of(1), info[2])
        wait_bands(shape, ins, x, band_sem)
        for n, branch in enumerate((2, 1)):
            wait_taps(w, w_sem, range(9 * n, 9 * n + 9))
            dilated_products(shape, branch, x, w, 9 * n, y)
            put_dilated(shape, branch, y, info[1], keep, sent, n * shape.out)

    return pl.pallas_call(
        kernel,
        out_shape=half_shapes(shape, 2),
        in_specs=[SMEM] + [ANY] * (nr + 2),
        out_specs=[VMEM] * 2,
        scratch_shapes=[
            pltpu.VMEM((shape.pixels, shape.width), jnp.bfloat16),
            pltpu.VMEM((18, shape.out, shape.width), jnp.bfloat16),
            pltpu.VMEM((3, shape.pixels, shape.out), jnp.float32),
            pltpu.SemaphoreType.DMA((nr,)),
            pltpu.SemaphoreType.DMA((18,)),
        ],
        compiler_params=PARAMS,
        cost_estimate=LIGHT,
        name="far_sums",
    )(info, *bands, *weights)


def near_sums(shape, info, area, bands, weights):
    nr = shape.nr

    def kernel(info, area, *refs):
        ins, weights = refs[:nr], refs[nr : nr + 2]
        keep, sent, pooled, lifted, x, w, y, band_sem, w_sem = refs[nr + 2 :]
        start_bands(shape, ins, x, band_sem, info[5])
        start_taps(weights, w, w_sem, taps_of(0) + [27, 28], info[2])
        wait_bands(shape, ins, x, band_sem)
        wait_taps(w, w_sem, range(11))
        dilated_products(shape, 0, x, w, 0, y)
        put_dilated(shape, 0, y, info[1], keep, sent, 0)
        sums = jnp.zeros((1, shape.width), jnp.float32)
        for blk in range(shape.blocks):
            values = x[blk * shape.block : (blk + 1) * shape.block, :]
            sums = sums + jnp.sum(values.astype(jnp.float32), axis=0, keepdims=True)
            put_halves(shape, info[1], blk, dot(values, w[9], NT), keep, sent, shape.out)
        low = jnp.broadcast_to(sums / area[0], pooled.shape).astype(jnp.bfloat16)
        first = lax.broadcasted_iota(jnp.int32, pooled.shape, 0) == 0
        pooled[...] = jnp.where(first, low.astype(jnp.float32), 0.0).astype(jnp.bfloat16)
        lifted[...] = dot(pooled[...], w[10], NT)

    return pl.pallas_call(
        kernel,
        out_shape=half_shapes(shape, 2)
        + [jax.ShapeDtypeStruct((16, shape.width), jnp.bfloat16), jax.ShapeDtypeStruct((16, shape.out), jnp.float32)],
        in_specs=[SMEM, SMEM] + [ANY] * (nr + 2),
        out_specs=[VMEM] * 4,
        scratch_shapes=[
            pltpu.VMEM((shape.pixels, shape.width), jnp.bfloat16),
            pltpu.VMEM((11, shape.out, shape.width), jnp.bfloat16),
            pltpu.VMEM((3, shape.pixels, shape.out), jnp.float32),
            pltpu.SemaphoreType.DMA((nr,)),
            pltpu.SemaphoreType.DMA((11,)),
        ],
        compiler_params=PARAMS,
        cost_estimate=LIGHT,
        name="near_sums",
    )(info, area, *bands, *weights)


def moved_columns(shape, delta, lane, lanes, branch, moved):
    for blk in range(shape.blocks):
        at = slice(blk * shape.block, (blk + 1) * shape.block)
        values = delta[at, lanes_at(lane, lanes)].astype(jnp.float32)
        for s in range(3):
            moved[at, s * lanes : (s + 1) * lanes] = shifted(
                values, (s - 1) * dilations[branch], shape.columns
            ).astype(jnp.bfloat16)


def input_gradient(shape, info, area, deltas, pool_delta, mask, weights):
    nr, columns = shape.nr, shape.columns

    def kernel(info, area, *refs):
        ins, pool_delta, mask, weights = refs[:nr], refs[nr], refs[nr + 1], refs[nr + 2 : nr + 4]
        outs = refs[nr + 4 : 2 * nr + 4]
        delta, moved, w, acc, delta_sem, w_sem = refs[2 * nr + 4 :]
        start_bands(shape, ins, delta, delta_sem, info[4])
        start_taps(weights, w, w_sem, range(29), info[2])
        wait_bands(shape, ins, delta, delta_sem)
        wait_taps(w, w_sem, range(29))
        pool = dot(pool_delta[...], w[28], NN)[0:1] / area[0]
        acc[...] = dot(delta[:, : shape.out], w[27], NN) + pool
        for branch in range(3):
            dilation = dilations[branch]
            moved_columns(shape, delta, (branch + 1) * shape.out, shape.out, branch, moved)
            for lo, hi, rs in shape.regions(dilation):
                rows = [2 - r for r in rs]
                pixels = jnp.concatenate(
                    [moved[(lo - (r - 1) * dilation) * columns : (hi - (r - 1) * dilation) * columns, :] for r in rows],
                    axis=1,
                )
                taps = jnp.concatenate([w[9 * branch + 3 * r + s] for r in rows for s in range(3)], axis=0)
                acc[lo * columns : hi * columns, :] += dot(pixels, taps, NN)
        for k in range(nr):
            at = pl.ds(pl.multiple_of((info[5] ^ k) * shape.band, shape.band), shape.band)
            outs[k][...] = (acc[at, :] * mask[at, :]).astype(jnp.bfloat16)

    return pl.pallas_call(
        kernel,
        out_shape=[jax.ShapeDtypeStruct((shape.band, shape.width), jnp.bfloat16)] * nr,
        in_specs=[SMEM, SMEM] + [ANY] * nr + [VMEM] * 2 + [ANY] * 2,
        out_specs=[VMEM] * nr,
        scratch_shapes=[
            pltpu.VMEM((shape.pixels, 4 * shape.out), jnp.bfloat16),
            pltpu.VMEM((shape.pixels, 3 * shape.out), jnp.bfloat16),
            pltpu.VMEM((29, shape.out, shape.width), jnp.bfloat16),
            pltpu.VMEM((shape.pixels, shape.width), jnp.float32),
            pltpu.SemaphoreType.DMA((nr,)),
            pltpu.SemaphoreType.DMA((29,)),
        ],
        compiler_params=PARAMS,
        cost_estimate=pl.CostEstimate(
            flops=44 * shape.pixels * shape.width * shape.out, bytes_accessed=2**24, transcendentals=0
        ),
        name="input_gradient",
    )(info, area, *deltas, pool_delta, mask, *weights)


def weight_gradients(shape, info, bands, far_bands, deltas, far_deltas, pool_deltas, pooled):
    nr, columns, half = shape.nr, shape.columns, shape.out // 2
    n_outs = 8 if shape.pieces else 1
    flat_far = [cut for cuts in far_bands for cut in cuts]
    n_far = len(flat_far)

    def kernel(info, *refs):
        ins, delta_ins, far_delta_ins = (refs[n * nr : (n + 1) * nr] for n in range(3))
        refs = refs[3 * nr :]
        far_flat, refs = refs[:n_far], refs[n_far:]
        flat = iter(far_flat)
        far_ins = [[next(flat) for _ in cuts] for cuts in far_bands]
        pool_deltas, pooled, outs = refs[0], refs[1], refs[2 : 2 + n_outs]
        x, far_x, delta, far_delta, moved, far_moved, sem = refs[2 + n_outs :]
        m, c, zh, part, z = info[0], info[1], info[2], info[4], info[5]
        start_bands(shape, delta_ins, delta, sem.at[0], part)
        start_bands(shape, ins, x, sem.at[1], z)
        start_bands(shape, far_delta_ins, far_delta, sem.at[2], part)
        start_cuts(shape, far_ins, far_x, sem.at[3], z)
        for n, target in enumerate((delta, x, far_delta, far_x)):
            for k in range(nr):
                some = target.at[pl.ds(k * shape.band, shape.band)]
                pltpu.make_async_copy(some, some, sem.at[n, k]).wait()

        def put(tap, value):
            value = value.astype(jnp.bfloat16)
            if not shape.pieces:
                outs[0][tap] = value
                return
            for i in range(4):
                if tap < 27:
                    v = 4 * tap + i
                    chip, slot = v // PER_CHIP, chip_slot(v % PER_CHIP, c)
                else:
                    chip, slot = i, FULL + tap - 27
                for rel in range(4):

                    @pl.when((m ^ rel) == chip)
                    def _():
                        for q in range(2):
                            rows = slice(q * shape.quarter, (q + 1) * shape.quarter)
                            outs[2 * rel + q][slot] = value[rows, i * LANES : (i + 1) * LANES]

        for branch in range(3):
            dilation = dilations[branch]
            move = dilation * columns
            moved_columns(shape, delta, (branch + 1) * shape.out + zh * half, half, branch, moved)
            moved_columns(shape, far_delta, (branch + 1) * half, half, branch, far_moved)
            for r in range(3):
                to = slice(max(0, 1 - r) * move, shape.pixels - max(0, r - 1) * move)
                of = slice(max(0, r - 1) * move, shape.pixels - max(0, 1 - r) * move)
                value = dot(moved[to, :], x[of, :], TN) + dot(far_moved[to, :], far_x[of, :], TN)
                for s in range(3):
                    put(9 * branch + 3 * r + s, value[s * half : (s + 1) * half])
        own = delta[:, lanes_at(zh * half, half)]
        put(27, dot(own, x[...], TN) + dot(far_delta[:, :half], far_x[...], TN))
        put(28, dot(pool_deltas[...], pooled[...], TN))

    if shape.pieces:
        out_shape = [jax.ShapeDtypeStruct((SLOTS, shape.quarter, LANES), jnp.bfloat16)] * 8
    else:
        out_shape = [jax.ShapeDtypeStruct((29, half, shape.width), jnp.bfloat16)]
    return pl.pallas_call(
        kernel,
        out_shape=out_shape,
        in_specs=[SMEM] + [ANY] * (3 * nr + n_far) + [VMEM] * 2,
        out_specs=[VMEM] * n_outs,
        scratch_shapes=[
            pltpu.VMEM((shape.pixels, shape.width), jnp.bfloat16),
            pltpu.VMEM((shape.pixels, shape.width), jnp.bfloat16),
            pltpu.VMEM((shape.pixels, 4 * shape.out), jnp.bfloat16),
            pltpu.VMEM((shape.pixels, 2 * shape.out), jnp.bfloat16),
            pltpu.VMEM((shape.pixels, 3 * half), jnp.bfloat16),
            pltpu.VMEM((shape.pixels, 3 * half), jnp.bfloat16),
            pltpu.SemaphoreType.DMA((4, nr)),
        ],
        compiler_params=PARAMS,
        cost_estimate=pl.CostEstimate(
            flops=44 * shape.pixels * shape.width * shape.out, bytes_accessed=2**24, transcendentals=0
        ),
        name="weight_gradients",
    )(info, *bands, *deltas, *far_deltas, *flat_far, pool_deltas, pooled)


def valid_pixels(extent, first_row, rows, columns):
    r = first_row + lax.broadcasted_iota(jnp.int32, (rows, columns), 0)
    w = lax.broadcasted_iota(jnp.int32, (rows, columns), 1)
    return ((r < extent[0]) & (w < extent[1])).astype(jnp.float32).reshape(rows * columns, 1)


def to_logical(place, x):
    return jnp.where(place.zh == place.c, x, place.swap(x, c=1, zh=1))


def on_device(
    features, extent, pointwise_weight, pooling_weight, dilated_weight, projection_weight, norm_gain, norm_bias, cotangent
):
    place = Place()
    nr, nzl = place.nr, place.nzl
    _, band_rows, columns, channels = features.shape
    width, out = channels // nr, norm_gain.shape[1]
    band = band_rows * columns
    pieces = nr == 4 and place.nd == 8 and dilated_weight.shape[0] == 2 * PER_CHIP * LANES
    shape = Shape(band_rows, columns, nr, width, out, pieces)
    images = place.nd

    partner = place.swap(extent, c=1)
    extent_here = jnp.where(place.zh == place.c, extent, partner)[0]
    area = (extent_here[0] * extent_here[1]).astype(jnp.float32)
    mask = valid_pixels(extent_here, place.part * band_rows, band_rows, columns)
    own_mask = valid_pixels(extent[0], place.z * band_rows, band_rows, columns)
    info = jnp.stack([place.m, place.c, place.zh, place.zl, place.part, place.z]).astype(jnp.int32)
    areas = area.reshape(1)

    if pieces:
        sources = line_pieces(place, dilated_weight, pointwise_weight, pooling_weight)
        crossed = place.swap(sources[0], zh=1)
        neighbour = after(place.swap(sources[1], zl=1), crossed)
        near = packed_half(shape, place.zl, [sources[0], neighbour])
        features, near = after((features, near), near)
    own_parts, other_parts = split_features(shape, features.reshape(band, channels), own_mask, place.c)
    held = by_xor([own_parts, place.swap(other_parts, c=1)], place.c)
    held = [by_xor([v[q] for q in range(nzl)], place.zl) for v in by_xor(held, place.zh)]
    line = [divmod(k, nzl) for k in range(nr)]

    def sent(image, k, some=slice(None), first=()):
        kh, kl = divmod(k, nzl)
        v = held[kh ^ image][kl][some]
        return place.swap(after(v, first), zh=kh, zl=kl) if k else v

    middle = band // 32 * 16
    cuts = [slice(0, middle), slice(middle, band)]
    steps = doubling(place)
    nd_bits = (place.nd // 2).bit_length() - 1
    projection = projection_weight.T
    if pieces:
        neighbour = place.swap(neighbour, zh=1)
        near_x, near_y = plane_direct(place, near)
        bands = [sent(0, k) for k in range(nzl)]
        projection = joined(place, projection, steps[0])
        far = packed_half(shape, place.zl, [crossed, after(neighbour, near_x, near_y, bands, projection)])
        near_d = plane_diagonal(place, near_x, near_y)
        bands.append(sent(0, nzl, first=neighbour))
        far_x, far_y = plane_direct(place, far)
        near = assembled_weights(shape, info, near, near_x, near_y, near_d)
        far_d = plane_diagonal(place, after(far_x, bands, near), far_y)
        bands.append(sent(0, nzl + 1, first=bands))
        weights = [near, assembled_weights(shape, info, far, far_x, far_y, far_d)]
    else:
        projection = joined(place, projection, steps[0])
        bands = [sent(0, k) for k in range(nr)]
        weights = gathered_tiles(place, dilated_weight, pointwise_weight, pooling_weight)
        weights = by_xor([weights[:, : out // 2], weights[:, out // 2 :]], place.zh)

    def reduce(keep, got):
        half = keep + got.astype(jnp.float32)
        rows = half.reshape(nzl, band, half.shape[1])
        mine = lax.dynamic_index_in_dim(rows, place.zl, 0, keepdims=False)
        for k in range(1, nzl):
            other = lax.dynamic_index_in_dim(rows, place.zl ^ k, 0, keepdims=False).astype(jnp.bfloat16)
            mine = mine + place.swap(other, zl=k).astype(jnp.float32)
        return mine

    whole_mask = after(valid_pixels(extent_here, 0, shape.rows, columns), bands)
    ready = (bands, weights)
    keep, given = far_sums(shape, info, bands, weights)
    far_bands = [[sent(1, k, first=ready)] for k in range(nzl)] + [[sent(1, nzl, cuts[0], ready)]]
    for step in steps[1:-nd_bits]:
        projection = joined(place, after(projection, ready), step)
    got = place.swap(after(given, far_bands), c=1)
    wide = reduce(keep, got)
    upstream_low = to_logical(place, after(cotangent.reshape(band, out), got))
    keep, given, pooled, lifted = near_sums(shape, info, areas, after(bands, got, projection, whole_mask), weights)
    for step in steps[-nd_bits:-1]:
        projection = joined(place, after(projection, got), step)
    got = place.swap(after(given, projection, upstream_low), c=1)
    projection = joined(place, after(projection, got), steps[-1])
    far_bands += [[sent(1, k, cuts[0], got)] for k in range(nzl + 1, nr)]
    narrow = after(reduce(keep, got), projection, far_bands)
    projection = projection.reshape((place.nd, nr) + projection_weight.shape[::-1])
    projection = jnp.transpose(projection, (1, 2, 0, 3)).reshape(out, -1)
    z = [narrow[:, out:], narrow[:, :out], wide[:, out:], wide[:, :out]]

    local_count = jnp.sum(mask)
    stats = [local_moments(v, mask, local_count) for v in z]
    table = (lax.broadcasted_iota(jnp.int32, (images, 1), 0) == place.image).astype(jnp.float32) * lifted[0:1]
    average, spread, count, pool_pre = moments(
        place,
        jnp.concatenate([s for s, _ in stats], axis=0),
        jnp.concatenate([q for _, q in stats], axis=0),
        local_count,
        table,
    )
    inv_std = lax.rsqrt(spread + epsilon)
    normed = [(z[k] - average[k : k + 1]) * inv_std[k : k + 1] for k in range(4)]
    pre_act = [norm_gain[k : k + 1] * normed[k] + norm_bias[k : k + 1] for k in range(4)]

    pool_average = jnp.mean(pool_pre, axis=0, keepdims=True)
    pool_centred = pool_pre - pool_average
    pool_inv = lax.rsqrt(jnp.mean(pool_centred * pool_centred, axis=0, keepdims=True) + epsilon)
    pool_normed = pool_centred * pool_inv
    pool_lift = norm_gain[4:5] * pool_normed + norm_bias[4:5]
    here = lambda rows: lax.dynamic_slice_in_dim(rows, place.image, 1, axis=0)
    pool_act = here(jax.nn.silu(pool_lift))

    concat = jnp.concatenate([jax.nn.silu(u) * mask for u in pre_act] + [pool_act * mask], axis=1).astype(jnp.bfloat16)
    pooled_far = place.swap(pooled, zh=1)
    proj_pre = dot(concat, projection, NT)
    proj_sums, proj_squares = local_moments(proj_pre, mask, local_count)
    proj_average, proj_spread, _, _ = moments(place, proj_sums, proj_squares, local_count)
    proj_inv = lax.rsqrt(proj_spread + epsilon)
    proj_normed = (proj_pre - proj_average) * proj_inv
    proj_lift = norm_gain[5:6] * proj_normed + norm_bias[5:6]
    output = to_logical(place, (jax.nn.silu(proj_lift) * mask).astype(jnp.bfloat16))

    upstream = upstream_low.astype(jnp.float32) * mask * silu_slope(proj_lift)
    sums = jnp.concatenate(
        [jnp.sum(upstream * proj_normed, axis=0, keepdims=True), jnp.sum(upstream, axis=0, keepdims=True)], axis=0
    )
    proj_totals = total(place, sums)
    proj_gain_grad, proj_bias_grad = proj_totals[0:1], proj_totals[1:2]
    gain = norm_gain[5:6]
    proj_delta = (
        mask
        * proj_inv
        * (gain * upstream - gain * proj_bias_grad / count - proj_normed * gain * proj_gain_grad / count)
    ).astype(jnp.bfloat16)
    concat_grad = dot(proj_delta, projection, NN)
    projection_partial = lambda first: dot(after(proj_delta, first), concat, TN)
    branch_up = [
        concat_grad[:, k * out : (k + 1) * out] * mask * silu_slope(pre_act[k]) for k in range(4)
    ]
    pool_part = jnp.sum(concat_grad[:, 4 * out :] * mask, axis=0, keepdims=True)
    table = (lax.broadcasted_iota(jnp.int32, (images, 1), 0) == place.image).astype(jnp.float32) * pool_part
    totals = total(
        place,
        after(jnp.concatenate(
            [jnp.sum(branch_up[k] * normed[k], axis=0, keepdims=True) for k in range(4)]
            + [jnp.sum(branch_up[k], axis=0, keepdims=True) for k in range(4)]
            + [table],
            axis=0,
        ), output, pooled_far),
    )
    branch_gain_grad, branch_bias_grad = totals[:4], totals[4:8]
    pool_up = totals[8:] * silu_slope(pool_lift)
    pool_gain_grad = jnp.sum(pool_up * pool_normed, axis=0, keepdims=True)
    pool_bias_grad = jnp.sum(pool_up, axis=0, keepdims=True)
    pool_deltas = pool_inv * (
        norm_gain[4:5] * pool_up
        - norm_gain[4:5] * pool_bias_grad / images
        - pool_normed * norm_gain[4:5] * pool_gain_grad / images
    )
    low_rows = lambda rows: jnp.pad(rows, ((0, 16 - rows.shape[0]), (0, 0))).astype(jnp.bfloat16)
    pool_pair = lax.dynamic_slice_in_dim(pool_deltas, 2 * place.m, 2, axis=0)
    halves = lambda v, n: by_xor([v[:, n * out : n * out + out // 2], v[:, n * out + out // 2 : (n + 1) * out]], place.zh)
    deltas = []
    for k in range(4):
        gain = norm_gain[k : k + 1]
        deltas.append(
            mask
            * inv_std[k : k + 1]
            * (
                gain * branch_up[k]
                - gain * branch_bias_grad[k : k + 1] / count
                - normed[k] * gain * branch_gain_grad[k : k + 1] / count
            )
        )
    delta = jnp.concatenate(deltas, axis=1).astype(jnp.bfloat16)
    crossing = jnp.concatenate([halves(delta, k)[1] for k in range(4)], axis=1)

    def over_group(v, first):
        near = [v] + [after(place.swap(v, zl=k), first) for k in range(1, nzl)]
        return near + [place.swap(n, c=1) for n in near]

    crossing = place.swap(crossing, zh=1)
    spread_deltas = over_group(delta, crossing)
    far_deltas = [crossing] + [place.swap(crossing, zl=k) for k in range(1, nzl)]
    inputs = input_gradient(shape, info, areas, spread_deltas, low_rows(here(pool_deltas)), whole_mask, weights)

    for k in range(nzl, nr):
        far_bands[k].append(sent(1, k, cuts[1], spread_deltas))
    rows = projection_weight.shape[0]
    part = projection_partial(spread_deltas).astype(jnp.bfloat16).reshape(nr, out // nr, images * rows)
    mine = by_xor([part[k] for k in range(nr)], place.z)
    part = add_low(mine[0], *[place.swap(mine[k], zh=k // nzl, zl=k % nzl) for k in range(1, nr)])
    crossing = after(far_deltas, inputs, part, far_bands)
    part = jnp.transpose(part.reshape(out // nr, images, rows), (1, 0, 2)).reshape(-1, 2, out // nr, rows)
    part = halved(place, [part[:, k] for k in range(2)], steps[-nd_bits - 1])

    pooled_pair = pooled + jnp.roll(pooled_far, 1, axis=0)
    pool_pair = jnp.concatenate([pool_pair[i : i + 1] for i in range(2)], axis=0)
    pool_pair = jnp.concatenate(by_xor([pool_pair[0:1], pool_pair[1:2]], place.zh), axis=0)
    pool_pair = halves(low_rows(pool_pair), 0)[0]
    far_deltas = crossing + [place.swap(n, c=1) for n in crossing]
    grads = weight_gradients(shape, info, bands, far_bands, spread_deltas, far_deltas, pool_pair, pooled_pair)

    returned = [place.swap(inputs[k], zh=kh, zl=kl) if k else inputs[0] for k, (kh, kl) in enumerate(line)]
    returned = by_xor(by_xor([returned[:nzl], returned[nzl:]], place.zh), place.c)
    traded = place.swap(jnp.stack(returned[1]), c=1)
    feature_gradient = join_features(shape, returned[0], [traded[k] for k in range(nzl)], place.c, place.zl)

    if pieces:
        pairs = [[grads[2 * rel], grads[2 * rel + 1]] for rel in range(4)]
        quarters = plane_scatter(place, pairs)
        dilated_gradient, pointwise_gradient, pooling_gradient = line_back(place, quarters)
    else:
        dilated_gradient, pointwise_gradient, pooling_gradient = scattered_tiles(place, grads[0])

    if pieces:
        part = after(part, quarters)
    for step in steps[-nd_bits:]:
        part = part.reshape(-1, 2, out // nr, rows)
        part = halved(place, [part[:, k] for k in range(2)], step)
    projection_gradient = part.reshape(out // nr, rows).astype(jnp.float32).T

    return (
        output.reshape(cotangent.shape),
        feature_gradient.reshape(features.shape),
        pointwise_gradient,
        pooling_gradient,
        dilated_gradient,
        projection_gradient,
        jnp.concatenate([branch_gain_grad, pool_gain_grad, proj_gain_grad], axis=0),
        jnp.concatenate([branch_bias_grad, pool_bias_grad, proj_bias_grad], axis=0),
    )


def solution(mesh):
    banded = P("dp", "rows", None, None)
    blocks = P("dp", "rows")
    return jax.shard_map(
        on_device,
        mesh=mesh,
        in_specs=(banded, P("dp", None), blocks, blocks, blocks, blocks, P(), P(), banded),
        out_specs=(banded, banded, blocks, blocks, blocks, blocks, P(), P()),
        check_vma=False,
    )
```

```python
import jax
import jax.numpy as jnp
from jax import lax
from jax.experimental import pallas as pl
from jax.experimental.pallas import tpu as pltpu
from jax.sharding import PartitionSpec as P

epsilon = 1e-05
dilations = (6, 12, 18)
LANES = 128
BLOCK_ROWS = 6
AXES = ("dp", "rows")
FULL, SHORT, PER_CHIP = 14, 13, 27
SLOTS = FULL + 2 + SHORT
FIRST = 14
CUT = 15
NT = (((1,), (1,)), ((), ()))
TN = (((0,), (0,)), ((), ()))
NN = (((1,), (0,)), ((), ()))


def dot(first, second, dims):
    return lax.dot_general(first, second, dims, preferred_element_type=jnp.float32)


def after(x, *first):
    return lax.optimization_barrier((x, first))[0]


def silu_slope(values):
    sigma = jax.nn.sigmoid(values)
    return sigma * (1.0 + values * (1.0 - sigma))


class Place:
    def __init__(self):
        self.nd, self.nr = lax.axis_size("dp"), lax.axis_size("rows")
        self.nzl = self.nr // 2
        d, z = lax.axis_index("dp"), lax.axis_index("rows")
        self.d, self.z = d, z
        self.m, self.c = d // 2, d % 2
        self.zh, self.zl = z // self.nzl, z % self.nzl
        self.part = self.c * self.nzl + self.zl
        self.image = 2 * self.m + self.zh

    def swap(self, x, m=0, c=0, zh=0, zl=0):
        nzl = self.nzl
        pairs = []
        for flat in range(self.nd * self.nr):
            d, z = divmod(flat, self.nr)
            pairs.append((flat, (d ^ (2 * m + c)) * self.nr + (z ^ (zh * nzl + zl))))
        return lax.ppermute(x, AXES, pairs)


def by_xor(items, index):
    items = list(items)
    bit = 1
    while bit < len(items):
        flip = (index & bit) != 0
        pick = lambda a, b: jnp.where(flip, a, b)
        items = [jax.tree.map(pick, items[k ^ bit], items[k]) for k in range(len(items))]
        bit *= 2
    return items


def tree(items):
    items = list(items)
    while len(items) > 1:
        items = [items[i] + items[i + 1] for i in range(0, len(items), 2)]
    return items[0]


def exchange_stages(place):
    return (
        [dict(c=1)],
        [dict(m=k) for k in range(1, place.nd // 2)],
        [dict(zh=k // place.nzl, zl=k % place.nzl) for k in range(1, place.nr)],
    )


def total(place, x):
    for stage in exchange_stages(place):
        x = tree([x] + [place.swap(x, **s) for s in stage])
    return x


def moments(place, sums, squares, count, extra=None):
    width = sums.shape[1]
    k = sums.shape[0]
    rows = [sums, squares, jnp.full((1, width), count, jnp.float32)]
    if extra is not None:
        rows.append(extra)
    x = jnp.concatenate(rows, axis=0)
    for stage in exchange_stages(place):
        xs = [x] + [place.swap(x, **s) for s in stage]
        whole = tree(xs)
        n = whole[2 * k : 2 * k + 1]
        mean = whole[:k] / jnp.maximum(n, 1.0)
        between = []
        for y in xs:
            own = y[2 * k : 2 * k + 1]
            gap = y[:k] / jnp.maximum(own, 1.0) - mean
            between.append(own * gap * gap)
        x = jnp.concatenate([whole[:k], whole[k : 2 * k] + tree(between), whole[2 * k :]], axis=0)
    n = x[2 * k : 2 * k + 1]
    return x[:k] / n, x[k : 2 * k] / n, n, x[2 * k + 1 :]


def local_moments(values, mask, count):
    sums = jnp.sum(values * mask, axis=0, keepdims=True)
    centred = (values - sums / jnp.maximum(count, 1.0)) * mask
    return sums, jnp.sum(centred * centred, axis=0, keepdims=True)


def line_pieces(place, dilated, pointwise, pooling):
    tiles = lambda w: jnp.transpose(w.T.reshape(w.shape[1], w.shape[0] // LANES, LANES), (1, 0, 2))
    dil, one, pool = tiles(dilated), tiles(pointwise), tiles(pooling)
    other = [dil[2 + r :: 4][:SHORT] for r in range(2)]
    got = place.swap(jnp.concatenate(other, axis=0), c=1)
    same = [jnp.concatenate([dil[r::4][:FULL], one[r : r + 1], pool[r : r + 1]], axis=0) for r in range(2)]
    whole = [jnp.concatenate([same[r], got[r * SHORT : (r + 1) * SHORT]], axis=0) for r in range(2)]
    return by_xor(whole, place.zl)


def plane_direct(place, half):
    return place.swap(half, m=1), place.swap(half, m=2)


def plane_diagonal(place, by_x, by_y):
    return place.swap(by_x[:CUT], m=2), place.swap(by_y[CUT:], m=1)


def add_low(first, *others):
    out = first.astype(jnp.float32)
    for o in others:
        out = out + o.astype(jnp.float32)
    return out.astype(jnp.bfloat16)


def plane_scatter_diagonal(place, pieces):
    return place.swap(pieces[3][0], m=2), place.swap(pieces[3][1], m=1)


def plane_scatter(place, pieces, first_d, second_d):
    to_x = jnp.stack([add_low(pieces[1][0], first_d), pieces[1][1]])
    to_y = jnp.stack([pieces[2][0], add_low(pieces[2][1], second_d)])
    by_x, by_y = place.swap(to_x, m=1), place.swap(to_y, m=2)
    return [add_low(pieces[0][q], by_x[q], by_y[q]) for q in range(2)]


def line_back(place, quarters, first):
    by_kl = by_xor(quarters, place.zl)
    by_part = by_xor([by_kl[0], after(place.swap(by_kl[1], zl=1), first)], place.zl)
    same = [p[: FULL + 2] for p in by_part]
    got = place.swap(jnp.concatenate([p[FULL + 2 :] for p in by_part], axis=0), c=1)
    other = [got[r * SHORT : (r + 1) * SHORT] for r in range(2)]
    gap = jnp.zeros((FULL - SHORT,) + other[0].shape[1:], other[0].dtype)
    dil = jnp.stack([s[:FULL] for s in same] + [jnp.concatenate([o, gap], axis=0) for o in other], axis=1)
    dil = dil.reshape((4 * FULL,) + dil.shape[2:])[: 2 * PER_CHIP]
    rows = lambda t: jnp.transpose(t, (1, 0, 2)).reshape(t.shape[1], t.shape[0] * LANES).astype(jnp.float32).T
    one = jnp.stack([s[FULL] for s in same])
    pool = jnp.stack([s[FULL + 1] for s in same])
    return rows(dil), rows(one), rows(pool)


def gathered_tiles(place, dilated, pointwise, pooling):
    whole = []
    for w in (dilated, pointwise, pooling):
        w = lax.all_gather(w, "rows", axis=1, tiled=True)
        w = lax.all_gather(w, "dp", axis=0, tiled=True)
        channels = pointwise.shape[0] * place.nd
        taps = w.shape[0] // channels
        w = w.reshape(taps, channels // (LANES * place.nr), place.nr, LANES, w.shape[1])
        w = lax.dynamic_index_in_dim(w, place.part, 2, keepdims=False)
        whole.append(jnp.transpose(w.reshape(taps, channels // place.nr, w.shape[-1]), (0, 2, 1)))
    return jnp.concatenate(whole, axis=0)


def scattered_tiles(place, gradients):
    outs = []
    taps, half, width = gradients.shape
    for g in (gradients[: taps - 2], gradients[taps - 2 : taps - 1], gradients[taps - 1 :]):
        g = jnp.transpose(g, (0, 2, 1)).reshape(g.shape[0], width // LANES, 1, LANES, half)
        spread = jnp.zeros((g.shape[0], width // LANES, place.nr, LANES, 2 * half), g.dtype)
        g = lax.dynamic_update_slice(spread, g, (0, 0, place.part, 0, place.zh * half)).reshape(-1, 2 * half)
        g = lax.psum_scatter(g, "dp", scatter_dimension=0, tiled=True)
        outs.append(lax.psum_scatter(g, "rows", scatter_dimension=1, tiled=True).astype(jnp.float32))
    return outs


def doubling(place):
    steps = []
    for name, index, size in (("zl", place.zl, place.nzl), ("zh", place.zh, 2), ("c", place.c, 2), ("m", place.m, place.nd // 2)):
        bit = 1
        while bit < size:
            steps.append(({name: bit}, (index & bit) != 0))
            bit *= 2
    return steps


def joined(place, x, step):
    swap, upper = step
    return jnp.stack(by_xor([x, place.swap(x, **swap)], upper.astype(jnp.int32)))


def halved(place, x, step):
    swap, upper = step
    mine = by_xor([x[0], x[1]], upper.astype(jnp.int32))
    return add_low(mine[0], place.swap(mine[1], **swap))


def m_halved(place, x, steps, first):
    for step in [step for step in steps if "m" in step[0]]:
        if (step[0]["m"] == 1) == (first == 1):
            x = x.reshape((-1, 2) + x.shape[1:])
            x = halved(place, [x[:, k] for k in range(2)], step)
    return x


class Shape:
    def __init__(self, band_rows, columns, nr, width, out, pieces):
        self.band_rows, self.columns, self.nr, self.width, self.out = band_rows, columns, nr, width, out
        self.rows = band_rows * nr
        self.band, self.pixels = band_rows * columns, band_rows * columns * nr
        self.block = BLOCK_ROWS * columns
        self.blocks = self.rows // BLOCK_ROWS
        self.pieces = pieces
        self.quarter = out // 4

    def regions(self, dilation):
        cuts = sorted({0, min(dilation, self.rows), max(self.rows - dilation, 0), self.rows})
        for lo, hi in zip(cuts, cuts[1:]):
            yield lo, hi, [r for r in range(3) if 0 <= lo + (r - 1) * dilation and hi + (r - 1) * dilation <= self.rows]


ANY = pl.BlockSpec(memory_space=pl.ANY)
SMEM = pl.BlockSpec(memory_space=pltpu.SMEM)
VMEM = pl.BlockSpec(memory_space=pltpu.VMEM)
PARAMS = pltpu.CompilerParams(vmem_limit_bytes=58 * 2**20)


LIGHT = pl.CostEstimate(flops=0, bytes_accessed=0, transcendentals=0)


def lanes_at(start, size=LANES):
    return pl.ds(pl.multiple_of(start, LANES), size)


def start_bands(shape, refs, scratch, sem, part):
    for k, ref in enumerate(refs):
        pltpu.make_async_copy(ref, scratch.at[pl.ds((part ^ k) * shape.band, shape.band), :], sem.at[k]).start()


def start_cuts(shape, refs, scratch, sem, part):
    for k, cuts in enumerate(refs):
        first = 0
        for ref in cuts:
            place = scratch.at[pl.ds((part ^ k) * shape.band + first, ref.shape[0]), :]
            pltpu.make_async_copy(ref, place, sem.at[k]).start()
            first += ref.shape[0]


def wait_bands(shape, refs, scratch, sem):
    for k, ref in enumerate(refs):
        pltpu.make_async_copy(ref, scratch.at[pl.ds(k * shape.band, shape.band), :], sem.at[k]).wait()


def split_features(shape, features, mask, c):
    tiles, n = shape.width // LANES, shape.nr // 2

    def kernel(info, x, mask_ref, *outs):
        valid = mask_ref[...].astype(jnp.bfloat16)
        for k, out in enumerate(outs):
            for q in range(n):
                for i in range(tiles):
                    at = (i * shape.nr + (info[0] ^ k) * n + q) * LANES
                    out[q, :, i * LANES : (i + 1) * LANES] = x[:, lanes_at(at)] * valid

    return pl.pallas_call(
        kernel,
        out_shape=[jax.ShapeDtypeStruct((n, shape.band, shape.width), jnp.bfloat16)] * 2,
        in_specs=[SMEM, VMEM, VMEM],
        out_specs=[VMEM] * 2,
        compiler_params=PARAMS,
        cost_estimate=LIGHT,
        name="split_features",
    )(c.reshape(1), features, mask)


def join_features(shape, own, other, c, zl):
    tiles, n = shape.width // LANES, shape.nr // 2

    def kernel(info, *refs):
        for k, part in enumerate(refs[: 2 * n]):
            core, q = info[0] ^ (k // n), info[1] ^ (k % n)
            for i in range(tiles):
                at = (i * shape.nr + core * n + q) * LANES
                refs[2 * n][:, lanes_at(at)] = part[:, i * LANES : (i + 1) * LANES]

    return pl.pallas_call(
        kernel,
        out_shape=jax.ShapeDtypeStruct((shape.band, shape.width * shape.nr), jnp.bfloat16),
        in_specs=[SMEM] + [VMEM] * shape.nr,
        out_specs=VMEM,
        compiler_params=PARAMS,
        cost_estimate=LIGHT,
        name="join_features",
    )(jnp.stack([c, zl]).astype(jnp.int32), *own, *other)


def packed_near(shape, zl, own, neighbour):
    size = shape.quarter

    def kernel(info, own, neighbour, out, rest):
        for kl, ref in enumerate((own, neighbour)):
            out[:, pl.ds(pl.multiple_of((info[0] ^ kl) * size, size), size), :] = ref[...]
        rest[: SLOTS - FIRST] = own[FIRST:]
        rest[SLOTS - FIRST :] = neighbour[...]

    return pl.pallas_call(
        kernel,
        out_shape=[
            jax.ShapeDtypeStruct((SLOTS, 2 * size, LANES), jnp.bfloat16),
            jax.ShapeDtypeStruct((2 * SLOTS - FIRST, size, LANES), jnp.bfloat16),
        ],
        in_specs=[SMEM, VMEM, VMEM],
        out_specs=[VMEM, VMEM],
        compiler_params=PARAMS,
        cost_estimate=LIGHT,
        name="packed_near",
    )(zl.reshape(1), own, neighbour)


def packed_far(shape, zl, first, rest):
    size = shape.quarter

    def kernel(info, first, rest, out):
        for kl in range(2):
            columns = pl.ds(pl.multiple_of((info[0] ^ kl) * size, size), size)
            if kl == 0:
                out[:FIRST, columns, :] = first[...]
                out[FIRST:, columns, :] = rest[: SLOTS - FIRST]
            else:
                out[:, columns, :] = rest[SLOTS - FIRST :]

    return pl.pallas_call(
        kernel,
        out_shape=jax.ShapeDtypeStruct((SLOTS, 2 * size, LANES), jnp.bfloat16),
        in_specs=[SMEM, VMEM, VMEM],
        out_specs=VMEM,
        compiler_params=PARAMS,
        cost_estimate=LIGHT,
        name="packed_far",
    )(zl.reshape(1), first, rest)


def chip_slot(t, c):
    return jnp.where(jnp.where(c == 0, t < FULL, t >= SHORT), t - SHORT * c, FULL + 2 + t - FULL * (1 - c))


def assembled_weights(shape, info, own, by_x, by_y, diagonal):
    def kernel(info, *refs):
        ins, out, sem = refs[:5], refs[5], refs[6]
        m, c = info[0], info[1]

        def copy(ref, slot, tap, lane):
            pltpu.make_async_copy(ref.at[slot], out.at[tap, :, lanes_at(lane)], sem).start()

        def place(rel, slot, tap, lane):
            if rel < 3:
                copy(ins[rel], slot, tap, lane)
            else:

                @pl.when(slot < CUT)
                def _():
                    copy(ins[3], slot, tap, lane)

                @pl.when(slot >= CUT)
                def _():
                    copy(ins[4], slot - CUT, tap, lane)

        for rel in range(4):
            chip = m ^ rel

            def body(t, carry):
                v = chip * PER_CHIP + t
                place(rel, chip_slot(t, c), v // 4, (v % 4) * LANES)
                return carry

            lax.fori_loop(0, PER_CHIP, body, 0)
            for extra in range(2):
                place(rel, FULL + extra, 27 + extra, chip * LANES)
        pltpu.make_async_copy(out, out, sem).wait()

    return pl.pallas_call(
        kernel,
        out_shape=jax.ShapeDtypeStruct((29, shape.out // 2, shape.width), jnp.bfloat16),
        in_specs=[SMEM] + [ANY] * 5,
        out_specs=VMEM,
        scratch_shapes=[pltpu.SemaphoreType.DMA],
        compiler_params=PARAMS,
        cost_estimate=LIGHT,
        name="assembled_weights",
    )(info, own, by_x, by_y, *diagonal)


def shifted(values, by, columns):
    if by == 0:
        return values
    pixels = values.shape[0]
    source = lax.broadcasted_iota(jnp.int32, (pixels, 1), 0) % columns - by
    return jnp.where((source >= 0) & (source < columns), pltpu.roll(values, by % pixels, 0), 0.0)


def put_halves(shape, c, blk, value, keep, sent, lane):
    half = shape.blocks // 2
    rows, lanes = pl.ds((blk % half) * shape.block, shape.block), slice(lane, lane + shape.out)

    @pl.when(c == blk // half)
    def _():
        keep[rows, lanes] = value

    @pl.when(c != blk // half)
    def _():
        sent[rows, lanes] = value.astype(sent.dtype)


def half_shapes(shape, n):
    half = shape.pixels // 2
    return [
        jax.ShapeDtypeStruct((half, n * shape.out), jnp.float32),
        jax.ShapeDtypeStruct((half, n * shape.out), jnp.bfloat16),
    ]


def start_taps(weights, scratch, sem, taps, zh):
    half = weights[0].shape[1]
    for n, tap in enumerate(taps):
        for kh, ref in enumerate(weights):
            columns = pl.ds(pl.multiple_of((zh ^ kh) * half, half), half)
            pltpu.make_async_copy(ref.at[tap], scratch.at[n, columns], sem.at[n]).start()


def wait_taps(scratch, sem, some):
    for n in some:
        pltpu.make_async_copy(scratch.at[n], scratch.at[n], sem.at[n]).wait()


def dilated_products(shape, branch, x, w, first, y):
    dilation, columns = dilations[branch], shape.columns
    for s in range(3):
        for lo, hi, rs in shape.regions(dilation):
            pixels = jnp.concatenate(
                [x[(lo + (r - 1) * dilation) * columns : (hi + (r - 1) * dilation) * columns, :] for r in rs], axis=1
            )
            taps = jnp.concatenate([w[first + 3 * s + r] for r in rs], axis=1)
            y[s, lo * columns : hi * columns, :] = dot(pixels, taps, NT)


def put_dilated(shape, branch, y, c, keep, sent, lane):
    dilation, columns = dilations[branch], shape.columns
    for blk in range(shape.blocks):
        at = slice(blk * shape.block, (blk + 1) * shape.block)
        z = y[1, at, :] + shifted(y[0, at, :], dilation, columns) + shifted(y[2, at, :], -dilation, columns)
        put_halves(shape, c, blk, z, keep, sent, lane)


def taps_of(branch):
    return [9 * branch + 3 * r + s for s in range(3) for r in range(3)]


def far_sums(shape, info, bands, weights):
    nr = shape.nr

    def kernel(info, *refs):
        ins, weights = refs[:nr], refs[nr : nr + 2]
        keep, sent, x, w, y, band_sem, w_sem = refs[nr + 2 :]
        start_bands(shape, ins, x, band_sem, info[5])
        start_taps(weights, w, w_sem, taps_of(2) + taps_of(1), info[2])
        wait_bands(shape, ins, x, band_sem)
        for n, branch in enumerate((2, 1)):
            wait_taps(w, w_sem, range(9 * n, 9 * n + 9))
            dilated_products(shape, branch, x, w, 9 * n, y)
            put_dilated(shape, branch, y, info[1], keep, sent, n * shape.out)

    return pl.pallas_call(
        kernel,
        out_shape=half_shapes(shape, 2),
        in_specs=[SMEM] + [ANY] * (nr + 2),
        out_specs=[VMEM] * 2,
        scratch_shapes=[
            pltpu.VMEM((shape.pixels, shape.width), jnp.bfloat16),
            pltpu.VMEM((18, shape.out, shape.width), jnp.bfloat16),
            pltpu.VMEM((3, shape.pixels, shape.out), jnp.float32),
            pltpu.SemaphoreType.DMA((nr,)),
            pltpu.SemaphoreType.DMA((18,)),
        ],
        compiler_params=PARAMS,
        cost_estimate=LIGHT,
        name="far_sums",
    )(info, *bands, *weights)


def near_sums(shape, info, area, bands, weights):
    nr = shape.nr

    def kernel(info, area, *refs):
        ins, weights = refs[:nr], refs[nr : nr + 2]
        keep, sent, pooled, lifted, x, w, y, band_sem, w_sem = refs[nr + 2 :]
        start_bands(shape, ins, x, band_sem, info[5])
        start_taps(weights, w, w_sem, taps_of(0) + [27, 28], info[2])
        wait_bands(shape, ins, x, band_sem)
        wait_taps(w, w_sem, range(11))
        dilated_products(shape, 0, x, w, 0, y)
        put_dilated(shape, 0, y, info[1], keep, sent, 0)
        sums = jnp.zeros((1, shape.width), jnp.float32)
        for blk in range(shape.blocks):
            values = x[blk * shape.block : (blk + 1) * shape.block, :]
            sums = sums + jnp.sum(values.astype(jnp.float32), axis=0, keepdims=True)
            put_halves(shape, info[1], blk, dot(values, w[9], NT), keep, sent, shape.out)
        low = jnp.broadcast_to(sums / area[0], pooled.shape).astype(jnp.bfloat16)
        first = lax.broadcasted_iota(jnp.int32, pooled.shape, 0) == 0
        pooled[...] = jnp.where(first, low.astype(jnp.float32), 0.0).astype(jnp.bfloat16)
        lifted[...] = dot(pooled[...], w[10], NT)

    return pl.pallas_call(
        kernel,
        out_shape=half_shapes(shape, 2)
        + [jax.ShapeDtypeStruct((16, shape.width), jnp.bfloat16), jax.ShapeDtypeStruct((16, shape.out), jnp.float32)],
        in_specs=[SMEM, SMEM] + [ANY] * (nr + 2),
        out_specs=[VMEM] * 4,
        scratch_shapes=[
            pltpu.VMEM((shape.pixels, shape.width), jnp.bfloat16),
            pltpu.VMEM((11, shape.out, shape.width), jnp.bfloat16),
            pltpu.VMEM((3, shape.pixels, shape.out), jnp.float32),
            pltpu.SemaphoreType.DMA((nr,)),
            pltpu.SemaphoreType.DMA((11,)),
        ],
        compiler_params=PARAMS,
        cost_estimate=LIGHT,
        name="near_sums",
    )(info, area, *bands, *weights)


def moved_columns(shape, delta, lane, lanes, branch, moved):
    for blk in range(shape.blocks):
        at = slice(blk * shape.block, (blk + 1) * shape.block)
        values = delta[at, lanes_at(lane, lanes)].astype(jnp.float32)
        for s in range(3):
            moved[at, s * lanes : (s + 1) * lanes] = shifted(
                values, (s - 1) * dilations[branch], shape.columns
            ).astype(jnp.bfloat16)


def input_gradient(shape, info, area, deltas, pool_delta, weights):
    nr, columns = shape.nr, shape.columns

    def kernel(info, area, *refs):
        ins, pool_delta, weights = refs[:nr], refs[nr], refs[nr + 1 : nr + 3]
        outs = refs[nr + 3 : 2 * nr + 3]
        delta, moved, w, acc, delta_sem, w_sem = refs[2 * nr + 3 :]
        start_bands(shape, ins, delta, delta_sem, info[4])
        start_taps(weights, w, w_sem, range(29), info[2])
        wait_bands(shape, ins, delta, delta_sem)
        wait_taps(w, w_sem, range(29))
        pool = dot(pool_delta[...], w[28], NN)[0:1] / area[0]
        acc[...] = dot(delta[:, : shape.out], w[27], NN) + pool
        for branch in range(3):
            dilation = dilations[branch]
            moved_columns(shape, delta, (branch + 1) * shape.out, shape.out, branch, moved)
            for lo, hi, rs in shape.regions(dilation):
                rows = [2 - r for r in rs]
                pixels = jnp.concatenate(
                    [moved[(lo - (r - 1) * dilation) * columns : (hi - (r - 1) * dilation) * columns, :] for r in rows],
                    axis=1,
                )
                taps = jnp.concatenate([w[9 * branch + 3 * r + s] for r in rows for s in range(3)], axis=0)
                acc[lo * columns : hi * columns, :] += dot(pixels, taps, NN)
        pixel = lax.broadcasted_iota(jnp.int32, (shape.band, 1), 0)
        for k in range(nr):
            first = (info[5] ^ k) * shape.band
            inside = ((pixel + first) // columns < info[6]) & (pixel % columns < info[7])
            values = acc[pl.ds(pl.multiple_of(first, shape.band), shape.band), :]
            outs[k][...] = jnp.where(inside, values, 0.0).astype(jnp.bfloat16)

    return pl.pallas_call(
        kernel,
        out_shape=[jax.ShapeDtypeStruct((shape.band, shape.width), jnp.bfloat16)] * nr,
        in_specs=[SMEM, SMEM] + [ANY] * nr + [VMEM] + [ANY] * 2,
        out_specs=[VMEM] * nr,
        scratch_shapes=[
            pltpu.VMEM((shape.pixels, 4 * shape.out), jnp.bfloat16),
            pltpu.VMEM((shape.pixels, 3 * shape.out), jnp.bfloat16),
            pltpu.VMEM((29, shape.out, shape.width), jnp.bfloat16),
            pltpu.VMEM((shape.pixels, shape.width), jnp.float32),
            pltpu.SemaphoreType.DMA((nr,)),
            pltpu.SemaphoreType.DMA((29,)),
        ],
        compiler_params=PARAMS,
        cost_estimate=pl.CostEstimate(
            flops=44 * shape.pixels * shape.width * shape.out, bytes_accessed=2**24, transcendentals=0
        ),
        name="input_gradient",
    )(info, area, *deltas, pool_delta, *weights)


def weight_gradients(shape, info, bands, far_bands, deltas, far_deltas, pool_deltas, pooled):
    nr, columns, half = shape.nr, shape.columns, shape.out // 2
    n_outs = 8 if shape.pieces else 1
    flat_far = [cut for cuts in far_bands for cut in cuts]
    n_far = len(flat_far)

    def kernel(info, *refs):
        ins, delta_ins, far_delta_ins = (refs[n * nr : (n + 1) * nr] for n in range(3))
        refs = refs[3 * nr :]
        far_flat, refs = refs[:n_far], refs[n_far:]
        flat = iter(far_flat)
        far_ins = [[next(flat) for _ in cuts] for cuts in far_bands]
        pool_deltas, pooled, outs = refs[0], refs[1], refs[2 : 2 + n_outs]
        x, far_x, delta, far_delta, moved, far_moved, sem = refs[2 + n_outs :]
        m, c, zh, part, z = info[0], info[1], info[2], info[4], info[5]
        start_bands(shape, delta_ins, delta, sem.at[0], part)
        start_bands(shape, ins, x, sem.at[1], z)
        start_bands(shape, far_delta_ins, far_delta, sem.at[2], part)
        start_cuts(shape, far_ins, far_x, sem.at[3], z)
        for n, target in enumerate((delta, x, far_delta, far_x)):
            for k in range(nr):
                some = target.at[pl.ds(k * shape.band, shape.band)]
                pltpu.make_async_copy(some, some, sem.at[n, k]).wait()

        def put(tap, value):
            value = value.astype(jnp.bfloat16)
            if not shape.pieces:
                outs[0][tap] = value
                return
            for i in range(4):
                if tap < 27:
                    v = 4 * tap + i
                    chip, slot = v // PER_CHIP, chip_slot(v % PER_CHIP, c)
                else:
                    chip, slot = i, FULL + tap - 27
                for rel in range(4):

                    @pl.when((m ^ rel) == chip)
                    def _():
                        for q in range(2):
                            rows = slice(q * shape.quarter, (q + 1) * shape.quarter)
                            outs[2 * rel + q][slot] = value[rows, i * LANES : (i + 1) * LANES]

        for branch in range(3):
            dilation = dilations[branch]
            move = dilation * columns
            moved_columns(shape, delta, (branch + 1) * shape.out + zh * half, half, branch, moved)
            moved_columns(shape, far_delta, (branch + 1) * half, half, branch, far_moved)
            for r in range(3):
                to = slice(max(0, 1 - r) * move, shape.pixels - max(0, r - 1) * move)
                of = slice(max(0, r - 1) * move, shape.pixels - max(0, 1 - r) * move)
                value = dot(moved[to, :], x[of, :], TN) + dot(far_moved[to, :], far_x[of, :], TN)
                for s in range(3):
                    put(9 * branch + 3 * r + s, value[s * half : (s + 1) * half])
        own = delta[:, lanes_at(zh * half, half)]
        put(27, dot(own, x[...], TN) + dot(far_delta[:, :half], far_x[...], TN))
        put(28, dot(pool_deltas[...], pooled[...], TN))

    if shape.pieces:
        out_shape = [jax.ShapeDtypeStruct((SLOTS, shape.quarter, LANES), jnp.bfloat16)] * 8
    else:
        out_shape = [jax.ShapeDtypeStruct((29, half, shape.width), jnp.bfloat16)]
    return pl.pallas_call(
        kernel,
        out_shape=out_shape,
        in_specs=[SMEM] + [ANY] * (3 * nr + n_far) + [VMEM] * 2,
        out_specs=[VMEM] * n_outs,
        scratch_shapes=[
            pltpu.VMEM((shape.pixels, shape.width), jnp.bfloat16),
            pltpu.VMEM((shape.pixels, shape.width), jnp.bfloat16),
            pltpu.VMEM((shape.pixels, 4 * shape.out), jnp.bfloat16),
            pltpu.VMEM((shape.pixels, 2 * shape.out), jnp.bfloat16),
            pltpu.VMEM((shape.pixels, 3 * half), jnp.bfloat16),
            pltpu.VMEM((shape.pixels, 3 * half), jnp.bfloat16),
            pltpu.SemaphoreType.DMA((4, nr)),
        ],
        compiler_params=PARAMS,
        cost_estimate=pl.CostEstimate(
            flops=44 * shape.pixels * shape.width * shape.out, bytes_accessed=2**24, transcendentals=0
        ),
        name="weight_gradients",
    )(info, *bands, *deltas, *far_deltas, *flat_far, pool_deltas, pooled)


def valid_pixels(extent, first_row, rows, columns):
    r = first_row + lax.broadcasted_iota(jnp.int32, (rows, columns), 0)
    w = lax.broadcasted_iota(jnp.int32, (rows, columns), 1)
    return ((r < extent[0]) & (w < extent[1])).astype(jnp.float32).reshape(rows * columns, 1)


def to_logical(place, x):
    return jnp.where(place.zh == place.c, x, place.swap(x, c=1, zh=1))


def on_device(
    features, extent, pointwise_weight, pooling_weight, dilated_weight, projection_weight, norm_gain, norm_bias, cotangent
):
    place = Place()
    nr, nzl = place.nr, place.nzl
    _, band_rows, columns, channels = features.shape
    width, out = channels // nr, norm_gain.shape[1]
    band = band_rows * columns
    pieces = nr == 4 and place.nd == 8 and dilated_weight.shape[0] == 2 * PER_CHIP * LANES
    shape = Shape(band_rows, columns, nr, width, out, pieces)
    images = place.nd

    partner = place.swap(extent, c=1)
    extent_here = jnp.where(place.zh == place.c, extent, partner)[0]
    area = (extent_here[0] * extent_here[1]).astype(jnp.float32)
    mask = valid_pixels(extent_here, place.part * band_rows, band_rows, columns)
    own_mask = valid_pixels(extent[0], place.z * band_rows, band_rows, columns)
    here_now = [place.m, place.c, place.zh, place.zl, place.part, place.z, extent_here[0], extent_here[1]]
    info = jnp.stack(here_now).astype(jnp.int32)
    areas = area.reshape(1)

    own_parts, other_parts = split_features(shape, features.reshape(band, channels), own_mask, place.c)
    held = by_xor([own_parts, place.swap(other_parts, c=1)], place.c)
    held = [by_xor([v[q] for q in range(nzl)], place.zl) for v in by_xor(held, place.zh)]

    def sent(image, k, some=slice(None), first=()):
        kh, kl = divmod(k, nzl)
        v = held[kh ^ image][kl][some]
        return place.swap(after(v, first), zh=kh, zl=kl) if k else v

    middle = band // 32 * 16
    cuts = [slice(0, middle), slice(middle, band)]
    steps = doubling(place)
    nd_bits = (place.nd // 2).bit_length() - 1
    projection = projection_weight.T
    if pieces:
        sources = line_pieces(place, dilated_weight, pointwise_weight, pooling_weight)
        crossed = place.swap(sources[0][:FIRST], zh=1)
        neighbour = after(place.swap(sources[1], zl=1), crossed, own_parts, other_parts, partner)
        near, rest = packed_near(shape, place.zl, sources[0], neighbour)
        rest = place.swap(rest, zh=1)
        near_x, near_y = plane_direct(place, near)
        near_d = plane_diagonal(place, near_x, near_y)
        far = packed_far(shape, place.zl, crossed, after(rest, near_d, held))
        crossing_band = sent(0, nzl, first=far)
        far_x, far_y = after(plane_direct(place, far), crossing_band)
        far_d = plane_diagonal(place, far_x, far_y)
        bands = [sent(0, k, first=far_x) for k in range(nzl)] + [crossing_band]
        bands += [sent(0, k, first=far_x) for k in range(nzl + 1, nr)]
        near = assembled_weights(shape, info, near, near_x, near_y, near_d)
        weights = [near, assembled_weights(shape, info, far, far_x, far_y, after(far_d, near))]
    else:
        bands = [sent(0, k) for k in range(nr)]
        weights = gathered_tiles(place, dilated_weight, pointwise_weight, pooling_weight)
        weights = by_xor([weights[:, : out // 2], weights[:, out // 2 :]], place.zh)

    def reduce(keep, got):
        half = keep + got.astype(jnp.float32)
        rows = half.reshape(nzl, band, half.shape[1])
        mine = lax.dynamic_index_in_dim(rows, place.zl, 0, keepdims=False)
        for k in range(1, nzl):
            other = lax.dynamic_index_in_dim(rows, place.zl ^ k, 0, keepdims=False).astype(jnp.bfloat16)
            mine = mine + place.swap(other, zl=k).astype(jnp.float32)
        return mine

    ready = (bands, weights)
    keep, given = far_sums(shape, info, bands, weights)
    far_bands = [[sent(1, k, first=ready)] for k in range(nzl)] + [[sent(1, nzl, cuts[0], ready)]]
    for step in steps[:-nd_bits]:
        projection = joined(place, after(projection, ready), step)
    got = place.swap(after(given, far_bands), c=1)
    wide = reduce(keep, got)
    upstream_low = to_logical(place, after(cotangent.reshape(band, out), got))
    keep, given, pooled, lifted = near_sums(shape, info, areas, after(bands, got, projection), weights)
    for step in steps[-nd_bits:-1]:
        projection = joined(place, after(projection, got), step)
    got = place.swap(after(given, projection, upstream_low), c=1)
    projection = joined(place, after(projection, got), steps[-1])
    far_bands += [[sent(1, k, cuts[0], got)] for k in range(nzl + 1, nr)]
    narrow = after(reduce(keep, got), projection, far_bands)
    projection = projection.reshape((place.nd, nr) + projection_weight.shape[::-1])
    projection = jnp.transpose(projection, (1, 2, 0, 3)).reshape(out, -1)
    z = [narrow[:, out:], narrow[:, :out], wide[:, out:], wide[:, :out]]

    local_count = jnp.sum(mask)
    stats = [local_moments(v, mask, local_count) for v in z]
    table = (lax.broadcasted_iota(jnp.int32, (images, 1), 0) == place.image).astype(jnp.float32) * lifted[0:1]
    average, spread, count, pool_pre = moments(
        place,
        jnp.concatenate([s for s, _ in stats], axis=0),
        jnp.concatenate([q for _, q in stats], axis=0),
        local_count,
        table,
    )
    inv_std = lax.rsqrt(spread + epsilon)
    normed = [(z[k] - average[k : k + 1]) * inv_std[k : k + 1] for k in range(4)]
    pre_act = [norm_gain[k : k + 1] * normed[k] + norm_bias[k : k + 1] for k in range(4)]

    pool_average = jnp.mean(pool_pre, axis=0, keepdims=True)
    pool_centred = pool_pre - pool_average
    pool_inv = lax.rsqrt(jnp.mean(pool_centred * pool_centred, axis=0, keepdims=True) + epsilon)
    pool_normed = pool_centred * pool_inv
    pool_lift = norm_gain[4:5] * pool_normed + norm_bias[4:5]
    here = lambda rows: lax.dynamic_slice_in_dim(rows, place.image, 1, axis=0)
    pool_act = here(jax.nn.silu(pool_lift))

    concat = jnp.concatenate([jax.nn.silu(u) * mask for u in pre_act] + [pool_act * mask], axis=1).astype(jnp.bfloat16)
    pooled_far = place.swap(pooled, zh=1)
    proj_pre = dot(concat, projection, NT)
    proj_sums, proj_squares = local_moments(proj_pre, mask, local_count)
    proj_average, proj_spread, _, _ = moments(place, proj_sums, proj_squares, local_count)
    proj_inv = lax.rsqrt(proj_spread + epsilon)
    proj_normed = (proj_pre - proj_average) * proj_inv
    proj_lift = norm_gain[5:6] * proj_normed + norm_bias[5:6]
    output_here = (jax.nn.silu(proj_lift) * mask).astype(jnp.bfloat16)

    upstream = upstream_low.astype(jnp.float32) * mask * silu_slope(proj_lift)
    sums = jnp.concatenate(
        [jnp.sum(upstream * proj_normed, axis=0, keepdims=True), jnp.sum(upstream, axis=0, keepdims=True)], axis=0
    )
    proj_totals = total(place, sums)
    proj_gain_grad, proj_bias_grad = proj_totals[0:1], proj_totals[1:2]
    gain = norm_gain[5:6]
    proj_delta = (
        mask
        * proj_inv
        * (gain * upstream - gain * proj_bias_grad / count - proj_normed * gain * proj_gain_grad / count)
    ).astype(jnp.bfloat16)
    concat_grad = dot(proj_delta, projection, NN)
    projection_partial = lambda first: dot(after(proj_delta, first), concat, TN)
    branch_up = [
        concat_grad[:, k * out : (k + 1) * out] * mask * silu_slope(pre_act[k]) for k in range(4)
    ]
    pool_part = jnp.sum(concat_grad[:, 4 * out :] * mask, axis=0, keepdims=True)
    table = (lax.broadcasted_iota(jnp.int32, (images, 1), 0) == place.image).astype(jnp.float32) * pool_part
    totals = total(
        place,
        after(jnp.concatenate(
            [jnp.sum(branch_up[k] * normed[k], axis=0, keepdims=True) for k in range(4)]
            + [jnp.sum(branch_up[k], axis=0, keepdims=True) for k in range(4)]
            + [table],
            axis=0,
        ), pooled_far),
    )
    branch_gain_grad, branch_bias_grad = totals[:4], totals[4:8]
    pool_up = totals[8:] * silu_slope(pool_lift)
    pool_gain_grad = jnp.sum(pool_up * pool_normed, axis=0, keepdims=True)
    pool_bias_grad = jnp.sum(pool_up, axis=0, keepdims=True)
    pool_deltas = pool_inv * (
        norm_gain[4:5] * pool_up
        - norm_gain[4:5] * pool_bias_grad / images
        - pool_normed * norm_gain[4:5] * pool_gain_grad / images
    )
    low_rows = lambda rows: jnp.pad(rows, ((0, 16 - rows.shape[0]), (0, 0))).astype(jnp.bfloat16)
    pool_pair = lax.dynamic_slice_in_dim(pool_deltas, 2 * place.m, 2, axis=0)
    halves = lambda v, n: by_xor([v[:, n * out : n * out + out // 2], v[:, n * out + out // 2 : (n + 1) * out]], place.zh)
    deltas = []
    for k in range(4):
        gain = norm_gain[k : k + 1]
        deltas.append(
            mask
            * inv_std[k : k + 1]
            * (
                gain * branch_up[k]
                - gain * branch_bias_grad[k : k + 1] / count
                - normed[k] * gain * branch_gain_grad[k : k + 1] / count
            )
        )
    delta = jnp.concatenate(deltas, axis=1).astype(jnp.bfloat16)
    crossing = jnp.concatenate([halves(delta, k)[1] for k in range(4)], axis=1)

    def over_group(v, first):
        near = [v] + [after(place.swap(v, zl=k), first) for k in range(1, nzl)]
        return near + [place.swap(n, c=1) for n in near]

    crossing = place.swap(crossing, zh=1)
    rows = projection_weight.shape[0]
    part = projection_partial(delta).astype(jnp.bfloat16).reshape(out, images // 2, 2, rows)
    part = jnp.transpose(part, (2, 1, 0, 3)).reshape(2, images // 2, 2, nzl, out // nr, rows)
    part = halved(place, [part[k] for k in range(2)], steps[-nd_bits - 1])
    spread_deltas = over_group(delta, (crossing, part))
    part = m_halved(place, after(part, spread_deltas), steps, 1)
    far_deltas = [crossing] + [place.swap(crossing, zl=k) for k in range(1, nzl)]
    inputs = input_gradient(shape, info, areas, spread_deltas, low_rows(here(pool_deltas)), weights)

    for k in range(nzl, nr):
        far_bands[k].append(sent(1, k, cuts[1], spread_deltas))
    crossing = after(far_deltas, inputs, far_bands)
    pooled_pair = pooled + jnp.roll(pooled_far, 1, axis=0)
    pool_pair = jnp.concatenate([pool_pair[i : i + 1] for i in range(2)], axis=0)
    pool_pair = jnp.concatenate(by_xor([pool_pair[0:1], pool_pair[1:2]], place.zh), axis=0)
    pool_pair = halves(low_rows(pool_pair), 0)[0]
    far_deltas = crossing + [place.swap(n, c=1) for n in crossing]
    grads = weight_gradients(shape, info, bands, far_bands, spread_deltas, far_deltas, pool_pair, pooled_pair)

    crossed = place.swap(jnp.stack(after(inputs[nzl:], far_deltas, far_bands, part)), zh=1)
    part = m_halved(place, after(part, inputs), steps, 2)
    images_here = by_xor([list(inputs[:nzl]), [crossed[k] for k in range(nzl)]], place.zh)
    if pieces:
        pairs = [[grads[2 * rel], grads[2 * rel + 1]] for rel in range(4)]
        first_d, second_d = plane_scatter_diagonal(place, pairs)
        first_d, second_d = after((first_d, second_d), crossed, part)
        quarters = plane_scatter(place, pairs, first_d, second_d)
    else:
        quarters = grads
    images_here, part, output = after((images_here, part, output_here), crossed)
    part = part.reshape((2, nzl) + part.shape[-2:])
    part = halved(place, [part[k] for k in range(2)], steps[-nd_bits - 2])
    output = to_logical(place, output)
    returned = [[image[0] for image in images_here]]
    for k in range(1, nzl):
        got = place.swap(jnp.stack([image[k] for image in images_here]), zl=k)
        returned.append([got[i] for i in range(2)])
    quarters = after(quarters, part, output, returned)
    returned = by_xor([list(image) for image in zip(*returned)], place.c)
    traded = place.swap(jnp.stack(returned[1]), c=1)
    feature_gradient = join_features(shape, returned[0], [traded[k] for k in range(nzl)], place.c, place.zl)
    if pieces:
        dilated_gradient, pointwise_gradient, pooling_gradient = line_back(place, quarters, feature_gradient)
    else:
        dilated_gradient, pointwise_gradient, pooling_gradient = scattered_tiles(place, quarters[0])
    for step in [step for step in steps if "zl" in step[0]]:
        part = part.reshape((-1, 2) + part.shape[-2:])
        part = halved(place, [part[:, k] for k in range(2)], step)
    projection_gradient = part.reshape(out // nr, rows).astype(jnp.float32).T

    return (
        output.reshape(cotangent.shape),
        feature_gradient.reshape(features.shape),
        pointwise_gradient,
        pooling_gradient,
        dilated_gradient,
        projection_gradient,
        jnp.concatenate([branch_gain_grad, pool_gain_grad, proj_gain_grad], axis=0),
        jnp.concatenate([branch_bias_grad, pool_bias_grad, proj_bias_grad], axis=0),
    )


def solution(mesh):
    banded = P("dp", "rows", None, None)
    blocks = P("dp", "rows")
    return jax.shard_map(
        on_device,
        mesh=mesh,
        in_specs=(banded, P("dp", None), blocks, blocks, blocks, blocks, P(), P(), banded),
        out_specs=(banded, banded, blocks, blocks, blocks, blocks, P(), P()),
        check_vma=False,
    )
```

```python
import jax
import jax.numpy as jnp
from jax import lax
from jax.experimental import pallas as pl
from jax.experimental.pallas import tpu as pltpu
from jax.sharding import PartitionSpec as P

epsilon = 1e-05
dilations = (6, 12, 18)
LANES = 128
BLOCK_ROWS = 6
AXES = ("dp", "rows")
FULL, SHORT, PER_CHIP = 14, 13, 27
SLOTS = FULL + 2 + SHORT
FIRST = 14
CUT = 15
NT = (((1,), (1,)), ((), ()))
TN = (((0,), (0,)), ((), ()))
NN = (((1,), (0,)), ((), ()))


def dot(first, second, dims):
    return lax.dot_general(first, second, dims, preferred_element_type=jnp.float32)


def after(x, *first):
    return lax.optimization_barrier((x, first))[0]


def silu_slope(values):
    sigma = jax.nn.sigmoid(values)
    return sigma * (1.0 + values * (1.0 - sigma))


class Place:
    def __init__(self):
        self.nd, self.nr = lax.axis_size("dp"), lax.axis_size("rows")
        self.nzl = self.nr // 2
        d, z = lax.axis_index("dp"), lax.axis_index("rows")
        self.d, self.z = d, z
        self.m, self.c = d // 2, d % 2
        self.zh, self.zl = z // self.nzl, z % self.nzl
        self.part = self.c * self.nzl + self.zl
        self.image = 2 * self.m + self.zh

    def swap(self, x, m=0, c=0, zh=0, zl=0):
        nzl = self.nzl
        pairs = []
        for flat in range(self.nd * self.nr):
            d, z = divmod(flat, self.nr)
            pairs.append((flat, (d ^ (2 * m + c)) * self.nr + (z ^ (zh * nzl + zl))))
        return lax.ppermute(x, AXES, pairs)


def by_xor(items, index):
    items = list(items)
    bit = 1
    while bit < len(items):
        flip = (index & bit) != 0
        pick = lambda a, b: jnp.where(flip, a, b)
        items = [jax.tree.map(pick, items[k ^ bit], items[k]) for k in range(len(items))]
        bit *= 2
    return items


def tree(items):
    items = list(items)
    while len(items) > 1:
        items = [items[i] + items[i + 1] for i in range(0, len(items), 2)]
    return items[0]


def exchange_stages(place):
    return (
        [dict(c=1)],
        [dict(m=k) for k in range(1, place.nd // 2)],
        [dict(zh=k // place.nzl, zl=k % place.nzl) for k in range(1, place.nr)],
    )


def total(place, x):
    for stage in exchange_stages(place):
        x = tree([x] + [place.swap(x, **s) for s in stage])
    return x


def moments(place, sums, squares, count, extra=None):
    width = sums.shape[1]
    k = sums.shape[0]
    rows = [sums, squares, jnp.full((1, width), count, jnp.float32)]
    if extra is not None:
        rows.append(extra)
    x = jnp.concatenate(rows, axis=0)
    for stage in exchange_stages(place):
        xs = [x] + [place.swap(x, **s) for s in stage]
        whole = tree(xs)
        n = whole[2 * k : 2 * k + 1]
        mean = whole[:k] / jnp.maximum(n, 1.0)
        between = []
        for y in xs:
            own = y[2 * k : 2 * k + 1]
            gap = y[:k] / jnp.maximum(own, 1.0) - mean
            between.append(own * gap * gap)
        x = jnp.concatenate([whole[:k], whole[k : 2 * k] + tree(between), whole[2 * k :]], axis=0)
    n = x[2 * k : 2 * k + 1]
    return x[:k] / n, x[k : 2 * k] / n, n, x[2 * k + 1 :]


def local_moments(values, mask, count):
    sums = jnp.sum(values * mask, axis=0, keepdims=True)
    centred = (values - sums / jnp.maximum(count, 1.0)) * mask
    return sums, jnp.sum(centred * centred, axis=0, keepdims=True)


def line_pieces(place, dilated, pointwise, pooling):
    tiles = lambda w: jnp.transpose(w.T.reshape(w.shape[1], w.shape[0] // LANES, LANES), (1, 0, 2))
    dil, one, pool = tiles(dilated), tiles(pointwise), tiles(pooling)
    other = [dil[2 + r :: 4][:SHORT] for r in range(2)]
    got = place.swap(jnp.concatenate(other, axis=0), c=1)
    same = [jnp.concatenate([dil[r::4][:FULL], one[r : r + 1], pool[r : r + 1]], axis=0) for r in range(2)]
    whole = [jnp.concatenate([same[r], got[r * SHORT : (r + 1) * SHORT]], axis=0) for r in range(2)]
    return by_xor(whole, place.zl)


def plane_direct(place, half):
    return place.swap(half, m=1), place.swap(half, m=2)


def plane_diagonal(place, by_x, by_y):
    return place.swap(by_x[:CUT], m=2), place.swap(by_y[CUT:], m=1)


def add_low(first, *others):
    out = first.astype(jnp.float32)
    for o in others:
        out = out + o.astype(jnp.float32)
    return out.astype(jnp.bfloat16)


def plane_scatter_diagonal(place, pieces):
    return place.swap(pieces[3][0], m=2), place.swap(pieces[3][1], m=1)


def plane_scatter(place, pieces, first_d, second_d):
    to_x = jnp.stack([add_low(pieces[1][0], first_d), pieces[1][1]])
    to_y = jnp.stack([pieces[2][0], add_low(pieces[2][1], second_d)])
    by_x, by_y = place.swap(to_x, m=1), place.swap(to_y, m=2)
    return [add_low(pieces[0][q], by_x[q], by_y[q]) for q in range(2)]


def line_back(place, quarters, first):
    by_kl = by_xor(quarters, place.zl)
    by_part = by_xor([by_kl[0], after(place.swap(by_kl[1], zl=1), first)], place.zl)
    same = [p[: FULL + 2] for p in by_part]
    got = place.swap(jnp.concatenate([p[FULL + 2 :] for p in by_part], axis=0), c=1)
    other = [got[r * SHORT : (r + 1) * SHORT] for r in range(2)]
    gap = jnp.zeros((FULL - SHORT,) + other[0].shape[1:], other[0].dtype)
    dil = jnp.stack([s[:FULL] for s in same] + [jnp.concatenate([o, gap], axis=0) for o in other], axis=1)
    dil = dil.reshape((4 * FULL,) + dil.shape[2:])[: 2 * PER_CHIP]
    rows = lambda t: jnp.transpose(t, (1, 0, 2)).reshape(t.shape[1], t.shape[0] * LANES).astype(jnp.float32).T
    one = jnp.stack([s[FULL] for s in same])
    pool = jnp.stack([s[FULL + 1] for s in same])
    return rows(dil), rows(one), rows(pool)


def gathered_tiles(place, dilated, pointwise, pooling):
    whole = []
    for w in (dilated, pointwise, pooling):
        w = lax.all_gather(w, "rows", axis=1, tiled=True)
        w = lax.all_gather(w, "dp", axis=0, tiled=True)
        channels = pointwise.shape[0] * place.nd
        taps = w.shape[0] // channels
        w = w.reshape(taps, channels // (LANES * place.nr), place.nr, LANES, w.shape[1])
        w = lax.dynamic_index_in_dim(w, place.part, 2, keepdims=False)
        whole.append(jnp.transpose(w.reshape(taps, channels // place.nr, w.shape[-1]), (0, 2, 1)))
    return jnp.concatenate(whole, axis=0)


def scattered_tiles(place, gradients):
    outs = []
    taps, half, width = gradients.shape
    for g in (gradients[: taps - 2], gradients[taps - 2 : taps - 1], gradients[taps - 1 :]):
        g = jnp.transpose(g, (0, 2, 1)).reshape(g.shape[0], width // LANES, 1, LANES, half)
        spread = jnp.zeros((g.shape[0], width // LANES, place.nr, LANES, 2 * half), g.dtype)
        g = lax.dynamic_update_slice(spread, g, (0, 0, place.part, 0, place.zh * half)).reshape(-1, 2 * half)
        g = lax.psum_scatter(g, "dp", scatter_dimension=0, tiled=True)
        outs.append(lax.psum_scatter(g, "rows", scatter_dimension=1, tiled=True).astype(jnp.float32))
    return outs


def doubling(place):
    steps = []
    for name, index, size in (("zl", place.zl, place.nzl), ("zh", place.zh, 2), ("c", place.c, 2), ("m", place.m, place.nd // 2)):
        bit = 1
        while bit < size:
            steps.append(({name: bit}, (index & bit) != 0))
            bit *= 2
    return steps


def joined(place, x, step):
    swap, upper = step
    return jnp.stack(by_xor([x, place.swap(x, **swap)], upper.astype(jnp.int32)))


def halved(place, x, step):
    swap, upper = step
    mine = by_xor([x[0], x[1]], upper.astype(jnp.int32))
    return add_low(mine[0], place.swap(mine[1], **swap))


def m_halved(place, x, steps, first):
    for step in [step for step in steps if "m" in step[0]]:
        if (step[0]["m"] == 1) == (first == 1):
            x = x.reshape((-1, 2) + x.shape[1:])
            x = halved(place, [x[:, k] for k in range(2)], step)
    return x


class Shape:
    def __init__(self, band_rows, columns, nr, width, out, pieces):
        self.band_rows, self.columns, self.nr, self.width, self.out = band_rows, columns, nr, width, out
        self.rows = band_rows * nr
        self.band, self.pixels = band_rows * columns, band_rows * columns * nr
        self.block = BLOCK_ROWS * columns
        self.blocks = self.rows // BLOCK_ROWS
        self.pieces = pieces
        self.quarter = out // 4

    def regions(self, dilation):
        cuts = sorted({0, min(dilation, self.rows), max(self.rows - dilation, 0), self.rows})
        for lo, hi in zip(cuts, cuts[1:]):
            yield lo, hi, [r for r in range(3) if 0 <= lo + (r - 1) * dilation and hi + (r - 1) * dilation <= self.rows]


ANY = pl.BlockSpec(memory_space=pl.ANY)
SMEM = pl.BlockSpec(memory_space=pltpu.SMEM)
VMEM = pl.BlockSpec(memory_space=pltpu.VMEM)
PARAMS = pltpu.CompilerParams(vmem_limit_bytes=58 * 2**20)


LIGHT = pl.CostEstimate(flops=0, bytes_accessed=0, transcendentals=0)


def lanes_at(start, size=LANES):
    return pl.ds(pl.multiple_of(start, LANES), size)


def start_bands(shape, refs, scratch, sem, part):
    for k, ref in enumerate(refs):
        pltpu.make_async_copy(ref, scratch.at[pl.ds((part ^ k) * shape.band, shape.band), :], sem.at[k]).start()


def wait_bands(shape, refs, scratch, sem):
    for k, ref in enumerate(refs):
        pltpu.make_async_copy(ref, scratch.at[pl.ds(k * shape.band, shape.band), :], sem.at[k]).wait()


def split_features(shape, features, mask, c):
    tiles, n = shape.width // LANES, shape.nr // 2

    def kernel(info, x, mask_ref, *outs):
        valid = mask_ref[...].astype(jnp.bfloat16)
        for k, out in enumerate(outs):
            for q in range(n):
                for i in range(tiles):
                    at = (i * shape.nr + (info[0] ^ k) * n + q) * LANES
                    out[q, :, i * LANES : (i + 1) * LANES] = x[:, lanes_at(at)] * valid

    return pl.pallas_call(
        kernel,
        out_shape=[jax.ShapeDtypeStruct((n, shape.band, shape.width), jnp.bfloat16)] * 2,
        in_specs=[SMEM, VMEM, VMEM],
        out_specs=[VMEM] * 2,
        compiler_params=PARAMS,
        cost_estimate=LIGHT,
        name="split_features",
    )(c.reshape(1), features, mask)


def join_features(shape, own, other, c, zl):
    tiles, n = shape.width // LANES, shape.nr // 2

    def kernel(info, *refs):
        for k, part in enumerate(refs[: 2 * n]):
            core, q = info[0] ^ (k // n), info[1] ^ (k % n)
            for i in range(tiles):
                at = (i * shape.nr + core * n + q) * LANES
                refs[2 * n][:, lanes_at(at)] = part[:, i * LANES : (i + 1) * LANES]

    return pl.pallas_call(
        kernel,
        out_shape=jax.ShapeDtypeStruct((shape.band, shape.width * shape.nr), jnp.bfloat16),
        in_specs=[SMEM] + [VMEM] * shape.nr,
        out_specs=VMEM,
        compiler_params=PARAMS,
        cost_estimate=LIGHT,
        name="join_features",
    )(jnp.stack([c, zl]).astype(jnp.int32), *own, *other)


def packed_near(shape, zl, own, neighbour):
    size = shape.quarter

    def kernel(info, own, neighbour, out, rest):
        for kl, ref in enumerate((own, neighbour)):
            out[:, pl.ds(pl.multiple_of((info[0] ^ kl) * size, size), size), :] = ref[...]
        rest[: SLOTS - FIRST] = own[FIRST:]
        rest[SLOTS - FIRST :] = neighbour[...]

    return pl.pallas_call(
        kernel,
        out_shape=[
            jax.ShapeDtypeStruct((SLOTS, 2 * size, LANES), jnp.bfloat16),
            jax.ShapeDtypeStruct((2 * SLOTS - FIRST, size, LANES), jnp.bfloat16),
        ],
        in_specs=[SMEM, VMEM, VMEM],
        out_specs=[VMEM, VMEM],
        compiler_params=PARAMS,
        cost_estimate=LIGHT,
        name="packed_near",
    )(zl.reshape(1), own, neighbour)


def packed_far(shape, zl, first, rest):
    size = shape.quarter

    def kernel(info, first, rest, out):
        for kl in range(2):
            columns = pl.ds(pl.multiple_of((info[0] ^ kl) * size, size), size)
            if kl == 0:
                out[:FIRST, columns, :] = first[...]
                out[FIRST:, columns, :] = rest[: SLOTS - FIRST]
            else:
                out[:, columns, :] = rest[SLOTS - FIRST :]

    return pl.pallas_call(
        kernel,
        out_shape=jax.ShapeDtypeStruct((SLOTS, 2 * size, LANES), jnp.bfloat16),
        in_specs=[SMEM, VMEM, VMEM],
        out_specs=VMEM,
        compiler_params=PARAMS,
        cost_estimate=LIGHT,
        name="packed_far",
    )(zl.reshape(1), first, rest)


def chip_slot(t, c):
    return jnp.where(jnp.where(c == 0, t < FULL, t >= SHORT), t - SHORT * c, FULL + 2 + t - FULL * (1 - c))


def assembled_weights(shape, info, own, by_x, by_y, diagonal):
    def kernel(info, *refs):
        ins, out, sem = refs[:5], refs[5], refs[6]
        m, c = info[0], info[1]

        def copy(ref, slot, tap, lane):
            pltpu.make_async_copy(ref.at[slot], out.at[tap, :, lanes_at(lane)], sem).start()

        def place(rel, slot, tap, lane):
            if rel < 3:
                copy(ins[rel], slot, tap, lane)
            else:

                @pl.when(slot < CUT)
                def _():
                    copy(ins[3], slot, tap, lane)

                @pl.when(slot >= CUT)
                def _():
                    copy(ins[4], slot - CUT, tap, lane)

        for rel in range(4):
            chip = m ^ rel

            def body(t, carry):
                v = chip * PER_CHIP + t
                place(rel, chip_slot(t, c), v // 4, (v % 4) * LANES)
                return carry

            lax.fori_loop(0, PER_CHIP, body, 0)
            for extra in range(2):
                place(rel, FULL + extra, 27 + extra, chip * LANES)
        pltpu.make_async_copy(out, out, sem).wait()

    return pl.pallas_call(
        kernel,
        out_shape=jax.ShapeDtypeStruct((29, shape.out // 2, shape.width), jnp.bfloat16),
        in_specs=[SMEM] + [ANY] * 5,
        out_specs=VMEM,
        scratch_shapes=[pltpu.SemaphoreType.DMA],
        compiler_params=PARAMS,
        cost_estimate=LIGHT,
        name="assembled_weights",
    )(info, own, by_x, by_y, *diagonal)


def shifted(values, by, columns):
    if by == 0:
        return values
    pixels = values.shape[0]
    source = lax.broadcasted_iota(jnp.int32, (pixels, 1), 0) % columns - by
    return jnp.where((source >= 0) & (source < columns), pltpu.roll(values, by % pixels, 0), 0.0)


def send_halves(shape, c, kept, low, outs, sem):
    half = shape.pixels // 2
    copies = []
    for n, (source, core) in enumerate(((kept, c), (low, 1 - c))):
        rows = source.at[pl.ds(pl.multiple_of(core * half, half), half)]
        copies.append(pltpu.make_async_copy(rows, outs[n], sem.at[n]))
    for copy in copies:
        copy.start()
    for copy in copies:
        copy.wait()


def half_shapes(shape, n):
    half = shape.pixels // 2
    return [
        jax.ShapeDtypeStruct((half, n * shape.out), jnp.float32),
        jax.ShapeDtypeStruct((half, n * shape.out), jnp.bfloat16),
    ]


def start_taps(weights, scratch, sem, taps, zh):
    half = weights[0].shape[1]
    for n, tap in enumerate(taps):
        for kh, ref in enumerate(weights):
            columns = pl.ds(pl.multiple_of((zh ^ kh) * half, half), half)
            pltpu.make_async_copy(ref.at[tap], scratch.at[n, columns], sem.at[n]).start()


def wait_taps(scratch, sem, some):
    for n in some:
        pltpu.make_async_copy(scratch.at[n], scratch.at[n], sem.at[n]).wait()


def dilated_products(shape, branch, x, w, first, y):
    dilation, columns = dilations[branch], shape.columns
    for s in range(3):
        for lo, hi, rs in shape.regions(dilation):
            pixels = jnp.concatenate(
                [x[(lo + (r - 1) * dilation) * columns : (hi + (r - 1) * dilation) * columns, :] for r in rs], axis=1
            )
            taps = jnp.concatenate([w[first + 3 * s + r] for r in rs], axis=1)
            y[s, lo * columns : hi * columns, :] = dot(pixels, taps, NT)


def put_dilated(shape, branch, y, kept, low, lane):
    dilation, columns = dilations[branch], shape.columns
    for blk in range(shape.blocks):
        at = slice(blk * shape.block, (blk + 1) * shape.block)
        z = y[1, at, :] + shifted(y[0, at, :], dilation, columns) + shifted(y[2, at, :], -dilation, columns)
        kept[at, lane : lane + shape.out] = z
        low[at, lane : lane + shape.out] = z.astype(jnp.bfloat16)


def taps_of(branch):
    return [9 * branch + 3 * r + s for s in range(3) for r in range(3)]


def branch_sums(shape, info, area, bands, weights):
    nr = shape.nr

    def kernel(info, area, *refs):
        ins, weights = refs[:nr], refs[nr : nr + 2]
        keep, sent, pooled, lifted, x, w, y, kept, low_sums, band_sem, w_sem, out_sem = refs[nr + 2 :]
        start_bands(shape, ins, x, band_sem, info[5])
        start_taps(weights, w, w_sem, taps_of(2) + taps_of(1) + taps_of(0) + [27, 28], info[2])
        wait_bands(shape, ins, x, band_sem)
        wait_taps(w, w_sem, range(29))
        for n, branch in enumerate((2, 1, 0)):
            dilated_products(shape, branch, x, w, 9 * n, y.at[n % 2])
            put_dilated(shape, branch, y.at[n % 2], kept, low_sums, n * shape.out)
        z = dot(x[...], w[27], NT)
        kept[:, 3 * shape.out :] = z
        low_sums[:, 3 * shape.out :] = z.astype(jnp.bfloat16)
        sums = jnp.zeros((1, shape.width), jnp.float32)
        for blk in range(shape.blocks):
            values = x[blk * shape.block : (blk + 1) * shape.block, :]
            sums = sums + jnp.sum(values.astype(jnp.float32), axis=0, keepdims=True)
        low = jnp.broadcast_to(sums / area[0], pooled.shape).astype(jnp.bfloat16)
        first = lax.broadcasted_iota(jnp.int32, pooled.shape, 0) == 0
        pooled[...] = jnp.where(first, low.astype(jnp.float32), 0.0).astype(jnp.bfloat16)
        lifted[...] = dot(pooled[...], w[28], NT)
        send_halves(shape, info[1], kept, low_sums, (keep, sent), out_sem)

    return pl.pallas_call(
        kernel,
        out_shape=half_shapes(shape, 4)
        + [jax.ShapeDtypeStruct((16, shape.width), jnp.bfloat16), jax.ShapeDtypeStruct((16, shape.out), jnp.float32)],
        in_specs=[SMEM, SMEM] + [ANY] * (nr + 2),
        out_specs=[ANY] * 2 + [VMEM] * 2,
        scratch_shapes=[
            pltpu.VMEM((shape.pixels, shape.width), jnp.bfloat16),
            pltpu.VMEM((29, shape.out, shape.width), jnp.bfloat16),
            pltpu.VMEM((2, 3, shape.pixels, shape.out), jnp.float32),
            pltpu.VMEM((shape.pixels, 4 * shape.out), jnp.float32),
            pltpu.VMEM((shape.pixels, 4 * shape.out), jnp.bfloat16),
            pltpu.SemaphoreType.DMA((nr,)),
            pltpu.SemaphoreType.DMA((29,)),
            pltpu.SemaphoreType.DMA((2,)),
        ],
        compiler_params=PARAMS,
        cost_estimate=LIGHT,
        name="branch_sums",
    )(info, area, *bands, *weights)


def moved_columns(shape, delta, lane, lanes, branch, moved):
    for blk in range(shape.blocks):
        at = slice(blk * shape.block, (blk + 1) * shape.block)
        values = delta[at, lanes_at(lane, lanes)].astype(jnp.float32)
        for s in range(3):
            moved[at, s * lanes : (s + 1) * lanes] = shifted(
                values, (s - 1) * dilations[branch], shape.columns
            ).astype(jnp.bfloat16)


def input_gradient(shape, info, area, deltas, pool_delta, weights):
    nr, columns = shape.nr, shape.columns

    def kernel(info, area, *refs):
        ins, pool_delta, weights = refs[:nr], refs[nr], refs[nr + 1 : nr + 3]
        outs = refs[nr + 3 : 2 * nr + 3]
        delta, moved, w, acc, delta_sem, w_sem = refs[2 * nr + 3 :]
        start_bands(shape, ins, delta, delta_sem, info[4])
        start_taps(weights, w, w_sem, range(29), info[2])
        wait_bands(shape, ins, delta, delta_sem)
        wait_taps(w, w_sem, range(29))
        pool = dot(pool_delta[...], w[28], NN)[0:1] / area[0]
        acc[...] = dot(delta[:, : shape.out], w[27], NN) + pool
        for branch in range(3):
            dilation = dilations[branch]
            moved_columns(shape, delta, (branch + 1) * shape.out, shape.out, branch, moved)
            for lo, hi, rs in shape.regions(dilation):
                rows = [2 - r for r in rs]
                cut = lambda r: moved[(lo - (r - 1) * dilation) * columns : (hi - (r - 1) * dilation) * columns, :]
                pixels = jnp.concatenate([cut(r) for r in rows], axis=1)
                taps = jnp.concatenate([w[9 * branch + 3 * r + s] for r in rows for s in range(3)], axis=0)
                acc[lo * columns : hi * columns, :] += dot(pixels, taps, NN)
        pixel = lax.broadcasted_iota(jnp.int32, (shape.band, 1), 0)
        for k in range(nr):
            first = (info[5] ^ k) * shape.band
            inside = ((pixel + first) // columns < info[6]) & (pixel % columns < info[7])
            values = acc[pl.ds(pl.multiple_of(first, shape.band), shape.band), :]
            outs[k][...] = jnp.where(inside, values, 0.0).astype(jnp.bfloat16)

    return pl.pallas_call(
        kernel,
        out_shape=[jax.ShapeDtypeStruct((shape.band, shape.width), jnp.bfloat16)] * nr,
        in_specs=[SMEM, SMEM] + [ANY] * nr + [VMEM] + [ANY] * 2,
        out_specs=[VMEM] * nr,
        scratch_shapes=[
            pltpu.VMEM((shape.pixels, 4 * shape.out), jnp.bfloat16),
            pltpu.VMEM((shape.pixels, 3 * shape.out), jnp.bfloat16),
            pltpu.VMEM((29, shape.out, shape.width), jnp.bfloat16),
            pltpu.VMEM((shape.pixels, shape.width), jnp.float32),
            pltpu.SemaphoreType.DMA((nr,)),
            pltpu.SemaphoreType.DMA((29,)),
        ],
        compiler_params=PARAMS,
        cost_estimate=pl.CostEstimate(
            flops=44 * shape.pixels * shape.width * shape.out, bytes_accessed=2**24, transcendentals=0
        ),
        name="input_gradient",
    )(info, area, *deltas, pool_delta, *weights)


def weight_gradients(shape, info, bands, far_bands, deltas, far_deltas, pool_deltas, pooled):
    nr, columns, half = shape.nr, shape.columns, shape.out // 2
    n_outs = 8 if shape.pieces else 1
    by_rows = lambda v: v.reshape(v.shape[0] // columns, columns, v.shape[1])
    bands = [by_rows(band) for band in [*bands, *far_bands]]

    def kernel(info, *refs):
        ins, delta_ins, far_delta_ins = (refs[n * nr : (n + 1) * nr] for n in range(3))
        far_ins, refs = refs[3 * nr : 4 * nr], refs[4 * nr :]
        pool_deltas, pooled, outs = refs[0], refs[1], refs[2 : 2 + n_outs]
        x, delta, far_delta, moved, grads, sem, out_sem = refs[2 + n_outs :]
        m, c, zh, part, z = info[0], info[1], info[2], info[4], info[5]
        rows = shape.band_rows
        start_bands(shape, delta_ins, delta, sem.at[0], part)
        start_bands(shape, far_delta_ins, far_delta, sem.at[1], part)
        for image, sources in enumerate((ins, far_ins)):
            for k, ref in enumerate(sources):
                pltpu.make_async_copy(ref, x.at[pl.ds((z ^ k) * rows, rows), image], sem.at[2 + image, k]).start()

        def arrive(n):
            for k in range(nr):
                if n < 2:
                    some = (delta, far_delta)[n].at[pl.ds(k * shape.band, shape.band)]
                else:
                    some = x.at[pl.ds(k * rows, rows), n - 2]
                pltpu.make_async_copy(some, some, sem.at[n, k]).wait()

        def move(branch):
            for image, source in enumerate((delta, far_delta)):
                lane = (branch + 1) * half if image else (branch + 1) * shape.out + zh * half
                for blk in range(shape.blocks):
                    at = slice(blk * shape.block, (blk + 1) * shape.block)
                    values = source[at, lanes_at(lane, half)].astype(jnp.float32)
                    for s in range(3):
                        value = shifted(values, (s - 1) * dilations[branch], columns).astype(jnp.bfloat16)
                        moved[blk * BLOCK_ROWS : (blk + 1) * BLOCK_ROWS, image, :, s * half : (s + 1) * half] = (
                            value.reshape(BLOCK_ROWS, columns, half)
                        )

        flat = lambda v: v.reshape(-1, v.shape[-1])

        def put(tap, value):
            value = value.astype(jnp.bfloat16)
            if not shape.pieces:
                grads[tap] = value
                return
            for i in range(4):
                if tap < 27:
                    v = 4 * tap + i
                    chip, slot = v // PER_CHIP, chip_slot(v % PER_CHIP, c)
                else:
                    chip, slot = i, FULL + tap - 27
                for q in range(2):
                    rows = slice(q * shape.quarter, (q + 1) * shape.quarter)
                    grads[2 * (m ^ chip) + q, slot] = value[rows, i * LANES : (i + 1) * LANES]

        arrive(0)
        arrive(1)
        for branch in range(3):
            move(branch)
            if branch == 0:
                arrive(2)
                arrive(3)
            dilation = dilations[branch]
            for r in range(3):
                up, down = max(0, 1 - r) * dilation, max(0, r - 1) * dilation
                to = flat(moved[up : shape.rows - down])
                value = dot(to, flat(x[down : shape.rows - up]), TN)
                for s in range(3):
                    put(9 * branch + 3 * r + s, value[s * half : (s + 1) * half])
        one = jnp.concatenate(
            [
                delta[:, lanes_at(zh * half, half)].reshape(shape.rows, 1, columns, half),
                far_delta[:, :half].reshape(shape.rows, 1, columns, half),
            ],
            axis=1,
        )
        put(27, dot(flat(one), flat(x[...]), TN))
        put(28, dot(pool_deltas[...], pooled[...], TN))
        copies = [pltpu.make_async_copy(grads.at[n] if shape.pieces else grads, outs[n], out_sem.at[n]) for n in range(n_outs)]
        for copy in copies:
            copy.start()
        for copy in copies:
            copy.wait()

    if shape.pieces:
        out_shape = [jax.ShapeDtypeStruct((SLOTS, shape.quarter, LANES), jnp.bfloat16)] * 8
        grads_shape = (8, SLOTS, shape.quarter, LANES)
    else:
        out_shape = [jax.ShapeDtypeStruct((29, half, shape.width), jnp.bfloat16)]
        grads_shape = (29, half, shape.width)
    return pl.pallas_call(
        kernel,
        out_shape=out_shape,
        in_specs=[SMEM] + [ANY] * (4 * nr) + [VMEM] * 2,
        out_specs=[ANY] * n_outs,
        scratch_shapes=[
            pltpu.VMEM((shape.rows, 2, columns, shape.width), jnp.bfloat16),
            pltpu.VMEM((shape.pixels, 4 * shape.out), jnp.bfloat16),
            pltpu.VMEM((shape.pixels, 2 * shape.out), jnp.bfloat16),
            pltpu.VMEM((shape.rows, 2, columns, 3 * half), jnp.bfloat16),
            pltpu.VMEM(grads_shape, jnp.bfloat16),
            pltpu.SemaphoreType.DMA((4, nr)),
            pltpu.SemaphoreType.DMA((n_outs,)),
        ],
        compiler_params=PARAMS,
        cost_estimate=pl.CostEstimate(
            flops=44 * shape.pixels * shape.width * shape.out, bytes_accessed=2**24, transcendentals=0
        ),
        name="weight_gradients",
    )(info, *bands[:nr], *deltas, *far_deltas, *bands[nr:], pool_deltas, pooled)


def valid_pixels(extent, first_row, rows, columns):
    r = first_row + lax.broadcasted_iota(jnp.int32, (rows, columns), 0)
    w = lax.broadcasted_iota(jnp.int32, (rows, columns), 1)
    return ((r < extent[0]) & (w < extent[1])).astype(jnp.float32).reshape(rows * columns, 1)


def to_logical(place, x):
    return jnp.where(place.zh == place.c, x, place.swap(x, c=1, zh=1))


def on_device(
    features, extent, pointwise_weight, pooling_weight, dilated_weight, projection_weight, norm_gain, norm_bias, cotangent
):
    place = Place()
    nr, nzl = place.nr, place.nzl
    _, band_rows, columns, channels = features.shape
    width, out = channels // nr, norm_gain.shape[1]
    band = band_rows * columns
    pieces = nr == 4 and place.nd == 8 and dilated_weight.shape[0] == 2 * PER_CHIP * LANES
    shape = Shape(band_rows, columns, nr, width, out, pieces)
    images = place.nd

    partner = place.swap(extent, c=1)
    extent_here = jnp.where(place.zh == place.c, extent, partner)[0]
    area = (extent_here[0] * extent_here[1]).astype(jnp.float32)
    mask = valid_pixels(extent_here, place.part * band_rows, band_rows, columns)
    own_mask = valid_pixels(extent[0], place.z * band_rows, band_rows, columns)
    here_now = [place.m, place.c, place.zh, place.zl, place.part, place.z, extent_here[0], extent_here[1]]
    info = jnp.stack(here_now).astype(jnp.int32)
    areas = area.reshape(1)

    own_parts, other_parts = split_features(shape, features.reshape(band, channels), own_mask, place.c)
    held = by_xor([own_parts, place.swap(other_parts, c=1)], place.c)
    held = [by_xor([v[q] for q in range(nzl)], place.zl) for v in by_xor(held, place.zh)]

    def sent(image, k, first=()):
        kh, kl = divmod(k, nzl)
        v = held[kh ^ image][kl]
        return place.swap(after(v, first), zh=kh, zl=kl) if k else v

    steps = doubling(place)
    nd_bits = (place.nd // 2).bit_length() - 1
    projection = projection_weight.T
    if pieces:
        sources = line_pieces(place, dilated_weight, pointwise_weight, pooling_weight)
        crossed = place.swap(sources[0][:FIRST], zh=1)
        neighbour = after(place.swap(sources[1], zl=1), crossed, own_parts, other_parts, partner)
        near, rest = packed_near(shape, place.zl, sources[0], neighbour)
        rest = place.swap(rest, zh=1)
        near_x, near_y = plane_direct(place, near)
        near_d = plane_diagonal(place, near_x, near_y)
        far = packed_far(shape, place.zl, crossed, after(rest, near_d, held))
        crossing_band = sent(0, nzl, first=far)
        far_x, far_y = after(plane_direct(place, far), crossing_band)
        far_d = plane_diagonal(place, far_x, far_y)
        bands = [sent(0, k, first=far_x) for k in range(nzl)] + [crossing_band]
        bands += [sent(0, k, first=far_x) for k in range(nzl + 1, nr)]
        near = assembled_weights(shape, info, near, near_x, near_y, near_d)
        weights = [near, assembled_weights(shape, info, far, far_x, far_y, after(far_d, near))]
    else:
        bands = [sent(0, k) for k in range(nr)]
        weights = gathered_tiles(place, dilated_weight, pointwise_weight, pooling_weight)
        weights = by_xor([weights[:, : out // 2], weights[:, out // 2 :]], place.zh)

    def reduce(keep, got):
        bands_of = lambda v: v.reshape(nzl, band, v.shape[1])
        at = lambda k: [lax.dynamic_index_in_dim(bands_of(v), place.zl ^ k, 0, keepdims=False) for v in (keep, got)]
        summed = lambda k: at(k)[0] + at(k)[1].astype(jnp.float32)
        swapped = [place.swap(summed(k).astype(jnp.bfloat16), zl=k) for k in range(1, nzl)]
        return sum((v.astype(jnp.float32) for v in swapped), summed(0))

    ready = (bands, weights)
    keep, given, pooled, lifted = branch_sums(shape, info, areas, bands, weights)
    far_bands = [sent(1, k, first=ready) for k in range(nzl + 1)]
    projection = after(projection, ready)
    for step in steps[: -nd_bits - 2]:
        projection = joined(place, projection, step)
    given = after(given, far_bands, projection)
    projection = joined(place, after(projection, given), steps[-nd_bits - 2])
    got, projection = after((place.swap(given, c=1), projection), projection)
    projection = joined(place, projection, steps[-nd_bits - 1])
    upstream_low = to_logical(place, after(cotangent.reshape(band, out), got))
    plane = [projection] + [place.swap(projection, m=k) for k in range(1, images // 2)]
    sums = after(reduce(keep, got), plane, upstream_low)
    projection = jnp.stack(by_xor(plane, place.m))
    projection = projection.reshape((place.nd, nr) + projection_weight.shape[::-1])
    projection = jnp.transpose(projection, (1, 2, 0, 3)).reshape(out, -1)
    z = [sums[:, k * out : (k + 1) * out] for k in (3, 2, 1, 0)]

    local_count = jnp.sum(mask)
    stats = [local_moments(v, mask, local_count) for v in z]
    table = (lax.broadcasted_iota(jnp.int32, (images, 1), 0) == place.image).astype(jnp.float32) * lifted[0:1]
    average, spread, count, pool_pre = moments(
        place,
        jnp.concatenate([s for s, _ in stats], axis=0),
        jnp.concatenate([q for _, q in stats], axis=0),
        local_count,
        table,
    )
    inv_std = lax.rsqrt(spread + epsilon)
    normed = [(z[k] - average[k : k + 1]) * inv_std[k : k + 1] for k in range(4)]
    pre_act = [norm_gain[k : k + 1] * normed[k] + norm_bias[k : k + 1] for k in range(4)]

    pool_average = jnp.mean(pool_pre, axis=0, keepdims=True)
    pool_centred = pool_pre - pool_average
    pool_inv = lax.rsqrt(jnp.mean(pool_centred * pool_centred, axis=0, keepdims=True) + epsilon)
    pool_normed = pool_centred * pool_inv
    pool_lift = norm_gain[4:5] * pool_normed + norm_bias[4:5]
    here = lambda rows: lax.dynamic_slice_in_dim(rows, place.image, 1, axis=0)
    pool_act = here(jax.nn.silu(pool_lift))

    concat = jnp.concatenate([jax.nn.silu(u) * mask for u in pre_act] + [pool_act * mask], axis=1).astype(jnp.bfloat16)
    pooled_far = place.swap(pooled, zh=1)
    proj_pre = dot(concat, projection, NT)
    proj_sums, proj_squares = local_moments(proj_pre, mask, local_count)
    proj_average, proj_spread, _, _ = moments(place, proj_sums, proj_squares, local_count)
    proj_inv = lax.rsqrt(proj_spread + epsilon)
    proj_normed = (proj_pre - proj_average) * proj_inv
    proj_lift = norm_gain[5:6] * proj_normed + norm_bias[5:6]
    output_here = (jax.nn.silu(proj_lift) * mask).astype(jnp.bfloat16)

    upstream = upstream_low.astype(jnp.float32) * mask * silu_slope(proj_lift)
    sums = jnp.concatenate(
        [jnp.sum(upstream * proj_normed, axis=0, keepdims=True), jnp.sum(upstream, axis=0, keepdims=True)], axis=0
    )
    proj_totals = total(place, sums)
    proj_gain_grad, proj_bias_grad = proj_totals[0:1], proj_totals[1:2]
    gain = norm_gain[5:6]
    proj_delta = (
        mask
        * proj_inv
        * (gain * upstream - gain * proj_bias_grad / count - proj_normed * gain * proj_gain_grad / count)
    ).astype(jnp.bfloat16)
    concat_grad = dot(proj_delta, projection, NN)
    projection_partial = lambda first: dot(after(proj_delta, first), concat, TN)
    branch_up = [
        concat_grad[:, k * out : (k + 1) * out] * mask * silu_slope(pre_act[k]) for k in range(4)
    ]
    pool_part = jnp.sum(concat_grad[:, 4 * out :] * mask, axis=0, keepdims=True)
    table = (lax.broadcasted_iota(jnp.int32, (images, 1), 0) == place.image).astype(jnp.float32) * pool_part
    totals = total(
        place,
        after(jnp.concatenate(
            [jnp.sum(branch_up[k] * normed[k], axis=0, keepdims=True) for k in range(4)]
            + [jnp.sum(branch_up[k], axis=0, keepdims=True) for k in range(4)]
            + [table],
            axis=0,
        ), pooled_far),
    )
    branch_gain_grad, branch_bias_grad = totals[:4], totals[4:8]
    pool_up = totals[8:] * silu_slope(pool_lift)
    pool_gain_grad = jnp.sum(pool_up * pool_normed, axis=0, keepdims=True)
    pool_bias_grad = jnp.sum(pool_up, axis=0, keepdims=True)
    pool_deltas = pool_inv * (
        norm_gain[4:5] * pool_up
        - norm_gain[4:5] * pool_bias_grad / images
        - pool_normed * norm_gain[4:5] * pool_gain_grad / images
    )
    low_rows = lambda rows: jnp.pad(rows, ((0, 16 - rows.shape[0]), (0, 0))).astype(jnp.bfloat16)
    pool_pair = lax.dynamic_slice_in_dim(pool_deltas, 2 * place.m, 2, axis=0)
    halves = lambda v, n: by_xor([v[:, n * out : n * out + out // 2], v[:, n * out + out // 2 : (n + 1) * out]], place.zh)
    deltas = []
    for k in range(4):
        gain = norm_gain[k : k + 1]
        deltas.append(
            mask
            * inv_std[k : k + 1]
            * (
                gain * branch_up[k]
                - gain * branch_bias_grad[k : k + 1] / count
                - normed[k] * gain * branch_gain_grad[k : k + 1] / count
            )
        )
    delta = jnp.concatenate(deltas, axis=1).astype(jnp.bfloat16)
    crossing = jnp.concatenate([halves(delta, k)[1] for k in range(4)], axis=1)

    def over_group(v, first):
        near = [v] + [after(place.swap(v, zl=k), first) for k in range(1, nzl)]
        return near + [place.swap(n, c=1) for n in near]

    crossing = place.swap(crossing, zh=1)
    rows = projection_weight.shape[0]
    part = projection_partial(delta).astype(jnp.bfloat16).reshape(out, images // 2, 2, rows)
    part = jnp.transpose(part, (2, 1, 0, 3)).reshape(2, images // 2, 2, nzl, out // nr, rows)
    part = halved(place, [part[k] for k in range(2)], steps[-nd_bits - 1])
    spread_deltas = over_group(delta, (crossing, part))
    part = m_halved(place, after(part, spread_deltas), steps, 1)
    far_deltas = [crossing] + [place.swap(crossing, zl=k) for k in range(1, nzl)]
    inputs = input_gradient(shape, info, areas, spread_deltas, low_rows(here(pool_deltas)), weights)

    far_bands += [sent(1, k, first=spread_deltas) for k in range(nzl + 1, nr)]
    crossing = after(far_deltas, inputs, far_bands)
    pooled_pair = pooled + jnp.roll(pooled_far, 1, axis=0)
    pool_pair = jnp.concatenate([pool_pair[i : i + 1] for i in range(2)], axis=0)
    pool_pair = jnp.concatenate(by_xor([pool_pair[0:1], pool_pair[1:2]], place.zh), axis=0)
    pool_pair = halves(low_rows(pool_pair), 0)[0]
    far_deltas = crossing + [place.swap(n, c=1) for n in crossing]
    grads = weight_gradients(shape, info, bands, far_bands, spread_deltas, far_deltas, pool_pair, pooled_pair)

    done = (far_deltas, far_bands, part)
    handed = [place.swap(after(inputs[nzl + k], done), zh=1) for k in range(1, nzl)]
    near_handed = [place.swap(after(inputs[k], done), zl=k) for k in range(1, nzl)]
    output = to_logical(place, after(output_here, inputs))
    part = m_halved(place, after(part, inputs), steps, 2)
    crossed = (handed, near_handed, output, part)
    if pieces:
        pairs = [[grads[2 * rel], grads[2 * rel + 1]] for rel in range(4)]
        first_d, second_d = plane_scatter_diagonal(place, pairs)
        first_d, second_d = after((first_d, second_d), crossed, part)
        quarters = plane_scatter(place, pairs, first_d, second_d)
    else:
        quarters = grads
    part, last = after((part, inputs[nzl]), crossed)
    part = part.reshape((2, nzl) + part.shape[-2:])
    part = halved(place, [part[k] for k in range(2)], steps[-nd_bits - 2])
    last = place.swap(last, zh=1)
    handed = [place.swap(after(handed[k - 1], near_handed), zl=k) for k in range(1, nzl)]
    returned = by_xor([[inputs[0]] + near_handed, [last] + handed], place.zh)
    quarters = after(quarters, part, output, returned)
    returned = by_xor(returned, place.c)
    traded = place.swap(jnp.stack(returned[1]), c=1)
    feature_gradient = join_features(shape, returned[0], [traded[k] for k in range(nzl)], place.c, place.zl)
    if pieces:
        dilated_gradient, pointwise_gradient, pooling_gradient = line_back(place, quarters, feature_gradient)
    else:
        dilated_gradient, pointwise_gradient, pooling_gradient = scattered_tiles(place, quarters[0])
    part = after(part, quarters)
    for step in [step for step in steps if "zl" in step[0]]:
        part = part.reshape((-1, 2) + part.shape[-2:])
        part = halved(place, [part[:, k] for k in range(2)], step)
    projection_gradient = part.reshape(out // nr, rows).astype(jnp.float32).T

    return (
        output.reshape(cotangent.shape),
        feature_gradient.reshape(features.shape),
        pointwise_gradient,
        pooling_gradient,
        dilated_gradient,
        projection_gradient,
        jnp.concatenate([branch_gain_grad, pool_gain_grad, proj_gain_grad], axis=0),
        jnp.concatenate([branch_bias_grad, pool_bias_grad, proj_bias_grad], axis=0),
    )


def solution(mesh):
    banded = P("dp", "rows", None, None)
    blocks = P("dp", "rows")
    return jax.shard_map(
        on_device,
        mesh=mesh,
        in_specs=(banded, P("dp", None), blocks, blocks, blocks, blocks, P(), P(), banded),
        out_specs=(banded, banded, blocks, blocks, blocks, blocks, P(), P()),
        check_vma=False,
    )
```

```python
import jax
import jax.numpy as jnp
from jax import lax
from jax.experimental import pallas as pl
from jax.experimental.pallas import tpu as pltpu
from jax.sharding import PartitionSpec as P

epsilon = 1e-05
dilations = (6, 12, 18)
LANES = 128
BLOCK_ROWS = 6
AXES = ("dp", "rows")
FULL, SHORT, PER_CHIP = 14, 13, 27
SLOTS = FULL + 2 + SHORT
FIRST = 14
CUT = 15
NT = (((1,), (1,)), ((), ()))
TN = (((0,), (0,)), ((), ()))
NN = (((1,), (0,)), ((), ()))


def dot(first, second, dims):
    return lax.dot_general(first, second, dims, preferred_element_type=jnp.float32)


def after(x, *first):
    return lax.optimization_barrier((x, first))[0]


def silu_slope(values):
    sigma = jax.nn.sigmoid(values)
    return sigma * (1.0 + values * (1.0 - sigma))


class Place:
    def __init__(self):
        self.nd, self.nr = lax.axis_size("dp"), lax.axis_size("rows")
        self.nzl = self.nr // 2
        d, z = lax.axis_index("dp"), lax.axis_index("rows")
        self.d, self.z = d, z
        self.m, self.c = d // 2, d % 2
        self.zh, self.zl = z // self.nzl, z % self.nzl
        self.part = self.c * self.nzl + self.zl
        self.image = 2 * self.m + self.zh

    def swap(self, x, m=0, c=0, zh=0, zl=0):
        nzl = self.nzl
        pairs = []
        for flat in range(self.nd * self.nr):
            d, z = divmod(flat, self.nr)
            pairs.append((flat, (d ^ (2 * m + c)) * self.nr + (z ^ (zh * nzl + zl))))
        return lax.ppermute(x, AXES, pairs)


def by_xor(items, index):
    items = list(items)
    bit = 1
    while bit < len(items):
        flip = (index & bit) != 0
        pick = lambda a, b: jnp.where(flip, a, b)
        items = [jax.tree.map(pick, items[k ^ bit], items[k]) for k in range(len(items))]
        bit *= 2
    return items


def tree(items):
    items = list(items)
    while len(items) > 1:
        items = [items[i] + items[i + 1] for i in range(0, len(items), 2)]
    return items[0]


def exchange_stages(place):
    return (
        [dict(c=1)],
        [dict(m=k) for k in range(1, place.nd // 2)],
        [dict(zh=k // place.nzl, zl=k % place.nzl) for k in range(1, place.nr)],
    )


def total(place, x):
    for stage in exchange_stages(place):
        x = tree([x] + [place.swap(x, **s) for s in stage])
    return x


def merged(xs, k):
    whole = tree(xs)
    mean = whole[:k] / jnp.maximum(whole[2 * k : 2 * k + 1], 1.0)
    between = []
    for y in xs:
        own = y[2 * k : 2 * k + 1]
        gap = y[:k] / jnp.maximum(own, 1.0) - mean
        between.append(own * gap * gap)
    return jnp.concatenate([whole[:k], whole[k : 2 * k] + tree(between), whole[2 * k :]], axis=0)


def exchanged(place, x, combine):
    *stages, last = exchange_stages(place)
    for stage in stages:
        x = combine([x] + [place.swap(x, **s) for s in stage])
    return [x] + [place.swap(x, **s) for s in last]


def line_pieces(place, dilated, pointwise, pooling):
    tiles = lambda w: jnp.transpose(w.T.reshape(w.shape[1], w.shape[0] // LANES, LANES), (1, 0, 2))
    dil, one, pool = tiles(dilated), tiles(pointwise), tiles(pooling)
    other = [dil[2 + r :: 4][:SHORT] for r in range(2)]
    got = place.swap(jnp.concatenate(other, axis=0), c=1)
    same = [jnp.concatenate([dil[r::4][:FULL], one[r : r + 1], pool[r : r + 1]], axis=0) for r in range(2)]
    whole = [jnp.concatenate([same[r], got[r * SHORT : (r + 1) * SHORT]], axis=0) for r in range(2)]
    return by_xor(whole, place.zl)


def plane_direct(place, half):
    return place.swap(half, m=1), place.swap(half, m=2)


def plane_diagonal(place, by_x, by_y):
    return place.swap(by_x[:CUT], m=2), place.swap(by_y[CUT:], m=1)


def add_low(first, *others):
    out = first.astype(jnp.float32)
    for o in others:
        out = out + o.astype(jnp.float32)
    return out.astype(jnp.bfloat16)


def plane_scatter_diagonal(place, pieces):
    return place.swap(pieces[3][0], m=2), place.swap(pieces[3][1], m=1)


def plane_scatter(place, pieces, first_d, second_d):
    to_x = jnp.stack([add_low(pieces[1][0], first_d), pieces[1][1]])
    to_y = jnp.stack([pieces[2][0], add_low(pieces[2][1], second_d)])
    by_x, by_y = place.swap(to_x, m=1), place.swap(to_y, m=2)
    return [add_low(pieces[0][q], by_x[q], by_y[q]) for q in range(2)]


def line_back(place, quarters, first):
    by_kl = by_xor(quarters, place.zl)
    by_part = by_xor([by_kl[0], after(place.swap(by_kl[1], zl=1), first)], place.zl)
    same = [p[: FULL + 2] for p in by_part]
    got = place.swap(jnp.concatenate([p[FULL + 2 :] for p in by_part], axis=0), c=1)
    other = [got[r * SHORT : (r + 1) * SHORT] for r in range(2)]
    gap = jnp.zeros((FULL - SHORT,) + other[0].shape[1:], other[0].dtype)
    dil = jnp.stack([s[:FULL] for s in same] + [jnp.concatenate([o, gap], axis=0) for o in other], axis=1)
    dil = dil.reshape((4 * FULL,) + dil.shape[2:])[: 2 * PER_CHIP]
    rows = lambda t: jnp.transpose(t, (1, 0, 2)).reshape(t.shape[1], t.shape[0] * LANES).astype(jnp.float32).T
    one = jnp.stack([s[FULL] for s in same])
    pool = jnp.stack([s[FULL + 1] for s in same])
    return rows(dil), rows(one), rows(pool)


def gathered_tiles(place, dilated, pointwise, pooling):
    whole = []
    for w in (dilated, pointwise, pooling):
        w = lax.all_gather(w, "rows", axis=1, tiled=True)
        w = lax.all_gather(w, "dp", axis=0, tiled=True)
        channels = pointwise.shape[0] * place.nd
        taps = w.shape[0] // channels
        w = w.reshape(taps, channels // (LANES * place.nr), place.nr, LANES, w.shape[1])
        w = lax.dynamic_index_in_dim(w, place.part, 2, keepdims=False)
        whole.append(jnp.transpose(w.reshape(taps, channels // place.nr, w.shape[-1]), (0, 2, 1)))
    return jnp.concatenate(whole, axis=0)


def scattered_tiles(place, gradients):
    outs = []
    taps, half, width = gradients.shape
    for g in (gradients[: taps - 2], gradients[taps - 2 : taps - 1], gradients[taps - 1 :]):
        g = jnp.transpose(g, (0, 2, 1)).reshape(g.shape[0], width // LANES, 1, LANES, half)
        spread = jnp.zeros((g.shape[0], width // LANES, place.nr, LANES, 2 * half), g.dtype)
        g = lax.dynamic_update_slice(spread, g, (0, 0, place.part, 0, place.zh * half)).reshape(-1, 2 * half)
        g = lax.psum_scatter(g, "dp", scatter_dimension=0, tiled=True)
        outs.append(lax.psum_scatter(g, "rows", scatter_dimension=1, tiled=True).astype(jnp.float32))
    return outs


def doubling(place):
    steps = []
    for name, index, size in (("zl", place.zl, place.nzl), ("zh", place.zh, 2), ("c", place.c, 2), ("m", place.m, place.nd // 2)):
        bit = 1
        while bit < size:
            steps.append(({name: bit}, (index & bit) != 0))
            bit *= 2
    return steps


def joined(place, x, step):
    swap, upper = step
    return jnp.stack(by_xor([x, place.swap(x, **swap)], upper.astype(jnp.int32)))


def halved(place, x, step):
    swap, upper = step
    mine = by_xor([x[0], x[1]], upper.astype(jnp.int32))
    return add_low(mine[0], place.swap(mine[1], **swap))


def m_halved(place, x, steps, first):
    for step in [step for step in steps if "m" in step[0]]:
        if (step[0]["m"] == 1) == (first == 1):
            x = x.reshape((-1, 2) + x.shape[1:])
            x = halved(place, [x[:, k] for k in range(2)], step)
    return x


class Shape:
    def __init__(self, band_rows, columns, nr, width, out, pieces):
        self.band_rows, self.columns, self.nr, self.width, self.out = band_rows, columns, nr, width, out
        self.rows = band_rows * nr
        self.band, self.pixels = band_rows * columns, band_rows * columns * nr
        self.block = BLOCK_ROWS * columns
        self.blocks = self.rows // BLOCK_ROWS
        self.pieces = pieces
        self.quarter = out // 4

    def regions(self, dilation):
        cuts = sorted({0, min(dilation, self.rows), max(self.rows - dilation, 0), self.rows})
        for lo, hi in zip(cuts, cuts[1:]):
            yield lo, hi, [r for r in range(3) if 0 <= lo + (r - 1) * dilation and hi + (r - 1) * dilation <= self.rows]


ANY = pl.BlockSpec(memory_space=pl.ANY)
SMEM = pl.BlockSpec(memory_space=pltpu.SMEM)
VMEM = pl.BlockSpec(memory_space=pltpu.VMEM)
PARAMS = pltpu.CompilerParams(vmem_limit_bytes=58 * 2**20)
SMALL = pltpu.CompilerParams(vmem_limit_bytes=12 * 2**20)


LIGHT = pl.CostEstimate(flops=0, bytes_accessed=0, transcendentals=0)


def lanes_at(start, size=LANES):
    return pl.ds(pl.multiple_of(start, LANES), size)


def start_bands(shape, refs, scratch, sem, part):
    for k, ref in enumerate(refs):
        pltpu.make_async_copy(ref, scratch.at[pl.ds((part ^ k) * shape.band, shape.band), :], sem.at[k]).start()


def wait_bands(shape, refs, scratch, sem):
    for k, ref in enumerate(refs):
        pltpu.make_async_copy(ref, scratch.at[pl.ds(k * shape.band, shape.band), :], sem.at[k]).wait()


def split_features(shape, features, mask, c):
    tiles, n = shape.width // LANES, shape.nr // 2

    def kernel(info, x, mask_ref, *outs):
        valid = mask_ref[...].astype(jnp.bfloat16)
        for k, out in enumerate(outs):
            for q in range(n):
                for i in range(tiles):
                    at = (i * shape.nr + (info[0] ^ k) * n + q) * LANES
                    out[q, :, i * LANES : (i + 1) * LANES] = x[:, lanes_at(at)] * valid

    return pl.pallas_call(
        kernel,
        out_shape=[jax.ShapeDtypeStruct((n, shape.band, shape.width), jnp.bfloat16)] * 2,
        in_specs=[SMEM, VMEM, VMEM],
        out_specs=[VMEM] * 2,
        compiler_params=SMALL,
        cost_estimate=LIGHT,
        name="split_features",
    )(c.reshape(1), features, mask)


def join_features(shape, own, other, c, zl):
    tiles, n = shape.width // LANES, shape.nr // 2

    def kernel(info, *refs):
        for k, part in enumerate(refs[: 2 * n]):
            core, q = info[0] ^ (k // n), info[1] ^ (k % n)
            for i in range(tiles):
                at = (i * shape.nr + core * n + q) * LANES
                refs[2 * n][:, lanes_at(at)] = part[:, i * LANES : (i + 1) * LANES]

    return pl.pallas_call(
        kernel,
        out_shape=jax.ShapeDtypeStruct((shape.band, shape.width * shape.nr), jnp.bfloat16),
        in_specs=[SMEM] + [VMEM] * shape.nr,
        out_specs=VMEM,
        compiler_params=SMALL,
        cost_estimate=LIGHT,
        name="join_features",
    )(jnp.stack([c, zl]).astype(jnp.int32), *own, *other)


def packed_near(shape, zl, own, neighbour):
    size = shape.quarter

    def kernel(info, own, neighbour, out, rest):
        for kl, ref in enumerate((own, neighbour)):
            out[:, pl.ds(pl.multiple_of((info[0] ^ kl) * size, size), size), :] = ref[...]
        rest[: SLOTS - FIRST] = own[FIRST:]
        rest[SLOTS - FIRST :] = neighbour[...]

    return pl.pallas_call(
        kernel,
        out_shape=[
            jax.ShapeDtypeStruct((SLOTS, 2 * size, LANES), jnp.bfloat16),
            jax.ShapeDtypeStruct((2 * SLOTS - FIRST, size, LANES), jnp.bfloat16),
        ],
        in_specs=[SMEM, VMEM, VMEM],
        out_specs=[VMEM, VMEM],
        compiler_params=SMALL,
        cost_estimate=LIGHT,
        name="packed_near",
    )(zl.reshape(1), own, neighbour)


def packed_far(shape, zl, first, rest):
    size = shape.quarter

    def kernel(info, first, rest, out):
        for kl in range(2):
            columns = pl.ds(pl.multiple_of((info[0] ^ kl) * size, size), size)
            if kl == 0:
                out[:FIRST, columns, :] = first[...]
                out[FIRST:, columns, :] = rest[: SLOTS - FIRST]
            else:
                out[:, columns, :] = rest[SLOTS - FIRST :]

    return pl.pallas_call(
        kernel,
        out_shape=jax.ShapeDtypeStruct((SLOTS, 2 * size, LANES), jnp.bfloat16),
        in_specs=[SMEM, VMEM, VMEM],
        out_specs=VMEM,
        compiler_params=SMALL,
        cost_estimate=LIGHT,
        name="packed_far",
    )(zl.reshape(1), first, rest)


def chip_slot(t, c):
    return jnp.where(jnp.where(c == 0, t < FULL, t >= SHORT), t - SHORT * c, FULL + 2 + t - FULL * (1 - c))


def assembled_weights(shape, info, own, by_x, by_y, diagonal):
    def kernel(info, *refs):
        ins, out, sem = refs[:5], refs[5], refs[6]
        m, c = info[0], info[1]

        def copy(ref, slot, tap, lane):
            pltpu.make_async_copy(ref.at[slot], out.at[tap, :, lanes_at(lane)], sem).start()

        def place(rel, slot, tap, lane):
            if rel < 3:
                copy(ins[rel], slot, tap, lane)
            else:

                @pl.when(slot < CUT)
                def _():
                    copy(ins[3], slot, tap, lane)

                @pl.when(slot >= CUT)
                def _():
                    copy(ins[4], slot - CUT, tap, lane)

        for rel in range(4):
            chip = m ^ rel

            def body(t, carry):
                v = chip * PER_CHIP + t
                place(rel, chip_slot(t, c), v // 4, (v % 4) * LANES)
                return carry

            lax.fori_loop(0, PER_CHIP, body, 0)
            for extra in range(2):
                place(rel, FULL + extra, 27 + extra, chip * LANES)
        pltpu.make_async_copy(out, out, sem).wait()

    return pl.pallas_call(
        kernel,
        out_shape=jax.ShapeDtypeStruct((29, shape.out // 2, shape.width), jnp.bfloat16),
        in_specs=[SMEM] + [ANY] * 5,
        out_specs=VMEM,
        scratch_shapes=[pltpu.SemaphoreType.DMA],
        compiler_params=PARAMS,
        cost_estimate=LIGHT,
        name="assembled_weights",
    )(info, own, by_x, by_y, *diagonal)


def shifted(values, by, columns):
    if by == 0:
        return values
    pixels = values.shape[0]
    source = lax.broadcasted_iota(jnp.int32, (pixels, 1), 0) % columns - by
    return jnp.where((source >= 0) & (source < columns), pltpu.roll(values, by % pixels, 0), 0.0)


def send_halves(shape, c, kept, low, outs, sem):
    half = shape.pixels // 2
    copies = []
    for n, (source, core) in enumerate(((kept, c), (low, 1 - c))):
        rows = source.at[pl.ds(pl.multiple_of(core * half, half), half)]
        copies.append(pltpu.make_async_copy(rows, outs[n], sem.at[n]))
    for copy in copies:
        copy.start()
    for copy in copies:
        copy.wait()


def half_shapes(shape, n):
    half = shape.pixels // 2
    return [
        jax.ShapeDtypeStruct((half, n * shape.out), jnp.float32),
        jax.ShapeDtypeStruct((half, n * shape.out), jnp.bfloat16),
    ]


def start_taps(weights, scratch, sem, taps, zh):
    half = weights[0].shape[1]
    for n, tap in enumerate(taps):
        for kh, ref in enumerate(weights):
            columns = pl.ds(pl.multiple_of((zh ^ kh) * half, half), half)
            pltpu.make_async_copy(ref.at[tap], scratch.at[n, columns], sem.at[n]).start()


def wait_taps(scratch, sem, some):
    for n in some:
        pltpu.make_async_copy(scratch.at[n], scratch.at[n], sem.at[n]).wait()


def dilated_products(shape, branch, x, w, first, y):
    dilation, columns = dilations[branch], shape.columns
    for s in range(3):
        for lo, hi, rs in shape.regions(dilation):
            pixels = jnp.concatenate(
                [x[(lo + (r - 1) * dilation) * columns : (hi + (r - 1) * dilation) * columns, :] for r in rs], axis=1
            )
            taps = jnp.concatenate([w[first + 3 * s + r] for r in rs], axis=1)
            y[s, lo * columns : hi * columns, :] = dot(pixels, taps, NT)


def put_dilated(shape, branch, y, kept, low, lane):
    dilation, columns = dilations[branch], shape.columns
    for blk in range(shape.blocks):
        at = slice(blk * shape.block, (blk + 1) * shape.block)
        z = y[1, at, :] + shifted(y[0, at, :], dilation, columns) + shifted(y[2, at, :], -dilation, columns)
        kept[at, lane : lane + shape.out] = z
        low[at, lane : lane + shape.out] = z.astype(jnp.bfloat16)


def taps_of(branch):
    return [9 * branch + 3 * r + s for s in range(3) for r in range(3)]


def branch_sums(shape, info, area, bands, weights):
    nr = shape.nr

    def kernel(info, area, *refs):
        ins, weights = refs[:nr], refs[nr : nr + 2]
        keep, sent, pooled, lifted, x, w, y, kept, low_sums, band_sem, w_sem, out_sem = refs[nr + 2 :]
        start_bands(shape, ins, x, band_sem, info[5])
        start_taps(weights, w, w_sem, taps_of(2) + taps_of(1) + taps_of(0) + [27, 28], info[2])
        wait_bands(shape, ins, x, band_sem)
        wait_taps(w, w_sem, range(29))
        for n, branch in enumerate((2, 1, 0)):
            dilated_products(shape, branch, x, w, 9 * n, y.at[n % 2])
            put_dilated(shape, branch, y.at[n % 2], kept, low_sums, n * shape.out)
        z = dot(x[...], w[27], NT)
        kept[:, 3 * shape.out :] = z
        low_sums[:, 3 * shape.out :] = z.astype(jnp.bfloat16)
        sums = jnp.zeros((1, shape.width), jnp.float32)
        for blk in range(shape.blocks):
            values = x[blk * shape.block : (blk + 1) * shape.block, :]
            sums = sums + jnp.sum(values.astype(jnp.float32), axis=0, keepdims=True)
        low = jnp.broadcast_to(sums / area[0], pooled.shape).astype(jnp.bfloat16)
        first = lax.broadcasted_iota(jnp.int32, pooled.shape, 0) == 0
        pooled[...] = jnp.where(first, low.astype(jnp.float32), 0.0).astype(jnp.bfloat16)
        lifted[...] = dot(pooled[...], w[28], NT)
        send_halves(shape, info[1], kept, low_sums, (keep, sent), out_sem)

    return pl.pallas_call(
        kernel,
        out_shape=half_shapes(shape, 4)
        + [jax.ShapeDtypeStruct((16, shape.width), jnp.bfloat16), jax.ShapeDtypeStruct((16, shape.out), jnp.float32)],
        in_specs=[SMEM, SMEM] + [ANY] * (nr + 2),
        out_specs=[ANY] * 2 + [VMEM] * 2,
        scratch_shapes=[
            pltpu.VMEM((shape.pixels, shape.width), jnp.bfloat16),
            pltpu.VMEM((29, shape.out, shape.width), jnp.bfloat16),
            pltpu.VMEM((2, 3, shape.pixels, shape.out), jnp.float32),
            pltpu.VMEM((shape.pixels, 4 * shape.out), jnp.float32),
            pltpu.VMEM((shape.pixels, 4 * shape.out), jnp.bfloat16),
            pltpu.SemaphoreType.DMA((nr,)),
            pltpu.SemaphoreType.DMA((29,)),
            pltpu.SemaphoreType.DMA((2,)),
        ],
        compiler_params=PARAMS,
        cost_estimate=LIGHT,
        name="branch_sums",
    )(info, area, *bands, *weights)


def band_mask(shape, info):
    pixel = lax.broadcasted_iota(jnp.int32, (shape.band, 1), 0)
    row, column = info[4] * shape.band_rows + pixel // shape.columns, pixel % shape.columns
    return ((row < info[6]) & (column < info[7])).astype(jnp.float32)


def put_moments(values, mask, ref, at_sum, at_square, count):
    total = jnp.sum(values * mask, axis=0, keepdims=True)
    centred = (values - total / jnp.maximum(count, 1.0)) * mask
    ref[at_sum : at_sum + 1, :] = total
    ref[at_square : at_square + 1, :] = jnp.sum(centred * centred, axis=0, keepdims=True)


def merged_rows(refs, k, n):
    count = tree([ref[2 * n : 2 * n + 1, :] for ref in refs])
    mean = tree([ref[k : k + 1, :] for ref in refs]) / jnp.maximum(count, 1.0)
    between = []
    for ref in refs:
        own = ref[2 * n : 2 * n + 1, :]
        gap = ref[k : k + 1, :] / jnp.maximum(own, 1.0) - mean
        between.append(own * gap * gap)
    squares = tree([ref[n + k : n + k + 1, :] for ref in refs]) + tree(between)
    return mean, squares / count, count


def silu(v):
    return v * jax.nn.sigmoid(v)


def call(shape, kernel, name, outs, out_specs, in_specs, scratch=()):
    return pl.pallas_call(
        kernel,
        out_shape=[jax.ShapeDtypeStruct(*o) for o in outs],
        in_specs=in_specs,
        out_specs=out_specs,
        scratch_shapes=list(scratch),
        compiler_params=SMALL,
        cost_estimate=LIGHT,
        name=name,
    )


TABLE = 16


def branch_moments(shape, info, images, mine, others, lifted):
    n = len(others)

    def kernel(info, mine, lifted, *refs):
        others, (z, rows) = refs[:n], refs[n:]
        mask = band_mask(shape, info)
        count = jnp.sum(mask)
        rows[...] = jnp.zeros(rows.shape, jnp.float32)
        for k in range(4):
            lanes = slice((3 - k) * shape.out, (4 - k) * shape.out)
            value = mine[:, lanes]
            for other in others:
                value = value + other[:, lanes].astype(jnp.float32)
            z[:, k * shape.out : (k + 1) * shape.out] = value
            put_moments(value, mask, rows, k, 4 + k, count)
        rows[8:9, :] = jnp.full((1, shape.out), count, jnp.float32)
        rows[pl.ds(TABLE + 2 * info[0] + info[2], 1), :] = lifted[0:1, :]

    return call(
        shape,
        kernel,
        "branch_moments",
        [((shape.band, 4 * shape.out), jnp.float32), ((TABLE + images, shape.out), jnp.float32)],
        [VMEM] * 2,
        [SMEM] + [VMEM] * (2 + n),
    )(info, mine, lifted, *others)


def projected(shape, info, images, rows, z, projection, gain, bias):
    out = shape.out

    def kernel(info, z, projection, gain, bias, *refs):
        n = len(rows)
        rows_in, (concat, pre, moments, stats) = refs[:n], refs[n:]
        mask = band_mask(shape, info)
        pool = tree([ref[TABLE : TABLE + images, :] for ref in rows_in])
        pool = pool - jnp.sum(pool, axis=0, keepdims=True) / images
        pool_inv = lax.rsqrt(jnp.sum(pool * pool, axis=0, keepdims=True) / images + epsilon)
        pool = pool * pool_inv
        stats[9:10, :] = pool_inv
        stats[TABLE : TABLE + images, :] = pool
        stats[TABLE + images :, :] = gain[4:5, :] * pool + bias[4:5, :]
        for k in range(4):
            average, spread, count = merged_rows(rows_in, k, 4)
            inv = lax.rsqrt(spread + epsilon)
            stats[k : k + 1, :] = average
            stats[4 + k : 5 + k, :] = inv
            lanes = slice(k * out, (k + 1) * out)
            lifted = gain[k : k + 1, :] * ((z[:, lanes] - average) * inv) + bias[k : k + 1, :]
            concat[:, lanes] = (silu(lifted) * mask).astype(jnp.bfloat16)
        stats[8:9, :] = count
        line = stats[pl.ds(TABLE + images + 2 * info[0] + info[2], 1), :]
        concat[:, 4 * out :] = (silu(line) * mask).astype(jnp.bfloat16)
        value = dot(concat[...], projection[...], NT)
        pre[...] = value
        local = jnp.sum(mask)
        put_moments(value, mask, moments, 0, 1, local)
        moments[2:, :] = jnp.full((6, out), local, jnp.float32)

    return call(
        shape,
        kernel,
        "projected",
        [
            ((shape.band, 5 * out), jnp.bfloat16),
            ((shape.band, out), jnp.float32),
            ((8, out), jnp.float32),
            ((TABLE + 2 * images, out), jnp.float32),
        ],
        [VMEM] * 4,
        [SMEM] + [VMEM] * (4 + len(rows)),
    )(info, z, projection, gain, bias, *rows)


def branch_gradients(shape, info, images, rows, upstream, normed, inv, z, stats, projection, gain, bias):
    out = shape.out

    def kernel(info, upstream, normed, inv, z, stats, projection, gain, bias, *refs):
        n = len(rows)
        rows_in, (delta, up, sums, totals) = refs[:n], refs[n:]
        mask = band_mask(shape, info)
        whole = tree([ref[...] for ref in rows_in])
        totals[...] = whole
        count, scale = stats[8:9, :], gain[5:6, :]
        low = (
            mask
            * inv[...]
            * (scale * upstream[...] - scale * whole[1:2] / count - normed[...] * scale * whole[0:1] / count)
        ).astype(jnp.bfloat16)
        delta[...] = low
        sums[...] = jnp.zeros(sums.shape, jnp.float32)
        for k in range(4):
            lanes = slice(k * out, (k + 1) * out)
            at = (z[:, lanes] - stats[k : k + 1, :]) * stats[4 + k : 5 + k, :]
            slope = silu_slope(gain[k : k + 1, :] * at + bias[k : k + 1, :])
            value = dot(low, projection[:, lanes], NN) * mask * slope
            up[:, lanes] = value
            sums[k : k + 1, :] = jnp.sum(value * at, axis=0, keepdims=True)
            sums[4 + k : 5 + k, :] = jnp.sum(value, axis=0, keepdims=True)
        line = jnp.sum(dot(low, projection[:, 4 * out :], NN) * mask, axis=0, keepdims=True)
        sums[pl.ds(8 + 2 * info[0] + info[2], 1), :] = line

    return call(
        shape,
        kernel,
        "branch_gradients",
        [
            ((shape.band, out), jnp.bfloat16),
            ((shape.band, 4 * out), jnp.float32),
            ((8 + images, out), jnp.float32),
            ((8, out), jnp.float32),
        ],
        [VMEM] * 4,
        [SMEM] + [VMEM] * (8 + len(rows)),
    )(info, upstream, normed, inv, z, stats, projection, gain, bias, *rows)


def branch_deltas(shape, info, rows, up, z, stats, gain):
    out, half = shape.out, shape.out // 2

    def kernel(info, up, z, stats, gain, *refs):
        n = len(rows)
        rows_in, (delta, crossing, totals) = refs[:n], refs[n:]
        mask = band_mask(shape, info)
        totals[...] = tree([ref[...] for ref in rows_in])
        count = stats[8:9, :]
        for k in range(4):
            lanes = slice(k * out, (k + 1) * out)
            inv, scale = stats[4 + k : 5 + k, :], gain[k : k + 1, :]
            at = (z[:, lanes] - stats[k : k + 1, :]) * inv
            by_gain, by_bias = totals[k : k + 1, :], totals[4 + k : 5 + k, :]
            value = mask * inv * (scale * up[:, lanes] - scale * by_bias / count - at * scale * by_gain / count)
            delta[:, lanes] = value.astype(jnp.bfloat16)
            crossing[:, k * half : (k + 1) * half] = delta[:, lanes_at(k * out + (1 - info[2]) * half, half)]

    return call(
        shape,
        kernel,
        "branch_deltas",
        [
            ((shape.band, 4 * out), jnp.bfloat16),
            ((shape.band, 4 * half), jnp.bfloat16),
            (rows[0].shape, jnp.float32),
        ],
        [VMEM] * 3,
        [SMEM] + [VMEM] * (4 + len(rows)),
    )(info, up, z, stats, gain, *rows)


def moved_columns(shape, delta, lane, lanes, branch, moved):
    for blk in range(shape.blocks):
        at = slice(blk * shape.block, (blk + 1) * shape.block)
        values = delta[at, lanes_at(lane, lanes)].astype(jnp.float32)
        for s in range(3):
            moved[at, s * lanes : (s + 1) * lanes] = shifted(
                values, (s - 1) * dilations[branch], shape.columns
            ).astype(jnp.bfloat16)


def input_gradient(shape, info, area, deltas, pool_delta, weights):
    nr, columns = shape.nr, shape.columns

    def kernel(info, area, *refs):
        ins, pool_delta, weights = refs[:nr], refs[nr], refs[nr + 1 : nr + 3]
        outs = refs[nr + 3 : 2 * nr + 3]
        delta, moved, w, acc, delta_sem, w_sem = refs[2 * nr + 3 :]
        start_bands(shape, ins, delta, delta_sem, info[4])
        start_taps(weights, w, w_sem, range(29), info[2])
        wait_bands(shape, ins, delta, delta_sem)
        wait_taps(w, w_sem, range(29))
        pool = dot(pool_delta[...], w[28], NN)[0:1] / area[0]
        acc[...] = dot(delta[:, : shape.out], w[27], NN) + pool
        for branch in range(3):
            dilation = dilations[branch]
            moved_columns(shape, delta, (branch + 1) * shape.out, shape.out, branch, moved)
            for lo, hi, rs in shape.regions(dilation):
                rows = [2 - r for r in rs]
                cut = lambda r: moved[(lo - (r - 1) * dilation) * columns : (hi - (r - 1) * dilation) * columns, :]
                pixels = jnp.concatenate([cut(r) for r in rows], axis=1)
                taps = jnp.concatenate([w[9 * branch + 3 * r + s] for r in rows for s in range(3)], axis=0)
                acc[lo * columns : hi * columns, :] += dot(pixels, taps, NN)
        pixel = lax.broadcasted_iota(jnp.int32, (shape.band, 1), 0)
        for k in range(nr):
            first = (info[5] ^ k) * shape.band
            inside = ((pixel + first) // columns < info[6]) & (pixel % columns < info[7])
            values = acc[pl.ds(pl.multiple_of(first, shape.band), shape.band), :]
            outs[k][...] = jnp.where(inside, values, 0.0).astype(jnp.bfloat16)

    return pl.pallas_call(
        kernel,
        out_shape=[jax.ShapeDtypeStruct((shape.band, shape.width), jnp.bfloat16)] * nr,
        in_specs=[SMEM, SMEM] + [ANY] * nr + [VMEM] + [ANY] * 2,
        out_specs=[VMEM] * nr,
        scratch_shapes=[
            pltpu.VMEM((shape.pixels, 4 * shape.out), jnp.bfloat16),
            pltpu.VMEM((shape.pixels, 3 * shape.out), jnp.bfloat16),
            pltpu.VMEM((29, shape.out, shape.width), jnp.bfloat16),
            pltpu.VMEM((shape.pixels, shape.width), jnp.float32),
            pltpu.SemaphoreType.DMA((nr,)),
            pltpu.SemaphoreType.DMA((29,)),
        ],
        compiler_params=PARAMS,
        cost_estimate=pl.CostEstimate(
            flops=44 * shape.pixels * shape.width * shape.out, bytes_accessed=2**24, transcendentals=0
        ),
        name="input_gradient",
    )(info, area, *deltas, pool_delta, *weights)


def weight_gradients(shape, info, bands, far_bands, deltas, far_deltas, pool_deltas, pooled):
    nr, columns, half = shape.nr, shape.columns, shape.out // 2
    n_outs = 8 if shape.pieces else 1
    by_rows = lambda v: v.reshape(v.shape[0] // columns, columns, v.shape[1])
    bands = [by_rows(band) for band in [*bands, *far_bands]]

    def kernel(info, *refs):
        ins, delta_ins, far_delta_ins = (refs[n * nr : (n + 1) * nr] for n in range(3))
        far_ins, refs = refs[3 * nr : 4 * nr], refs[4 * nr :]
        pool_deltas, pooled, outs = refs[0], refs[1], refs[2 : 2 + n_outs]
        x, delta, far_delta, moved, grads, sem, out_sem = refs[2 + n_outs :]
        m, c, zh, part, z = info[0], info[1], info[2], info[4], info[5]
        rows = shape.band_rows
        start_bands(shape, delta_ins, delta, sem.at[0], part)
        start_bands(shape, far_delta_ins, far_delta, sem.at[1], part)
        for image, sources in enumerate((ins, far_ins)):
            for k, ref in enumerate(sources):
                pltpu.make_async_copy(ref, x.at[pl.ds((z ^ k) * rows, rows), image], sem.at[2 + image, k]).start()

        def arrive(n):
            for k in range(nr):
                if n < 2:
                    some = (delta, far_delta)[n].at[pl.ds(k * shape.band, shape.band)]
                else:
                    some = x.at[pl.ds(k * rows, rows), n - 2]
                pltpu.make_async_copy(some, some, sem.at[n, k]).wait()

        def move(branch):
            for image, source in enumerate((delta, far_delta)):
                lane = (branch + 1) * half if image else (branch + 1) * shape.out + zh * half
                for blk in range(shape.blocks):
                    at = slice(blk * shape.block, (blk + 1) * shape.block)
                    values = source[at, lanes_at(lane, half)].astype(jnp.float32)
                    for s in range(3):
                        value = shifted(values, (s - 1) * dilations[branch], columns).astype(jnp.bfloat16)
                        moved[blk * BLOCK_ROWS : (blk + 1) * BLOCK_ROWS, image, :, s * half : (s + 1) * half] = (
                            value.reshape(BLOCK_ROWS, columns, half)
                        )

        flat = lambda v: v.reshape(-1, v.shape[-1])

        def put(tap, value):
            value = value.astype(jnp.bfloat16)
            if not shape.pieces:
                grads[tap] = value
                return
            for i in range(4):
                if tap < 27:
                    v = 4 * tap + i
                    chip, slot = v // PER_CHIP, chip_slot(v % PER_CHIP, c)
                else:
                    chip, slot = i, FULL + tap - 27
                for q in range(2):
                    rows = slice(q * shape.quarter, (q + 1) * shape.quarter)
                    grads[2 * (m ^ chip) + q, slot] = value[rows, i * LANES : (i + 1) * LANES]

        arrive(0)
        arrive(1)
        for branch in range(3):
            move(branch)
            if branch == 0:
                arrive(2)
                arrive(3)
            dilation = dilations[branch]
            for r in range(3):
                up, down = max(0, 1 - r) * dilation, max(0, r - 1) * dilation
                to = flat(moved[up : shape.rows - down])
                value = dot(to, flat(x[down : shape.rows - up]), TN)
                for s in range(3):
                    put(9 * branch + 3 * r + s, value[s * half : (s + 1) * half])
        one = jnp.concatenate(
            [
                delta[:, lanes_at(zh * half, half)].reshape(shape.rows, 1, columns, half),
                far_delta[:, :half].reshape(shape.rows, 1, columns, half),
            ],
            axis=1,
        )
        put(27, dot(flat(one), flat(x[...]), TN))
        put(28, dot(pool_deltas[...], pooled[...], TN))
        copies = [pltpu.make_async_copy(grads.at[n] if shape.pieces else grads, outs[n], out_sem.at[n]) for n in range(n_outs)]
        for copy in copies:
            copy.start()
        for copy in copies:
            copy.wait()

    if shape.pieces:
        out_shape = [jax.ShapeDtypeStruct((SLOTS, shape.quarter, LANES), jnp.bfloat16)] * 8
        grads_shape = (8, SLOTS, shape.quarter, LANES)
    else:
        out_shape = [jax.ShapeDtypeStruct((29, half, shape.width), jnp.bfloat16)]
        grads_shape = (29, half, shape.width)
    return pl.pallas_call(
        kernel,
        out_shape=out_shape,
        in_specs=[SMEM] + [ANY] * (4 * nr) + [VMEM] * 2,
        out_specs=[ANY] * n_outs,
        scratch_shapes=[
            pltpu.VMEM((shape.rows, 2, columns, shape.width), jnp.bfloat16),
            pltpu.VMEM((shape.pixels, 4 * shape.out), jnp.bfloat16),
            pltpu.VMEM((shape.pixels, 2 * shape.out), jnp.bfloat16),
            pltpu.VMEM((shape.rows, 2, columns, 3 * half), jnp.bfloat16),
            pltpu.VMEM(grads_shape, jnp.bfloat16),
            pltpu.SemaphoreType.DMA((4, nr)),
            pltpu.SemaphoreType.DMA((n_outs,)),
        ],
        compiler_params=PARAMS,
        cost_estimate=pl.CostEstimate(
            flops=44 * shape.pixels * shape.width * shape.out, bytes_accessed=2**24, transcendentals=0
        ),
        name="weight_gradients",
    )(info, *bands[:nr], *deltas, *far_deltas, *bands[nr:], pool_deltas, pooled)


def valid_pixels(extent, first_row, rows, columns):
    r = first_row + lax.broadcasted_iota(jnp.int32, (rows, columns), 0)
    w = lax.broadcasted_iota(jnp.int32, (rows, columns), 1)
    return ((r < extent[0]) & (w < extent[1])).astype(jnp.float32).reshape(rows * columns, 1)


def to_logical(place, x):
    return jnp.where(place.zh == place.c, x, place.swap(x, c=1, zh=1))


def on_device(
    features, extent, pointwise_weight, pooling_weight, dilated_weight, projection_weight, norm_gain, norm_bias, cotangent
):
    place = Place()
    nr, nzl = place.nr, place.nzl
    _, band_rows, columns, channels = features.shape
    width, out = channels // nr, norm_gain.shape[1]
    band = band_rows * columns
    pieces = nr == 4 and place.nd == 8 and dilated_weight.shape[0] == 2 * PER_CHIP * LANES
    shape = Shape(band_rows, columns, nr, width, out, pieces)
    images = place.nd

    partner = place.swap(extent, c=1)
    extent_here = jnp.where(place.zh == place.c, extent, partner)[0]
    area = (extent_here[0] * extent_here[1]).astype(jnp.float32)
    mask = valid_pixels(extent_here, place.part * band_rows, band_rows, columns)
    own_mask = valid_pixels(extent[0], place.z * band_rows, band_rows, columns)
    here_now = [place.m, place.c, place.zh, place.zl, place.part, place.z, extent_here[0], extent_here[1]]
    info = jnp.stack(here_now).astype(jnp.int32)
    areas = area.reshape(1)

    own_parts, other_parts = split_features(shape, features.reshape(band, channels), own_mask, place.c)
    held = by_xor([own_parts, place.swap(other_parts, c=1)], place.c)
    held = [by_xor([v[q] for q in range(nzl)], place.zl) for v in by_xor(held, place.zh)]

    def sent(image, k, first=()):
        kh, kl = divmod(k, nzl)
        v = held[kh ^ image][kl]
        return place.swap(after(v, first), zh=kh, zl=kl) if k else v

    steps = doubling(place)
    nd_bits = (place.nd // 2).bit_length() - 1
    projection = projection_weight.T
    if pieces:
        sources = line_pieces(place, dilated_weight, pointwise_weight, pooling_weight)
        crossed = place.swap(sources[0][:FIRST], zh=1)
        neighbour = after(place.swap(sources[1], zl=1), crossed, own_parts, other_parts, partner)
        near, rest = packed_near(shape, place.zl, sources[0], neighbour)
        rest = place.swap(rest, zh=1)
        near_x, near_y = plane_direct(place, near)
        near_d = plane_diagonal(place, near_x, near_y)
        far = packed_far(shape, place.zl, crossed, after(rest, near_d, held))
        crossing_band = sent(0, nzl, first=far)
        far_x, far_y = after(plane_direct(place, far), crossing_band)
        far_d = plane_diagonal(place, far_x, far_y)
        bands = [sent(0, k, first=far_x) for k in range(nzl)] + [crossing_band]
        bands += [sent(0, k, first=crossing_band) for k in range(nzl + 1, nr)]
        near = assembled_weights(shape, info, near, near_x, near_y, near_d)
        weights = [near, assembled_weights(shape, info, far, far_x, far_y, after(far_d, near))]
    else:
        bands = [sent(0, k) for k in range(nr)]
        weights = gathered_tiles(place, dilated_weight, pointwise_weight, pooling_weight)
        weights = by_xor([weights[:, : out // 2], weights[:, out // 2 :]], place.zh)

    def given_on(keep, got):
        bands_of = lambda v: v.reshape(nzl, band, v.shape[1])
        at = lambda k: [lax.dynamic_index_in_dim(bands_of(v), place.zl ^ k, 0, keepdims=False) for v in (keep, got)]
        summed = lambda k: at(k)[0] + at(k)[1].astype(jnp.float32)
        return summed(0), [place.swap(summed(k).astype(jnp.bfloat16), zl=k) for k in range(1, nzl)]

    ready = (bands, weights)
    keep, given, pooled, lifted = branch_sums(shape, info, areas, bands, weights)
    far_bands = [sent(1, k, first=ready) for k in range(nzl + 1)]
    projection = after(projection, ready)
    for step in steps[: -nd_bits - 2]:
        projection = joined(place, projection, step)
    given = after(given, far_bands, projection)
    projection = joined(place, after(projection, given), steps[-nd_bits - 2])
    got, projection = after((place.swap(given, c=1), projection), projection)
    projection = joined(place, projection, steps[-nd_bits - 1])
    upstream_low = to_logical(place, after(cotangent.reshape(band, out), got))
    plane = [projection] + [place.swap(projection, m=k) for k in range(1, images // 2)]
    mine, others = given_on(keep, got)
    mine, others = after((mine, others), plane, upstream_low)
    z, rows = branch_moments(shape, info, images, mine, others, lifted)
    projection = jnp.stack(by_xor(plane, place.m))
    projection = projection.reshape((place.nd, nr) + projection_weight.shape[::-1])
    projection = jnp.transpose(projection, (1, 2, 0, 3)).reshape(out, -1)
    rows = exchanged(place, rows, lambda xs: merged(xs, 4))
    concat, proj_pre, rows, stats = projected(shape, info, images, rows, z, projection, norm_gain, norm_bias)
    pooled_far = place.swap(pooled, zh=1)
    rows = merged(exchanged(place, rows, lambda xs: merged(xs, 1)), 1)
    proj_average, proj_spread = rows[0:1] / rows[2:3], rows[1:2] / rows[2:3]
    proj_inv = lax.rsqrt(proj_spread + epsilon)
    proj_normed = (proj_pre - proj_average) * proj_inv
    proj_lift = norm_gain[5:6] * proj_normed + norm_bias[5:6]
    output_here = (jax.nn.silu(proj_lift) * mask).astype(jnp.bfloat16)

    upstream = upstream_low.astype(jnp.float32) * mask * silu_slope(proj_lift)
    sums = [jnp.sum(upstream * proj_normed, axis=0, keepdims=True), jnp.sum(upstream, axis=0, keepdims=True)]
    rows = exchanged(place, jnp.concatenate(sums + [jnp.zeros((6, out), jnp.float32)], axis=0), tree)
    proj_delta, branch_up, rows, proj_totals = branch_gradients(
        shape, info, images, rows, upstream, proj_normed, proj_inv, z, stats, projection, norm_gain, norm_bias
    )
    projection_partial = lambda first: dot(after(proj_delta, first), concat, TN)
    rows = exchanged(place, rows, tree)
    delta, crossing, totals = branch_deltas(shape, info, after(rows, pooled_far), branch_up, z, stats, norm_gain)
    proj_gain_grad, proj_bias_grad = proj_totals[0:1], proj_totals[1:2]
    branch_gain_grad, branch_bias_grad = totals[:4], totals[4:8]
    pool_inv, pool_normed, pool_lift = stats[9:10], stats[TABLE : TABLE + images], stats[TABLE + images :]
    here = lambda rows: lax.dynamic_slice_in_dim(rows, place.image, 1, axis=0)
    pool_up = totals[8:] * silu_slope(pool_lift)
    pool_gain_grad = jnp.sum(pool_up * pool_normed, axis=0, keepdims=True)
    pool_bias_grad = jnp.sum(pool_up, axis=0, keepdims=True)
    pool_deltas = pool_inv * (
        norm_gain[4:5] * pool_up
        - norm_gain[4:5] * pool_bias_grad / images
        - pool_normed * norm_gain[4:5] * pool_gain_grad / images
    )
    low_rows = lambda rows: jnp.pad(rows, ((0, 16 - rows.shape[0]), (0, 0))).astype(jnp.bfloat16)
    pool_pair = lax.dynamic_slice_in_dim(pool_deltas, 2 * place.m, 2, axis=0)
    halves = lambda v, n: by_xor([v[:, n * out : n * out + out // 2], v[:, n * out + out // 2 : (n + 1) * out]], place.zh)
    def over_group(v, first):
        near = [v] + [after(place.swap(v, zl=k), first) for k in range(1, nzl)]
        return near + [place.swap(n, c=1) for n in near]

    crossing = place.swap(crossing, zh=1)
    rows = projection_weight.shape[0]
    part = projection_partial(delta).astype(jnp.bfloat16).reshape(out, images // 2, 2, rows)
    part = jnp.transpose(part, (2, 1, 0, 3)).reshape(2, images // 2, 2, nzl, out // nr, rows)
    part = halved(place, [part[k] for k in range(2)], steps[-nd_bits - 1])
    spread_deltas = over_group(delta, (crossing, part))
    part = m_halved(place, after(part, spread_deltas), steps, 1)
    far_deltas = [crossing] + [place.swap(crossing, zl=k) for k in range(1, nzl)]
    inputs = input_gradient(shape, info, areas, spread_deltas, low_rows(here(pool_deltas)), weights)

    far_bands += [sent(1, k, first=spread_deltas) for k in range(nzl + 1, nr)]
    crossing = after(far_deltas, inputs, far_bands)
    pooled_pair = pooled + jnp.roll(pooled_far, 1, axis=0)
    pool_pair = jnp.concatenate([pool_pair[i : i + 1] for i in range(2)], axis=0)
    pool_pair = jnp.concatenate(by_xor([pool_pair[0:1], pool_pair[1:2]], place.zh), axis=0)
    pool_pair = halves(low_rows(pool_pair), 0)[0]
    far_deltas = crossing + [place.swap(n, c=1) for n in crossing]
    grads = weight_gradients(shape, info, bands, far_bands, spread_deltas, far_deltas, pool_pair, pooled_pair)

    done = (far_deltas, far_bands, part)
    handed = [place.swap(after(inputs[nzl + k], done), zh=1) for k in range(1, nzl)]
    near_handed = [place.swap(after(inputs[k], done), zl=k) for k in range(1, nzl)]
    output = to_logical(place, after(output_here, inputs))
    part = m_halved(place, after(part, inputs), steps, 2)
    crossed = (handed, near_handed, output, part)
    if pieces:
        pairs = [[grads[2 * rel], grads[2 * rel + 1]] for rel in range(4)]
        first_d, second_d = plane_scatter_diagonal(place, pairs)
        first_d, second_d = after((first_d, second_d), crossed, part)
        quarters = plane_scatter(place, pairs, first_d, second_d)
    else:
        quarters = grads
    part, last = after((part, inputs[nzl]), crossed)
    part = part.reshape((2, nzl) + part.shape[-2:])
    part = halved(place, [part[k] for k in range(2)], steps[-nd_bits - 2])
    last = place.swap(last, zh=1)
    handed = [place.swap(after(handed[k - 1], near_handed), zl=k) for k in range(1, nzl)]
    returned = by_xor([[inputs[0]] + near_handed, [last] + handed], place.zh)
    quarters = after(quarters, part, output, returned)
    returned = by_xor(returned, place.c)
    traded = place.swap(jnp.stack(returned[1]), c=1)
    feature_gradient = join_features(shape, returned[0], [traded[k] for k in range(nzl)], place.c, place.zl)
    if pieces:
        dilated_gradient, pointwise_gradient, pooling_gradient = line_back(place, quarters, feature_gradient)
    else:
        dilated_gradient, pointwise_gradient, pooling_gradient = scattered_tiles(place, quarters[0])
    part = after(part, feature_gradient)
    for step in [step for step in steps if "zl" in step[0]]:
        part = part.reshape((-1, 2) + part.shape[-2:])
        part = halved(place, [part[:, k] for k in range(2)], step)
    projection_gradient = part.reshape(out // nr, rows).astype(jnp.float32).T

    return (
        output.reshape(cotangent.shape),
        feature_gradient.reshape(features.shape),
        pointwise_gradient,
        pooling_gradient,
        dilated_gradient,
        projection_gradient,
        jnp.concatenate([branch_gain_grad, pool_gain_grad, proj_gain_grad], axis=0),
        jnp.concatenate([branch_bias_grad, pool_bias_grad, proj_bias_grad], axis=0),
    )


def solution(mesh):
    banded = P("dp", "rows", None, None)
    blocks = P("dp", "rows")
    return jax.shard_map(
        on_device,
        mesh=mesh,
        in_specs=(banded, P("dp", None), blocks, blocks, blocks, blocks, P(), P(), banded),
        out_specs=(banded, banded, blocks, blocks, blocks, blocks, P(), P()),
        check_vma=False,
    )
```

```python
import jax
import jax.numpy as jnp
from jax import lax
from jax.experimental import pallas as pl
from jax.experimental.pallas import tpu as pltpu
from jax.sharding import PartitionSpec as P

epsilon = 1e-05
dilations = (6, 12, 18)
LANES = 128
BLOCK_ROWS = 6
AXES = ("dp", "rows")
FULL, SHORT, PER_CHIP = 14, 13, 27
SLOTS = FULL + 2 + SHORT
FIRST = 14
CUT = 15
NT = (((1,), (1,)), ((), ()))
TN = (((0,), (0,)), ((), ()))
NN = (((1,), (0,)), ((), ()))


def dot(first, second, dims):
    return lax.dot_general(first, second, dims, preferred_element_type=jnp.float32)


def after(x, *first):
    return lax.optimization_barrier((x, first))[0]


def silu_slope(values):
    sigma = jax.nn.sigmoid(values)
    return sigma * (1.0 + values * (1.0 - sigma))


class Place:
    def __init__(self):
        self.nd, self.nr = lax.axis_size("dp"), lax.axis_size("rows")
        self.nzl = self.nr // 2
        d, z = lax.axis_index("dp"), lax.axis_index("rows")
        self.d, self.z = d, z
        self.m, self.c = d // 2, d % 2
        self.zh, self.zl = z // self.nzl, z % self.nzl
        self.part = self.c * self.nzl + self.zl
        self.image = 2 * self.m + self.zh

    def swap(self, x, m=0, c=0, zh=0, zl=0):
        nzl = self.nzl
        pairs = []
        for flat in range(self.nd * self.nr):
            d, z = divmod(flat, self.nr)
            pairs.append((flat, (d ^ (2 * m + c)) * self.nr + (z ^ (zh * nzl + zl))))
        return lax.ppermute(x, AXES, pairs)


def by_xor(items, index):
    items = list(items)
    bit = 1
    while bit < len(items):
        flip = (index & bit) != 0
        pick = lambda a, b: jnp.where(flip, a, b)
        items = [jax.tree.map(pick, items[k ^ bit], items[k]) for k in range(len(items))]
        bit *= 2
    return items


def tree(items):
    items = list(items)
    while len(items) > 1:
        items = [items[i] + items[i + 1] for i in range(0, len(items), 2)]
    return items[0]


def exchange_stages(place):
    return (
        [dict(c=1)],
        [dict(m=k) for k in range(1, place.nd // 2)],
        [dict(zh=k // place.nzl, zl=k % place.nzl) for k in range(1, place.nr)],
    )


def total(place, x):
    for stage in exchange_stages(place):
        x = tree([x] + [place.swap(x, **s) for s in stage])
    return x


def merged(xs, k):
    whole = tree(xs)
    mean = whole[:k] / jnp.maximum(whole[2 * k : 2 * k + 1], 1.0)
    between = []
    for y in xs:
        own = y[2 * k : 2 * k + 1]
        gap = y[:k] / jnp.maximum(own, 1.0) - mean
        between.append(own * gap * gap)
    return jnp.concatenate([whole[:k], whole[k : 2 * k] + tree(between), whole[2 * k :]], axis=0)


def exchanged(place, x, combine):
    *stages, last = exchange_stages(place)
    for stage in stages:
        x = combine([x] + [place.swap(x, **s) for s in stage])
    return [x] + [place.swap(x, **s) for s in last]


def line_pieces(place, dilated, pointwise, pooling):
    tiles = lambda w: jnp.transpose(w.T.reshape(w.shape[1], w.shape[0] // LANES, LANES), (1, 0, 2))
    dil, one, pool = tiles(dilated), tiles(pointwise), tiles(pooling)
    other = [dil[2 + r :: 4][:SHORT] for r in range(2)]
    got = place.swap(jnp.concatenate(other, axis=0), c=1)
    same = [jnp.concatenate([dil[r::4][:FULL], one[r : r + 1], pool[r : r + 1]], axis=0) for r in range(2)]
    whole = [jnp.concatenate([same[r], got[r * SHORT : (r + 1) * SHORT]], axis=0) for r in range(2)]
    return by_xor(whole, place.zl)


def plane_direct(place, half):
    return place.swap(half, m=1), place.swap(half, m=2)


def plane_diagonal(place, by_x, by_y):
    return place.swap(by_x[:CUT], m=2), place.swap(by_y[CUT:], m=1)


def add_low(first, *others):
    out = first.astype(jnp.float32)
    for o in others:
        out = out + o.astype(jnp.float32)
    return out.astype(jnp.bfloat16)


def plane_scatter_diagonal(place, pieces):
    return place.swap(pieces[3][0], m=2), place.swap(pieces[3][1], m=1)


def plane_scatter(place, pieces, first_d, second_d):
    to_x = jnp.stack([add_low(pieces[1][0], first_d), pieces[1][1]])
    to_y = jnp.stack([pieces[2][0], add_low(pieces[2][1], second_d)])
    by_x, by_y = place.swap(to_x, m=1), place.swap(to_y, m=2)
    return [add_low(pieces[0][q], by_x[q], by_y[q]) for q in range(2)]


def line_back(place, quarters, first):
    by_kl = by_xor(quarters, place.zl)
    by_part = by_xor([by_kl[0], after(place.swap(by_kl[1], zl=1), first)], place.zl)
    same = [p[: FULL + 2] for p in by_part]
    got = place.swap(jnp.concatenate([p[FULL + 2 :] for p in by_part], axis=0), c=1)
    other = [got[r * SHORT : (r + 1) * SHORT] for r in range(2)]
    gap = jnp.zeros((FULL - SHORT,) + other[0].shape[1:], other[0].dtype)
    dil = jnp.stack([s[:FULL] for s in same] + [jnp.concatenate([o, gap], axis=0) for o in other], axis=1)
    dil = dil.reshape((4 * FULL,) + dil.shape[2:])[: 2 * PER_CHIP]
    rows = lambda t: jnp.transpose(t, (1, 0, 2)).reshape(t.shape[1], t.shape[0] * LANES).astype(jnp.float32).T
    one = jnp.stack([s[FULL] for s in same])
    pool = jnp.stack([s[FULL + 1] for s in same])
    return rows(dil), rows(one), rows(pool)


def gathered_tiles(place, dilated, pointwise, pooling):
    whole = []
    for w in (dilated, pointwise, pooling):
        w = lax.all_gather(w, "rows", axis=1, tiled=True)
        w = lax.all_gather(w, "dp", axis=0, tiled=True)
        channels = pointwise.shape[0] * place.nd
        taps = w.shape[0] // channels
        w = w.reshape(taps, channels // (LANES * place.nr), place.nr, LANES, w.shape[1])
        w = lax.dynamic_index_in_dim(w, place.part, 2, keepdims=False)
        whole.append(jnp.transpose(w.reshape(taps, channels // place.nr, w.shape[-1]), (0, 2, 1)))
    return jnp.concatenate(whole, axis=0)


def scattered_tiles(place, gradients):
    outs = []
    taps, half, width = gradients.shape
    for g in (gradients[: taps - 2], gradients[taps - 2 : taps - 1], gradients[taps - 1 :]):
        g = jnp.transpose(g, (0, 2, 1)).reshape(g.shape[0], width // LANES, 1, LANES, half)
        spread = jnp.zeros((g.shape[0], width // LANES, place.nr, LANES, 2 * half), g.dtype)
        g = lax.dynamic_update_slice(spread, g, (0, 0, place.part, 0, place.zh * half)).reshape(-1, 2 * half)
        g = lax.psum_scatter(g, "dp", scatter_dimension=0, tiled=True)
        outs.append(lax.psum_scatter(g, "rows", scatter_dimension=1, tiled=True).astype(jnp.float32))
    return outs


def doubling(place):
    steps = []
    for name, index, size in (("zl", place.zl, place.nzl), ("zh", place.zh, 2), ("c", place.c, 2), ("m", place.m, place.nd // 2)):
        bit = 1
        while bit < size:
            steps.append(({name: bit}, (index & bit) != 0))
            bit *= 2
    return steps


def joined(place, x, step):
    swap, upper = step
    return jnp.stack(by_xor([x, place.swap(x, **swap)], upper.astype(jnp.int32)))


def halved(place, x, step):
    swap, upper = step
    mine = by_xor([x[0], x[1]], upper.astype(jnp.int32))
    return add_low(mine[0], place.swap(mine[1], **swap))


def m_halved(place, x, steps, first):
    for step in [step for step in steps if "m" in step[0]]:
        if (step[0]["m"] == 1) == (first == 1):
            x = x.reshape((-1, 2) + x.shape[1:])
            x = halved(place, [x[:, k] for k in range(2)], step)
    return x


class Shape:
    def __init__(self, band_rows, columns, nr, width, out, pieces):
        self.band_rows, self.columns, self.nr, self.width, self.out = band_rows, columns, nr, width, out
        self.rows = band_rows * nr
        self.band, self.pixels = band_rows * columns, band_rows * columns * nr
        self.block = BLOCK_ROWS * columns
        self.blocks = self.rows // BLOCK_ROWS
        self.pieces = pieces
        self.quarter = out // 4

    def regions(self, dilation):
        cuts = sorted({0, min(dilation, self.rows), max(self.rows - dilation, 0), self.rows})
        for lo, hi in zip(cuts, cuts[1:]):
            yield lo, hi, [r for r in range(3) if 0 <= lo + (r - 1) * dilation and hi + (r - 1) * dilation <= self.rows]


ANY = pl.BlockSpec(memory_space=pl.ANY)
SMEM = pl.BlockSpec(memory_space=pltpu.SMEM)
VMEM = pl.BlockSpec(memory_space=pltpu.VMEM)
PARAMS = pltpu.CompilerParams(vmem_limit_bytes=58 * 2**20)
TINY = pltpu.CompilerParams(vmem_limit_bytes=8 * 2**20)
SMALL = pltpu.CompilerParams(vmem_limit_bytes=12 * 2**20)


LIGHT = pl.CostEstimate(flops=0, bytes_accessed=0, transcendentals=0)


def lanes_at(start, size=LANES):
    return pl.ds(pl.multiple_of(start, LANES), size)


def start_bands(shape, refs, scratch, sem, part):
    for k, ref in enumerate(refs):
        pltpu.make_async_copy(ref, scratch.at[pl.ds((part ^ k) * shape.band, shape.band), :], sem.at[k]).start()


def wait_bands(shape, refs, scratch, sem):
    for k, ref in enumerate(refs):
        pltpu.make_async_copy(ref, scratch.at[pl.ds(k * shape.band, shape.band), :], sem.at[k]).wait()


def split_features(shape, features, mask, c):
    tiles, n = shape.width // LANES, shape.nr // 2

    def kernel(info, x, mask_ref, *outs):
        valid = mask_ref[...].astype(jnp.bfloat16)
        for k, out in enumerate(outs):
            for q in range(n):
                for i in range(tiles):
                    at = (i * shape.nr + (info[0] ^ k) * n + q) * LANES
                    out[q, :, i * LANES : (i + 1) * LANES] = x[:, lanes_at(at)] * valid

    return pl.pallas_call(
        kernel,
        out_shape=[jax.ShapeDtypeStruct((n, shape.band, shape.width), jnp.bfloat16)] * 2,
        in_specs=[SMEM, VMEM, VMEM],
        out_specs=[VMEM] * 2,
        compiler_params=SMALL,
        cost_estimate=LIGHT,
        name="split_features",
    )(c.reshape(1), features, mask)


def join_features(shape, own, other, c, zl):
    tiles, n = shape.width // LANES, shape.nr // 2

    def kernel(info, *refs):
        for k, part in enumerate(refs[: 2 * n]):
            core, q = info[0] ^ (k // n), info[1] ^ (k % n)
            for i in range(tiles):
                at = (i * shape.nr + core * n + q) * LANES
                refs[2 * n][:, lanes_at(at)] = part[:, i * LANES : (i + 1) * LANES]

    return pl.pallas_call(
        kernel,
        out_shape=jax.ShapeDtypeStruct((shape.band, shape.width * shape.nr), jnp.bfloat16),
        in_specs=[SMEM] + [VMEM] * shape.nr,
        out_specs=VMEM,
        compiler_params=SMALL,
        cost_estimate=LIGHT,
        name="join_features",
    )(jnp.stack([c, zl]).astype(jnp.int32), *own, *other)


def packed_near(shape, zl, own, neighbour):
    size = shape.quarter

    def kernel(info, own, neighbour, out, rest):
        for kl, ref in enumerate((own, neighbour)):
            out[:, pl.ds(pl.multiple_of((info[0] ^ kl) * size, size), size), :] = ref[...]
        rest[: SLOTS - FIRST] = own[FIRST:]
        rest[SLOTS - FIRST :] = neighbour[...]

    return pl.pallas_call(
        kernel,
        out_shape=[
            jax.ShapeDtypeStruct((SLOTS, 2 * size, LANES), jnp.bfloat16),
            jax.ShapeDtypeStruct((2 * SLOTS - FIRST, size, LANES), jnp.bfloat16),
        ],
        in_specs=[SMEM, VMEM, VMEM],
        out_specs=[VMEM, VMEM],
        compiler_params=SMALL,
        cost_estimate=LIGHT,
        name="packed_near",
    )(zl.reshape(1), own, neighbour)


def packed_far(shape, zl, first, rest):
    size = shape.quarter

    def kernel(info, first, rest, out):
        for kl in range(2):
            columns = pl.ds(pl.multiple_of((info[0] ^ kl) * size, size), size)
            if kl == 0:
                out[:FIRST, columns, :] = first[...]
                out[FIRST:, columns, :] = rest[: SLOTS - FIRST]
            else:
                out[:, columns, :] = rest[SLOTS - FIRST :]

    return pl.pallas_call(
        kernel,
        out_shape=jax.ShapeDtypeStruct((SLOTS, 2 * size, LANES), jnp.bfloat16),
        in_specs=[SMEM, VMEM, VMEM],
        out_specs=VMEM,
        compiler_params=SMALL,
        cost_estimate=LIGHT,
        name="packed_far",
    )(zl.reshape(1), first, rest)


def chip_slot(t, c):
    return jnp.where(jnp.where(c == 0, t < FULL, t >= SHORT), t - SHORT * c, FULL + 2 + t - FULL * (1 - c))


def assembled_weights(shape, info, own, by_x, by_y, diagonal):
    def kernel(info, *refs):
        ins, out, sem = refs[:5], refs[5], refs[6]
        m, c = info[0], info[1]

        def copy(ref, slot, tap, lane):
            pltpu.make_async_copy(ref.at[slot], out.at[tap, :, lanes_at(lane)], sem).start()

        def place(rel, slot, tap, lane):
            if rel < 3:
                copy(ins[rel], slot, tap, lane)
            else:

                @pl.when(slot < CUT)
                def _():
                    copy(ins[3], slot, tap, lane)

                @pl.when(slot >= CUT)
                def _():
                    copy(ins[4], slot - CUT, tap, lane)

        for rel in range(4):
            chip = m ^ rel

            def body(t, carry):
                v = chip * PER_CHIP + t
                place(rel, chip_slot(t, c), v // 4, (v % 4) * LANES)
                return carry

            lax.fori_loop(0, PER_CHIP, body, 0)
            for extra in range(2):
                place(rel, FULL + extra, 27 + extra, chip * LANES)
        pltpu.make_async_copy(out, out, sem).wait()

    return pl.pallas_call(
        kernel,
        out_shape=jax.ShapeDtypeStruct((29, shape.out // 2, shape.width), jnp.bfloat16),
        in_specs=[SMEM] + [ANY] * 5,
        out_specs=VMEM,
        scratch_shapes=[pltpu.SemaphoreType.DMA],
        compiler_params=TINY,
        cost_estimate=LIGHT,
        name="assembled_weights",
    )(info, own, by_x, by_y, *diagonal)


def shifted(values, by, columns):
    if by == 0:
        return values
    pixels = values.shape[0]
    source = lax.broadcasted_iota(jnp.int32, (pixels, 1), 0) % columns - by
    return jnp.where((source >= 0) & (source < columns), pltpu.roll(values, by % pixels, 0), 0.0)


def send_halves(shape, c, kept, low, outs, sem):
    half = shape.pixels // 2
    copies = []
    for n, (source, core) in enumerate(((kept, c), (low, 1 - c))):
        rows = source.at[pl.ds(pl.multiple_of(core * half, half), half)]
        copies.append(pltpu.make_async_copy(rows, outs[n], sem.at[n]))
    for copy in copies:
        copy.start()
    for copy in copies:
        copy.wait()


def half_shapes(shape, n):
    half = shape.pixels // 2
    return [
        jax.ShapeDtypeStruct((half, n * shape.out), jnp.float32),
        jax.ShapeDtypeStruct((half, n * shape.out), jnp.bfloat16),
    ]


def start_taps(weights, scratch, sem, taps, zh):
    half = weights[0].shape[1]
    for n, tap in enumerate(taps):
        for kh, ref in enumerate(weights):
            columns = pl.ds(pl.multiple_of((zh ^ kh) * half, half), half)
            pltpu.make_async_copy(ref.at[tap], scratch.at[n, columns], sem.at[n]).start()


def wait_taps(scratch, sem, some):
    for n in some:
        pltpu.make_async_copy(scratch.at[n], scratch.at[n], sem.at[n]).wait()


def dilated_products(shape, branch, x, w, first, y):
    dilation, columns = dilations[branch], shape.columns
    for s in range(3):
        for lo, hi, rs in shape.regions(dilation):
            pixels = jnp.concatenate(
                [x[(lo + (r - 1) * dilation) * columns : (hi + (r - 1) * dilation) * columns, :] for r in rs], axis=1
            )
            taps = jnp.concatenate([w[first + 3 * s + r] for r in rs], axis=1)
            y[s, lo * columns : hi * columns, :] = dot(pixels, taps, NT)


def put_dilated(shape, branch, y, kept, low, lane):
    dilation, columns = dilations[branch], shape.columns
    for blk in range(shape.blocks):
        at = slice(blk * shape.block, (blk + 1) * shape.block)
        z = y[1, at, :] + shifted(y[0, at, :], dilation, columns) + shifted(y[2, at, :], -dilation, columns)
        kept[at, lane : lane + shape.out] = z
        low[at, lane : lane + shape.out] = z.astype(jnp.bfloat16)


def taps_of(branch):
    return [9 * branch + 3 * r + s for s in range(3) for r in range(3)]


def branch_sums(shape, info, area, bands, weights):
    nr = shape.nr

    def kernel(info, area, *refs):
        ins, weights = refs[:nr], refs[nr : nr + 2]
        keep, sent, pooled, lifted, x, w, y, kept, low_sums, band_sem, w_sem, out_sem = refs[nr + 2 :]
        start_bands(shape, ins, x, band_sem, info[5])
        start_taps(weights, w, w_sem, taps_of(2) + taps_of(1) + taps_of(0) + [27, 28], info[2])
        wait_bands(shape, ins, x, band_sem)
        wait_taps(w, w_sem, range(29))
        for n, branch in enumerate((2, 1, 0)):
            dilated_products(shape, branch, x, w, 9 * n, y.at[n % 2])
            put_dilated(shape, branch, y.at[n % 2], kept, low_sums, n * shape.out)
        z = dot(x[...], w[27], NT)
        kept[:, 3 * shape.out :] = z
        low_sums[:, 3 * shape.out :] = z.astype(jnp.bfloat16)
        sums = jnp.zeros((1, shape.width), jnp.float32)
        for blk in range(shape.blocks):
            values = x[blk * shape.block : (blk + 1) * shape.block, :]
            sums = sums + jnp.sum(values.astype(jnp.float32), axis=0, keepdims=True)
        low = jnp.broadcast_to(sums / area[0], pooled.shape).astype(jnp.bfloat16)
        first = lax.broadcasted_iota(jnp.int32, pooled.shape, 0) == 0
        pooled[...] = jnp.where(first, low.astype(jnp.float32), 0.0).astype(jnp.bfloat16)
        lifted[...] = dot(pooled[...], w[28], NT)
        send_halves(shape, info[1], kept, low_sums, (keep, sent), out_sem)

    return pl.pallas_call(
        kernel,
        out_shape=half_shapes(shape, 4)
        + [jax.ShapeDtypeStruct((16, shape.width), jnp.bfloat16), jax.ShapeDtypeStruct((16, shape.out), jnp.float32)],
        in_specs=[SMEM, SMEM] + [ANY] * (nr + 2),
        out_specs=[ANY] * 2 + [VMEM] * 2,
        scratch_shapes=[
            pltpu.VMEM((shape.pixels, shape.width), jnp.bfloat16),
            pltpu.VMEM((29, shape.out, shape.width), jnp.bfloat16),
            pltpu.VMEM((2, 3, shape.pixels, shape.out), jnp.float32),
            pltpu.VMEM((shape.pixels, 4 * shape.out), jnp.float32),
            pltpu.VMEM((shape.pixels, 4 * shape.out), jnp.bfloat16),
            pltpu.SemaphoreType.DMA((nr,)),
            pltpu.SemaphoreType.DMA((29,)),
            pltpu.SemaphoreType.DMA((2,)),
        ],
        compiler_params=PARAMS,
        cost_estimate=LIGHT,
        name="branch_sums",
    )(info, area, *bands, *weights)


def band_mask(shape, info):
    pixel = lax.broadcasted_iota(jnp.int32, (shape.band, 1), 0)
    row, column = info[4] * shape.band_rows + pixel // shape.columns, pixel % shape.columns
    return ((row < info[6]) & (column < info[7])).astype(jnp.float32)


def put_moments(values, mask, ref, at_sum, at_square, count):
    total = jnp.sum(values * mask, axis=0, keepdims=True)
    centred = (values - total / jnp.maximum(count, 1.0)) * mask
    ref[at_sum : at_sum + 1, :] = total
    ref[at_square : at_square + 1, :] = jnp.sum(centred * centred, axis=0, keepdims=True)


def merged_rows(refs, k, n):
    count = tree([ref[2 * n : 2 * n + 1, :] for ref in refs])
    mean = tree([ref[k : k + 1, :] for ref in refs]) / jnp.maximum(count, 1.0)
    between = []
    for ref in refs:
        own = ref[2 * n : 2 * n + 1, :]
        gap = ref[k : k + 1, :] / jnp.maximum(own, 1.0) - mean
        between.append(own * gap * gap)
    squares = tree([ref[n + k : n + k + 1, :] for ref in refs]) + tree(between)
    return mean, squares / count, count


def silu(v):
    return v * jax.nn.sigmoid(v)


def call(shape, kernel, name, outs, out_specs, in_specs, scratch=()):
    return pl.pallas_call(
        kernel,
        out_shape=[jax.ShapeDtypeStruct(*o) for o in outs],
        in_specs=in_specs,
        out_specs=out_specs,
        scratch_shapes=list(scratch),
        compiler_params=SMALL,
        cost_estimate=LIGHT,
        name=name,
    )


TABLE = 16


def branch_moments(shape, info, images, mine, others, lifted):
    n = len(others)

    def kernel(info, mine, lifted, *refs):
        others, (z, rows) = refs[:n], refs[n:]
        mask = band_mask(shape, info)
        count = jnp.sum(mask)
        rows[...] = jnp.zeros(rows.shape, jnp.float32)
        for k in range(4):
            lanes = slice((3 - k) * shape.out, (4 - k) * shape.out)
            value = mine[:, lanes]
            for other in others:
                value = value + other[:, lanes].astype(jnp.float32)
            z[:, k * shape.out : (k + 1) * shape.out] = value
            put_moments(value, mask, rows, k, 4 + k, count)
        rows[8:9, :] = jnp.full((1, shape.out), count, jnp.float32)
        rows[pl.ds(TABLE + 2 * info[0] + info[2], 1), :] = lifted[0:1, :]

    return call(
        shape,
        kernel,
        "branch_moments",
        [((shape.band, 4 * shape.out), jnp.float32), ((TABLE + images, shape.out), jnp.float32)],
        [VMEM] * 2,
        [SMEM] + [VMEM] * (2 + n),
    )(info, mine, lifted, *others)


def projected(shape, info, images, rows, z, projection, gain, bias):
    out = shape.out

    def kernel(info, z, projection, gain, bias, *refs):
        n = len(rows)
        rows_in, (concat, pre, moments, stats) = refs[:n], refs[n:]
        mask = band_mask(shape, info)
        pool = tree([ref[TABLE : TABLE + images, :] for ref in rows_in])
        pool = pool - jnp.sum(pool, axis=0, keepdims=True) / images
        pool_inv = lax.rsqrt(jnp.sum(pool * pool, axis=0, keepdims=True) / images + epsilon)
        pool = pool * pool_inv
        stats[9:10, :] = pool_inv
        stats[TABLE : TABLE + images, :] = pool
        stats[TABLE + images :, :] = gain[4:5, :] * pool + bias[4:5, :]
        for k in range(4):
            average, spread, count = merged_rows(rows_in, k, 4)
            inv = lax.rsqrt(spread + epsilon)
            stats[k : k + 1, :] = average
            stats[4 + k : 5 + k, :] = inv
            lanes = slice(k * out, (k + 1) * out)
            lifted = gain[k : k + 1, :] * ((z[:, lanes] - average) * inv) + bias[k : k + 1, :]
            concat[:, lanes] = (silu(lifted) * mask).astype(jnp.bfloat16)
        stats[8:9, :] = count
        line = stats[pl.ds(TABLE + images + 2 * info[0] + info[2], 1), :]
        concat[:, 4 * out :] = (silu(line) * mask).astype(jnp.bfloat16)
        value = dot(concat[...], projection[...], NT)
        pre[...] = value
        local = jnp.sum(mask)
        put_moments(value, mask, moments, 0, 1, local)
        moments[2:, :] = jnp.full((6, out), local, jnp.float32)

    return call(
        shape,
        kernel,
        "projected",
        [
            ((shape.band, 5 * out), jnp.bfloat16),
            ((shape.band, out), jnp.float32),
            ((8, out), jnp.float32),
            ((TABLE + 2 * images, out), jnp.float32),
        ],
        [VMEM] * 4,
        [SMEM] + [VMEM] * (4 + len(rows)),
    )(info, z, projection, gain, bias, *rows)


def branch_gradients(shape, info, images, rows, upstream, normed, inv, z, stats, projection, gain, bias):
    out = shape.out

    def kernel(info, upstream, normed, inv, z, stats, projection, gain, bias, *refs):
        n = len(rows)
        rows_in, (delta, up, sums, totals) = refs[:n], refs[n:]
        mask = band_mask(shape, info)
        whole = tree([ref[...] for ref in rows_in])
        totals[...] = whole
        count, scale = stats[8:9, :], gain[5:6, :]
        low = (
            mask
            * inv[...]
            * (scale * upstream[...] - scale * whole[1:2] / count - normed[...] * scale * whole[0:1] / count)
        ).astype(jnp.bfloat16)
        delta[...] = low
        sums[...] = jnp.zeros(sums.shape, jnp.float32)
        for k in range(4):
            lanes = slice(k * out, (k + 1) * out)
            at = (z[:, lanes] - stats[k : k + 1, :]) * stats[4 + k : 5 + k, :]
            slope = silu_slope(gain[k : k + 1, :] * at + bias[k : k + 1, :])
            value = dot(low, projection[:, lanes], NN) * mask * slope
            up[:, lanes] = value
            sums[k : k + 1, :] = jnp.sum(value * at, axis=0, keepdims=True)
            sums[4 + k : 5 + k, :] = jnp.sum(value, axis=0, keepdims=True)
        line = jnp.sum(dot(low, projection[:, 4 * out :], NN) * mask, axis=0, keepdims=True)
        sums[pl.ds(8 + 2 * info[0] + info[2], 1), :] = line

    return call(
        shape,
        kernel,
        "branch_gradients",
        [
            ((shape.band, out), jnp.bfloat16),
            ((shape.band, 4 * out), jnp.float32),
            ((8 + images, out), jnp.float32),
            ((8, out), jnp.float32),
        ],
        [VMEM] * 4,
        [SMEM] + [VMEM] * (8 + len(rows)),
    )(info, upstream, normed, inv, z, stats, projection, gain, bias, *rows)


def branch_deltas(shape, info, rows, up, z, stats, gain):
    out, half = shape.out, shape.out // 2

    def kernel(info, up, z, stats, gain, *refs):
        n = len(rows)
        rows_in, (delta, crossing, totals) = refs[:n], refs[n:]
        mask = band_mask(shape, info)
        totals[...] = tree([ref[...] for ref in rows_in])
        count = stats[8:9, :]
        for k in range(4):
            lanes = slice(k * out, (k + 1) * out)
            inv, scale = stats[4 + k : 5 + k, :], gain[k : k + 1, :]
            at = (z[:, lanes] - stats[k : k + 1, :]) * inv
            by_gain, by_bias = totals[k : k + 1, :], totals[4 + k : 5 + k, :]
            value = mask * inv * (scale * up[:, lanes] - scale * by_bias / count - at * scale * by_gain / count)
            delta[:, lanes] = value.astype(jnp.bfloat16)
            crossing[:, k * half : (k + 1) * half] = delta[:, lanes_at(k * out + (1 - info[2]) * half, half)]

    return call(
        shape,
        kernel,
        "branch_deltas",
        [
            ((shape.band, 4 * out), jnp.bfloat16),
            ((shape.band, 4 * half), jnp.bfloat16),
            (rows[0].shape, jnp.float32),
        ],
        [VMEM] * 3,
        [SMEM] + [VMEM] * (4 + len(rows)),
    )(info, up, z, stats, gain, *rows)


def moved_columns(shape, delta, lane, lanes, branch, moved):
    for blk in range(shape.blocks):
        at = slice(blk * shape.block, (blk + 1) * shape.block)
        values = delta[at, lanes_at(lane, lanes)].astype(jnp.float32)
        for s in range(3):
            moved[at, s * lanes : (s + 1) * lanes] = shifted(
                values, (s - 1) * dilations[branch], shape.columns
            ).astype(jnp.bfloat16)


def input_gradient(shape, info, area, deltas, pool_delta, weights):
    nr, columns = shape.nr, shape.columns

    def kernel(info, area, *refs):
        ins, pool_delta, weights = refs[:nr], refs[nr], refs[nr + 1 : nr + 3]
        outs = refs[nr + 3 : 2 * nr + 3]
        delta, moved, w, acc, delta_sem, w_sem = refs[2 * nr + 3 :]
        start_bands(shape, ins, delta, delta_sem, info[4])
        start_taps(weights, w, w_sem, range(29), info[2])
        wait_bands(shape, ins, delta, delta_sem)
        wait_taps(w, w_sem, range(29))
        pool = dot(pool_delta[...], w[28], NN)[0:1] / area[0]
        acc[...] = dot(delta[:, : shape.out], w[27], NN) + pool
        for branch in range(3):
            dilation = dilations[branch]
            moved_columns(shape, delta, (branch + 1) * shape.out, shape.out, branch, moved)
            for lo, hi, rs in shape.regions(dilation):
                rows = [2 - r for r in rs]
                cut = lambda r: moved[(lo - (r - 1) * dilation) * columns : (hi - (r - 1) * dilation) * columns, :]
                pixels = jnp.concatenate([cut(r) for r in rows], axis=1)
                taps = jnp.concatenate([w[9 * branch + 3 * r + s] for r in rows for s in range(3)], axis=0)
                acc[lo * columns : hi * columns, :] += dot(pixels, taps, NN)
        pixel = lax.broadcasted_iota(jnp.int32, (shape.band, 1), 0)
        for k in range(nr):
            first = (info[5] ^ k) * shape.band
            inside = ((pixel + first) // columns < info[6]) & (pixel % columns < info[7])
            values = acc[pl.ds(pl.multiple_of(first, shape.band), shape.band), :]
            outs[k][...] = jnp.where(inside, values, 0.0).astype(jnp.bfloat16)

    return pl.pallas_call(
        kernel,
        out_shape=[jax.ShapeDtypeStruct((shape.band, shape.width), jnp.bfloat16)] * nr,
        in_specs=[SMEM, SMEM] + [ANY] * nr + [VMEM] + [ANY] * 2,
        out_specs=[VMEM] * nr,
        scratch_shapes=[
            pltpu.VMEM((shape.pixels, 4 * shape.out), jnp.bfloat16),
            pltpu.VMEM((shape.pixels, 3 * shape.out), jnp.bfloat16),
            pltpu.VMEM((29, shape.out, shape.width), jnp.bfloat16),
            pltpu.VMEM((shape.pixels, shape.width), jnp.float32),
            pltpu.SemaphoreType.DMA((nr,)),
            pltpu.SemaphoreType.DMA((29,)),
        ],
        compiler_params=PARAMS,
        cost_estimate=pl.CostEstimate(
            flops=44 * shape.pixels * shape.width * shape.out, bytes_accessed=2**24, transcendentals=0
        ),
        name="input_gradient",
    )(info, area, *deltas, pool_delta, *weights)


def weight_gradients(shape, info, bands, far_bands, deltas, far_deltas, pool_deltas, pooled):
    nr, columns, half = shape.nr, shape.columns, shape.out // 2
    n_outs = 8 if shape.pieces else 1
    by_rows = lambda v: v.reshape(v.shape[0] // columns, columns, v.shape[1])
    bands = [by_rows(band) for band in [*bands, *far_bands]]

    def kernel(info, *refs):
        ins, delta_ins, far_delta_ins = (refs[n * nr : (n + 1) * nr] for n in range(3))
        far_ins, refs = refs[3 * nr : 4 * nr], refs[4 * nr :]
        pool_deltas, pooled, outs = refs[0], refs[1], refs[2 : 2 + n_outs]
        x, delta, far_delta, moved, grads, sem, out_sem = refs[2 + n_outs :]
        m, c, zh, part, z = info[0], info[1], info[2], info[4], info[5]
        rows = shape.band_rows
        start_bands(shape, delta_ins, delta, sem.at[0], part)
        start_bands(shape, far_delta_ins, far_delta, sem.at[1], part)
        for image, sources in enumerate((ins, far_ins)):
            for k, ref in enumerate(sources):
                pltpu.make_async_copy(ref, x.at[pl.ds((z ^ k) * rows, rows), image], sem.at[2 + image, k]).start()

        def arrive(n):
            for k in range(nr):
                if n < 2:
                    some = (delta, far_delta)[n].at[pl.ds(k * shape.band, shape.band)]
                else:
                    some = x.at[pl.ds(k * rows, rows), n - 2]
                pltpu.make_async_copy(some, some, sem.at[n, k]).wait()

        def move(branch):
            for image, source in enumerate((delta, far_delta)):
                lane = (branch + 1) * half if image else (branch + 1) * shape.out + zh * half
                for blk in range(shape.blocks):
                    at = slice(blk * shape.block, (blk + 1) * shape.block)
                    values = source[at, lanes_at(lane, half)].astype(jnp.float32)
                    for s in range(3):
                        value = shifted(values, (s - 1) * dilations[branch], columns).astype(jnp.bfloat16)
                        moved[blk * BLOCK_ROWS : (blk + 1) * BLOCK_ROWS, image, :, s * half : (s + 1) * half] = (
                            value.reshape(BLOCK_ROWS, columns, half)
                        )

        flat = lambda v: v.reshape(-1, v.shape[-1])

        def put(tap, value):
            value = value.astype(jnp.bfloat16)
            if not shape.pieces:
                grads[tap] = value
                return
            for i in range(4):
                if tap < 27:
                    v = 4 * tap + i
                    chip, slot = v // PER_CHIP, chip_slot(v % PER_CHIP, c)
                else:
                    chip, slot = i, FULL + tap - 27
                for q in range(2):
                    rows = slice(q * shape.quarter, (q + 1) * shape.quarter)
                    grads[2 * (m ^ chip) + q, slot] = value[rows, i * LANES : (i + 1) * LANES]

        arrive(0)
        arrive(1)
        for branch in range(3):
            move(branch)
            if branch == 0:
                arrive(2)
                arrive(3)
            dilation = dilations[branch]
            for r in range(3):
                up, down = max(0, 1 - r) * dilation, max(0, r - 1) * dilation
                to = flat(moved[up : shape.rows - down])
                value = dot(to, flat(x[down : shape.rows - up]), TN)
                for s in range(3):
                    put(9 * branch + 3 * r + s, value[s * half : (s + 1) * half])
        one = jnp.concatenate(
            [
                delta[:, lanes_at(zh * half, half)].reshape(shape.rows, 1, columns, half),
                far_delta[:, :half].reshape(shape.rows, 1, columns, half),
            ],
            axis=1,
        )
        put(27, dot(flat(one), flat(x[...]), TN))
        put(28, dot(pool_deltas[...], pooled[...], TN))
        copies = [pltpu.make_async_copy(grads.at[n] if shape.pieces else grads, outs[n], out_sem.at[n]) for n in range(n_outs)]
        for copy in copies:
            copy.start()
        for copy in copies:
            copy.wait()

    if shape.pieces:
        out_shape = [jax.ShapeDtypeStruct((SLOTS, shape.quarter, LANES), jnp.bfloat16)] * 8
        grads_shape = (8, SLOTS, shape.quarter, LANES)
    else:
        out_shape = [jax.ShapeDtypeStruct((29, half, shape.width), jnp.bfloat16)]
        grads_shape = (29, half, shape.width)
    return pl.pallas_call(
        kernel,
        out_shape=out_shape,
        in_specs=[SMEM] + [ANY] * (4 * nr) + [VMEM] * 2,
        out_specs=[ANY] * n_outs,
        scratch_shapes=[
            pltpu.VMEM((shape.rows, 2, columns, shape.width), jnp.bfloat16),
            pltpu.VMEM((shape.pixels, 4 * shape.out), jnp.bfloat16),
            pltpu.VMEM((shape.pixels, 2 * shape.out), jnp.bfloat16),
            pltpu.VMEM((shape.rows, 2, columns, 3 * half), jnp.bfloat16),
            pltpu.VMEM(grads_shape, jnp.bfloat16),
            pltpu.SemaphoreType.DMA((4, nr)),
            pltpu.SemaphoreType.DMA((n_outs,)),
        ],
        compiler_params=PARAMS,
        cost_estimate=pl.CostEstimate(
            flops=44 * shape.pixels * shape.width * shape.out, bytes_accessed=2**24, transcendentals=0
        ),
        name="weight_gradients",
    )(info, *bands[:nr], *deltas, *far_deltas, *bands[nr:], pool_deltas, pooled)


def valid_pixels(extent, first_row, rows, columns):
    r = first_row + lax.broadcasted_iota(jnp.int32, (rows, columns), 0)
    w = lax.broadcasted_iota(jnp.int32, (rows, columns), 1)
    return ((r < extent[0]) & (w < extent[1])).astype(jnp.float32).reshape(rows * columns, 1)


def to_logical(place, x):
    return jnp.where(place.zh == place.c, x, place.swap(x, c=1, zh=1))


def on_device(
    features, extent, pointwise_weight, pooling_weight, dilated_weight, projection_weight, norm_gain, norm_bias, cotangent
):
    place = Place()
    nr, nzl = place.nr, place.nzl
    _, band_rows, columns, channels = features.shape
    width, out = channels // nr, norm_gain.shape[1]
    band = band_rows * columns
    pieces = nr == 4 and place.nd == 8 and dilated_weight.shape[0] == 2 * PER_CHIP * LANES
    shape = Shape(band_rows, columns, nr, width, out, pieces)
    images = place.nd

    partner = place.swap(extent, c=1)
    extent_here = jnp.where(place.zh == place.c, extent, partner)[0]
    area = (extent_here[0] * extent_here[1]).astype(jnp.float32)
    mask = valid_pixels(extent_here, place.part * band_rows, band_rows, columns)
    own_mask = valid_pixels(extent[0], place.z * band_rows, band_rows, columns)
    here_now = [place.m, place.c, place.zh, place.zl, place.part, place.z, extent_here[0], extent_here[1]]
    info = jnp.stack(here_now).astype(jnp.int32)
    areas = area.reshape(1)

    own_parts, other_parts = split_features(shape, features.reshape(band, channels), own_mask, place.c)
    held = by_xor([own_parts, place.swap(other_parts, c=1)], place.c)
    held = [by_xor([v[q] for q in range(nzl)], place.zl) for v in by_xor(held, place.zh)]

    def sent(image, k, first=()):
        kh, kl = divmod(k, nzl)
        v = held[kh ^ image][kl]
        return place.swap(after(v, first), zh=kh, zl=kl) if k else v

    steps = doubling(place)
    nd_bits = (place.nd // 2).bit_length() - 1
    projection = projection_weight.T
    if pieces:
        sources = line_pieces(place, dilated_weight, pointwise_weight, pooling_weight)
        crossed = place.swap(sources[0][:FIRST], zh=1)
        neighbour = after(place.swap(sources[1], zl=1), crossed, own_parts, other_parts, partner)
        near, rest = packed_near(shape, place.zl, sources[0], neighbour)
        rest = place.swap(rest, zh=1)
        near_x, near_y = plane_direct(place, near)
        near_d = plane_diagonal(place, near_x, near_y)
        far = packed_far(shape, place.zl, crossed, after(rest, near_d, held))
        crossing_band = sent(0, nzl, first=far)
        far_x, far_y = after(plane_direct(place, far), crossing_band)
        far_d = plane_diagonal(place, far_x, far_y)
        bands = [sent(0, k, first=far_x) for k in range(nzl)] + [crossing_band]
        bands += [sent(0, k, first=crossing_band) for k in range(nzl + 1, nr)]
        near = assembled_weights(shape, info, near, near_x, near_y, near_d)
        weights = [near, assembled_weights(shape, info, far, far_x, far_y, after(far_d, near))]
    else:
        bands = [sent(0, k) for k in range(nr)]
        weights = gathered_tiles(place, dilated_weight, pointwise_weight, pooling_weight)
        weights = by_xor([weights[:, : out // 2], weights[:, out // 2 :]], place.zh)

    def given_on(keep, got):
        bands_of = lambda v: v.reshape(nzl, band, v.shape[1])
        at = lambda k: [lax.dynamic_index_in_dim(bands_of(v), place.zl ^ k, 0, keepdims=False) for v in (keep, got)]
        summed = lambda k: at(k)[0] + at(k)[1].astype(jnp.float32)
        return summed(0), [place.swap(summed(k).astype(jnp.bfloat16), zl=k) for k in range(1, nzl)]

    ready = (bands, weights)
    keep, given, pooled, lifted = branch_sums(shape, info, areas, bands, weights)
    far_bands = [sent(1, k, first=ready) for k in range(nzl + 1)]
    projection = after(projection, ready)
    for step in steps[: -nd_bits - 2]:
        projection = joined(place, projection, step)
    given = after(given, far_bands, projection)
    projection = joined(place, after(projection, given), steps[-nd_bits - 2])
    got, projection = after((place.swap(given, c=1), projection), projection)
    projection = joined(place, projection, steps[-nd_bits - 1])
    upstream_low = to_logical(place, after(cotangent.reshape(band, out), got))
    plane = [projection] + [place.swap(projection, m=k) for k in range(1, images // 2)]
    mine, others = given_on(keep, got)
    mine, others = after((mine, others), plane, upstream_low)
    z, rows = branch_moments(shape, info, images, mine, others, lifted)
    projection = jnp.stack(by_xor(plane, place.m))
    projection = projection.reshape((place.nd, nr) + projection_weight.shape[::-1])
    projection = jnp.transpose(projection, (1, 2, 0, 3)).reshape(out, -1)
    rows = exchanged(place, rows, lambda xs: merged(xs, 4))
    concat, proj_pre, rows, stats = projected(shape, info, images, rows, z, projection, norm_gain, norm_bias)
    pooled_far = place.swap(pooled, zh=1)
    rows = merged(exchanged(place, rows, lambda xs: merged(xs, 1)), 1)
    proj_average, proj_spread = rows[0:1] / rows[2:3], rows[1:2] / rows[2:3]
    proj_inv = lax.rsqrt(proj_spread + epsilon)
    proj_normed = (proj_pre - proj_average) * proj_inv
    proj_lift = norm_gain[5:6] * proj_normed + norm_bias[5:6]
    output_here = (jax.nn.silu(proj_lift) * mask).astype(jnp.bfloat16)

    upstream = upstream_low.astype(jnp.float32) * mask * silu_slope(proj_lift)
    sums = [jnp.sum(upstream * proj_normed, axis=0, keepdims=True), jnp.sum(upstream, axis=0, keepdims=True)]
    rows = exchanged(place, jnp.concatenate(sums + [jnp.zeros((6, out), jnp.float32)], axis=0), tree)
    proj_delta, branch_up, rows, proj_totals = branch_gradients(
        shape, info, images, rows, upstream, proj_normed, proj_inv, z, stats, projection, norm_gain, norm_bias
    )
    projection_partial = lambda first: dot(after(proj_delta, first), concat, TN)
    rows = exchanged(place, rows, tree)
    delta, crossing, totals = branch_deltas(shape, info, after(rows, pooled_far), branch_up, z, stats, norm_gain)
    proj_gain_grad, proj_bias_grad = proj_totals[0:1], proj_totals[1:2]
    branch_gain_grad, branch_bias_grad = totals[:4], totals[4:8]
    pool_inv, pool_normed, pool_lift = stats[9:10], stats[TABLE : TABLE + images], stats[TABLE + images :]
    here = lambda rows: lax.dynamic_slice_in_dim(rows, place.image, 1, axis=0)
    pool_up = totals[8:] * silu_slope(pool_lift)
    pool_gain_grad = jnp.sum(pool_up * pool_normed, axis=0, keepdims=True)
    pool_bias_grad = jnp.sum(pool_up, axis=0, keepdims=True)
    pool_deltas = pool_inv * (
        norm_gain[4:5] * pool_up
        - norm_gain[4:5] * pool_bias_grad / images
        - pool_normed * norm_gain[4:5] * pool_gain_grad / images
    )
    low_rows = lambda rows: jnp.pad(rows, ((0, 16 - rows.shape[0]), (0, 0))).astype(jnp.bfloat16)
    pool_pair = lax.dynamic_slice_in_dim(pool_deltas, 2 * place.m, 2, axis=0)
    halves = lambda v, n: by_xor([v[:, n * out : n * out + out // 2], v[:, n * out + out // 2 : (n + 1) * out]], place.zh)
    def over_group(v, first):
        near = [v] + [after(place.swap(v, zl=k), first) for k in range(1, nzl)]
        return near + [place.swap(n, c=1) for n in near]

    crossing = place.swap(crossing, zh=1)
    rows = projection_weight.shape[0]
    part = projection_partial(delta).astype(jnp.bfloat16).reshape(out, images // 2, 2, rows)
    part = jnp.transpose(part, (2, 1, 0, 3)).reshape(2, images // 2, 2, nzl, out // nr, rows)
    part = halved(place, [part[k] for k in range(2)], steps[-nd_bits - 1])
    spread_deltas = over_group(delta, (crossing, part))
    part = m_halved(place, after(part, spread_deltas), steps, 1)
    far_deltas = [crossing] + [place.swap(crossing, zl=k) for k in range(1, nzl)]
    inputs = input_gradient(shape, info, areas, spread_deltas, low_rows(here(pool_deltas)), weights)

    far_bands += [sent(1, k, first=spread_deltas) for k in range(nzl + 1, nr)]
    crossing = after(far_deltas, inputs, far_bands)
    pooled_pair = pooled + jnp.roll(pooled_far, 1, axis=0)
    pool_pair = jnp.concatenate([pool_pair[i : i + 1] for i in range(2)], axis=0)
    pool_pair = jnp.concatenate(by_xor([pool_pair[0:1], pool_pair[1:2]], place.zh), axis=0)
    pool_pair = halves(low_rows(pool_pair), 0)[0]
    far_deltas = crossing + [place.swap(n, c=1) for n in crossing]
    grads = weight_gradients(shape, info, bands, far_bands, spread_deltas, far_deltas, pool_pair, pooled_pair)

    done = (far_deltas, far_bands, part)
    handed = [place.swap(after(inputs[nzl + k], done), zh=1) for k in range(1, nzl)]
    near_handed = [place.swap(after(inputs[k], done), zl=k) for k in range(1, nzl)]
    output = to_logical(place, after(output_here, inputs))
    part = m_halved(place, after(part, inputs), steps, 2)
    crossed = (handed, near_handed, output, part)
    if pieces:
        pairs = [[grads[2 * rel], grads[2 * rel + 1]] for rel in range(4)]
        first_d, second_d = plane_scatter_diagonal(place, pairs)
        first_d, second_d = after((first_d, second_d), crossed, part)
        quarters = plane_scatter(place, pairs, first_d, second_d)
    else:
        quarters = grads
    part, last = after((part, inputs[nzl]), crossed)
    part = part.reshape((2, nzl) + part.shape[-2:])
    part = halved(place, [part[k] for k in range(2)], steps[-nd_bits - 2])
    last = place.swap(last, zh=1)
    handed = [place.swap(after(handed[k - 1], near_handed), zl=k) for k in range(1, nzl)]
    returned = by_xor([[inputs[0]] + near_handed, [last] + handed], place.zh)
    quarters = after(quarters, part, output, returned)
    returned = by_xor(returned, place.c)
    traded = place.swap(jnp.stack(returned[1]), c=1)
    feature_gradient = join_features(shape, returned[0], [traded[k] for k in range(nzl)], place.c, place.zl)
    if pieces:
        dilated_gradient, pointwise_gradient, pooling_gradient = line_back(place, quarters, feature_gradient)
    else:
        dilated_gradient, pointwise_gradient, pooling_gradient = scattered_tiles(place, quarters[0])
    part = after(part, feature_gradient)
    for step in [step for step in steps if "zl" in step[0]]:
        part = part.reshape((-1, 2) + part.shape[-2:])
        part = halved(place, [part[:, k] for k in range(2)], step)
    projection_gradient = part.reshape(out // nr, rows).astype(jnp.float32).T

    return (
        output.reshape(cotangent.shape),
        feature_gradient.reshape(features.shape),
        pointwise_gradient,
        pooling_gradient,
        dilated_gradient,
        projection_gradient,
        jnp.concatenate([branch_gain_grad, pool_gain_grad, proj_gain_grad], axis=0),
        jnp.concatenate([branch_bias_grad, pool_bias_grad, proj_bias_grad], axis=0),
    )


def solution(mesh):
    banded = P("dp", "rows", None, None)
    blocks = P("dp", "rows")
    return jax.shard_map(
        on_device,
        mesh=mesh,
        in_specs=(banded, P("dp", None), blocks, blocks, blocks, blocks, P(), P(), banded),
        out_specs=(banded, banded, blocks, blocks, blocks, blocks, P(), P()),
        check_vma=False,
    )
```

```python
import jax
import jax.numpy as jnp
from jax import lax
from jax.experimental import pallas as pl
from jax.experimental.pallas import tpu as pltpu
from jax.sharding import PartitionSpec as P

epsilon = 1e-05
dilations = (6, 12, 18)
LANES = 128
BLOCK_ROWS = 6
AXES = ("dp", "rows")
FULL, SHORT, PER_CHIP = 14, 13, 27
SLOTS = FULL + 2 + SHORT
FIRST = 16
CUT = 15
NT = (((1,), (1,)), ((), ()))
TN = (((0,), (0,)), ((), ()))
NN = (((1,), (0,)), ((), ()))


def dot(first, second, dims):
    return lax.dot_general(first, second, dims, preferred_element_type=jnp.float32)


def after(x, *first):
    return lax.optimization_barrier((x, first))[0]


def silu_slope(values):
    sigma = jax.nn.sigmoid(values)
    return sigma * (1.0 + values * (1.0 - sigma))


class Place:
    def __init__(self):
        self.nd, self.nr = lax.axis_size("dp"), lax.axis_size("rows")
        self.nzl = self.nr // 2
        d, z = lax.axis_index("dp"), lax.axis_index("rows")
        self.d, self.z = d, z
        self.m, self.c = d // 2, d % 2
        self.zh, self.zl = z // self.nzl, z % self.nzl
        self.part = self.c * self.nzl + self.zl
        self.image = 2 * self.m + self.zh

    def swap(self, x, m=0, c=0, zh=0, zl=0):
        nzl = self.nzl
        pairs = []
        for flat in range(self.nd * self.nr):
            d, z = divmod(flat, self.nr)
            pairs.append((flat, (d ^ (2 * m + c)) * self.nr + (z ^ (zh * nzl + zl))))
        return lax.ppermute(x, AXES, pairs)


def by_xor(items, index):
    items = list(items)
    bit = 1
    while bit < len(items):
        flip = (index & bit) != 0
        pick = lambda a, b: jnp.where(flip, a, b)
        items = [jax.tree.map(pick, items[k ^ bit], items[k]) for k in range(len(items))]
        bit *= 2
    return items


def tree(items):
    items = list(items)
    while len(items) > 1:
        items = [items[i] + items[i + 1] for i in range(0, len(items), 2)]
    return items[0]


def exchange_stages(place):
    return (
        [dict(c=1)],
        [dict(m=k) for k in range(1, place.nd // 2)],
        [dict(zh=k // place.nzl, zl=k % place.nzl) for k in range(1, place.nr)],
    )


def total(place, x):
    for stage in exchange_stages(place):
        x = tree([x] + [place.swap(x, **s) for s in stage])
    return x


def merged(xs, k):
    whole = tree(xs)
    mean = whole[:k] / jnp.maximum(whole[2 * k : 2 * k + 1], 1.0)
    between = []
    for y in xs:
        own = y[2 * k : 2 * k + 1]
        gap = y[:k] / jnp.maximum(own, 1.0) - mean
        between.append(own * gap * gap)
    return jnp.concatenate([whole[:k], whole[k : 2 * k] + tree(between), whole[2 * k :]], axis=0)


def exchanged(place, x, combine):
    *stages, last = exchange_stages(place)
    for stage in stages:
        x = combine([x] + [place.swap(x, **s) for s in stage])
    return [x] + [place.swap(x, **s) for s in last]


def line_pieces(place, dilated, pointwise, pooling):
    tiles = lambda w: jnp.transpose(w.T.reshape(w.shape[1], w.shape[0] // LANES, LANES), (1, 0, 2))
    dil, one, pool = tiles(dilated), tiles(pointwise), tiles(pooling)
    other = [dil[2 + r :: 4][:SHORT] for r in range(2)]
    got = place.swap(jnp.concatenate(other, axis=0), c=1)
    same = [jnp.concatenate([dil[r::4][:FULL], one[r : r + 1], pool[r : r + 1]], axis=0) for r in range(2)]
    whole = [jnp.concatenate([same[r], got[r * SHORT : (r + 1) * SHORT]], axis=0) for r in range(2)]
    return by_xor(whole, place.zl)


def plane_direct(place, half):
    return place.swap(half, m=1), place.swap(half, m=2)


def plane_diagonal(place, by_x, by_y):
    return place.swap(by_x[:CUT], m=2), place.swap(by_y[CUT:], m=1)


def add_low(first, *others):
    out = first.astype(jnp.float32)
    for o in others:
        out = out + o.astype(jnp.float32)
    return out.astype(jnp.bfloat16)


def plane_scatter_diagonal(place, pieces):
    return place.swap(pieces[3][0], m=2), place.swap(pieces[3][1], m=1)


def plane_scatter(place, pieces, first_d, second_d):
    to_x = jnp.stack([add_low(pieces[1][0], first_d), pieces[1][1]])
    to_y = jnp.stack([pieces[2][0], add_low(pieces[2][1], second_d)])
    by_x, by_y = place.swap(to_x, m=1), place.swap(to_y, m=2)
    return [add_low(pieces[0][q], by_x[q], by_y[q]) for q in range(2)]


def line_back(place, quarters, first):
    by_kl = by_xor(quarters, place.zl)
    by_part = by_xor([by_kl[0], after(place.swap(by_kl[1], zl=1), first)], place.zl)
    same = [p[: FULL + 2] for p in by_part]
    got = place.swap(jnp.concatenate([p[FULL + 2 :] for p in by_part], axis=0), c=1)
    other = [got[r * SHORT : (r + 1) * SHORT] for r in range(2)]
    gap = jnp.zeros((FULL - SHORT,) + other[0].shape[1:], other[0].dtype)
    dil = jnp.stack([s[:FULL] for s in same] + [jnp.concatenate([o, gap], axis=0) for o in other], axis=1)
    dil = dil.reshape((4 * FULL,) + dil.shape[2:])[: 2 * PER_CHIP]
    rows = lambda t: jnp.transpose(t, (1, 0, 2)).reshape(t.shape[1], t.shape[0] * LANES).astype(jnp.float32).T
    one = jnp.stack([s[FULL] for s in same])
    pool = jnp.stack([s[FULL + 1] for s in same])
    return rows(dil), rows(one), rows(pool)


def gathered_tiles(place, dilated, pointwise, pooling):
    whole = []
    for w in (dilated, pointwise, pooling):
        w = lax.all_gather(w, "rows", axis=1, tiled=True)
        w = lax.all_gather(w, "dp", axis=0, tiled=True)
        channels = pointwise.shape[0] * place.nd
        taps = w.shape[0] // channels
        w = w.reshape(taps, channels // (LANES * place.nr), place.nr, LANES, w.shape[1])
        w = lax.dynamic_index_in_dim(w, place.part, 2, keepdims=False)
        whole.append(jnp.transpose(w.reshape(taps, channels // place.nr, w.shape[-1]), (0, 2, 1)))
    return jnp.concatenate(whole, axis=0)


def scattered_tiles(place, gradients):
    outs = []
    taps, half, width = gradients.shape
    for g in (gradients[: taps - 2], gradients[taps - 2 : taps - 1], gradients[taps - 1 :]):
        g = jnp.transpose(g, (0, 2, 1)).reshape(g.shape[0], width // LANES, 1, LANES, half)
        spread = jnp.zeros((g.shape[0], width // LANES, place.nr, LANES, 2 * half), g.dtype)
        g = lax.dynamic_update_slice(spread, g, (0, 0, place.part, 0, place.zh * half)).reshape(-1, 2 * half)
        g = lax.psum_scatter(g, "dp", scatter_dimension=0, tiled=True)
        outs.append(lax.psum_scatter(g, "rows", scatter_dimension=1, tiled=True).astype(jnp.float32))
    return outs


def doubling(place):
    steps = []
    for name, index, size in (("zl", place.zl, place.nzl), ("zh", place.zh, 2), ("c", place.c, 2), ("m", place.m, place.nd // 2)):
        bit = 1
        while bit < size:
            steps.append(({name: bit}, (index & bit) != 0))
            bit *= 2
    return steps


def joined(place, x, step):
    swap, upper = step
    return jnp.stack(by_xor([x, place.swap(x, **swap)], upper.astype(jnp.int32)))


def halved(place, x, step):
    swap, upper = step
    mine = by_xor([x[0], x[1]], upper.astype(jnp.int32))
    return add_low(mine[0], place.swap(mine[1], **swap))


def m_halved(place, x, steps, first):
    for step in [step for step in steps if "m" in step[0]]:
        if (step[0]["m"] == 1) == (first == 1):
            x = x.reshape((-1, 2) + x.shape[1:])
            x = halved(place, [x[:, k] for k in range(2)], step)
    return x


class Shape:
    def __init__(self, band_rows, columns, nr, width, out, pieces):
        self.band_rows, self.columns, self.nr, self.width, self.out = band_rows, columns, nr, width, out
        self.rows = band_rows * nr
        self.band, self.pixels = band_rows * columns, band_rows * columns * nr
        self.block = BLOCK_ROWS * columns
        self.blocks = self.rows // BLOCK_ROWS
        self.pieces = pieces
        self.quarter = out // 4

    def regions(self, dilation):
        cuts = sorted({0, min(dilation, self.rows), max(self.rows - dilation, 0), self.rows})
        for lo, hi in zip(cuts, cuts[1:]):
            yield lo, hi, [r for r in range(3) if 0 <= lo + (r - 1) * dilation and hi + (r - 1) * dilation <= self.rows]


ANY = pl.BlockSpec(memory_space=pl.ANY)
SMEM = pl.BlockSpec(memory_space=pltpu.SMEM)
VMEM = pl.BlockSpec(memory_space=pltpu.VMEM)
PARAMS = pltpu.CompilerParams(vmem_limit_bytes=58 * 2**20)
TINY = pltpu.CompilerParams(vmem_limit_bytes=8 * 2**20)
SMALL = pltpu.CompilerParams(vmem_limit_bytes=12 * 2**20)


LIGHT = pl.CostEstimate(flops=0, bytes_accessed=0, transcendentals=0)


def lanes_at(start, size=LANES):
    return pl.ds(pl.multiple_of(start, LANES), size)


def start_bands(shape, refs, scratch, sem, part):
    for k, ref in enumerate(refs):
        pltpu.make_async_copy(ref, scratch.at[pl.ds((part ^ k) * shape.band, shape.band), :], sem.at[k]).start()


def wait_bands(shape, refs, scratch, sem):
    for k, ref in enumerate(refs):
        pltpu.make_async_copy(ref, scratch.at[pl.ds(k * shape.band, shape.band), :], sem.at[k]).wait()


def split_features(shape, features, mask, c):
    tiles, n = shape.width // LANES, shape.nr // 2

    def kernel(info, x, mask_ref, *outs):
        valid = mask_ref[...].astype(jnp.bfloat16)
        for k, out in enumerate(outs):
            for q in range(n):
                for i in range(tiles):
                    at = (i * shape.nr + (info[0] ^ k) * n + q) * LANES
                    out[q, :, i * LANES : (i + 1) * LANES] = x[:, lanes_at(at)] * valid

    return pl.pallas_call(
        kernel,
        out_shape=[jax.ShapeDtypeStruct((n, shape.band, shape.width), jnp.bfloat16)] * 2,
        in_specs=[SMEM, VMEM, VMEM],
        out_specs=[VMEM] * 2,
        compiler_params=SMALL,
        cost_estimate=LIGHT,
        name="split_features",
    )(c.reshape(1), features, mask)


def join_features(shape, own, other, c, zl):
    tiles, n = shape.width // LANES, shape.nr // 2

    def kernel(info, *refs):
        for k, part in enumerate(refs[: 2 * n]):
            core, q = info[0] ^ (k // n), info[1] ^ (k % n)
            for i in range(tiles):
                at = (i * shape.nr + core * n + q) * LANES
                refs[2 * n][:, lanes_at(at)] = part[:, i * LANES : (i + 1) * LANES]

    return pl.pallas_call(
        kernel,
        out_shape=jax.ShapeDtypeStruct((shape.band, shape.width * shape.nr), jnp.bfloat16),
        in_specs=[SMEM] + [VMEM] * shape.nr,
        out_specs=VMEM,
        compiler_params=SMALL,
        cost_estimate=LIGHT,
        name="join_features",
    )(jnp.stack([c, zl]).astype(jnp.int32), *own, *other)


def packed_near(shape, zl, own, neighbour):
    size = shape.quarter

    def kernel(info, own, neighbour, out, rest):
        for kl, ref in enumerate((own, neighbour)):
            out[:, pl.ds(pl.multiple_of((info[0] ^ kl) * size, size), size), :] = ref[...]
        rest[: SLOTS - FIRST] = own[FIRST:]
        rest[SLOTS - FIRST :] = neighbour[...]

    return pl.pallas_call(
        kernel,
        out_shape=[
            jax.ShapeDtypeStruct((SLOTS, 2 * size, LANES), jnp.bfloat16),
            jax.ShapeDtypeStruct((2 * SLOTS - FIRST, size, LANES), jnp.bfloat16),
        ],
        in_specs=[SMEM, VMEM, VMEM],
        out_specs=[VMEM, VMEM],
        compiler_params=SMALL,
        cost_estimate=LIGHT,
        name="packed_near",
    )(zl.reshape(1), own, neighbour)


def packed_far(shape, zl, first, rest):
    size = shape.quarter

    def kernel(info, first, rest, out):
        for kl in range(2):
            columns = pl.ds(pl.multiple_of((info[0] ^ kl) * size, size), size)
            if kl == 0:
                out[:FIRST, columns, :] = first[...]
                out[FIRST:, columns, :] = rest[: SLOTS - FIRST]
            else:
                out[:, columns, :] = rest[SLOTS - FIRST :]

    return pl.pallas_call(
        kernel,
        out_shape=jax.ShapeDtypeStruct((SLOTS, 2 * size, LANES), jnp.bfloat16),
        in_specs=[SMEM, VMEM, VMEM],
        out_specs=VMEM,
        compiler_params=SMALL,
        cost_estimate=LIGHT,
        name="packed_far",
    )(zl.reshape(1), first, rest)


def chip_slot(t, c):
    return jnp.where(jnp.where(c == 0, t < FULL, t >= SHORT), t - SHORT * c, FULL + 2 + t - FULL * (1 - c))


def assembled_weights(shape, info, own, by_x, by_y, diagonal):
    def kernel(info, *refs):
        ins, out, sem = refs[:5], refs[5], refs[6]
        m, c = info[0], info[1]

        def copy(ref, slot, tap, lane):
            pltpu.make_async_copy(ref.at[slot], out.at[tap, :, lanes_at(lane)], sem).start()

        def place(rel, slot, tap, lane):
            if rel < 3:
                copy(ins[rel], slot, tap, lane)
            else:

                @pl.when(slot < CUT)
                def _():
                    copy(ins[3], slot, tap, lane)

                @pl.when(slot >= CUT)
                def _():
                    copy(ins[4], slot - CUT, tap, lane)

        for rel in range(4):
            chip = m ^ rel

            def body(t, carry):
                v = chip * PER_CHIP + t
                place(rel, chip_slot(t, c), v // 4, (v % 4) * LANES)
                return carry

            lax.fori_loop(0, PER_CHIP, body, 0)
            for extra in range(2):
                place(rel, FULL + extra, 27 + extra, chip * LANES)
        pltpu.make_async_copy(out, out, sem).wait()

    return pl.pallas_call(
        kernel,
        out_shape=jax.ShapeDtypeStruct((29, shape.out // 2, shape.width), jnp.bfloat16),
        in_specs=[SMEM] + [ANY] * 5,
        out_specs=VMEM,
        scratch_shapes=[pltpu.SemaphoreType.DMA],
        compiler_params=TINY,
        cost_estimate=LIGHT,
        name="assembled_weights",
    )(info, own, by_x, by_y, *diagonal)


def shifted(values, by, columns):
    if by == 0:
        return values
    pixels = values.shape[0]
    source = lax.broadcasted_iota(jnp.int32, (pixels, 1), 0) % columns - by
    return jnp.where((source >= 0) & (source < columns), pltpu.roll(values, by % pixels, 0), 0.0)


def send_halves(shape, c, kept, low, outs, sem):
    half = shape.pixels // 2
    copies = []
    for n, (source, core) in enumerate(((kept, c), (low, 1 - c))):
        rows = source.at[pl.ds(pl.multiple_of(core * half, half), half)]
        copies.append(pltpu.make_async_copy(rows, outs[n], sem.at[n]))
    for copy in copies:
        copy.start()
    for copy in copies:
        copy.wait()


def half_shapes(shape, n):
    half = shape.pixels // 2
    return [
        jax.ShapeDtypeStruct((half, n * shape.out), jnp.float32),
        jax.ShapeDtypeStruct((half, n * shape.out), jnp.bfloat16),
    ]


def start_taps(weights, scratch, sem, taps, zh):
    half = weights[0].shape[1]
    for n, tap in enumerate(taps):
        for kh, ref in enumerate(weights):
            columns = pl.ds(pl.multiple_of((zh ^ kh) * half, half), half)
            pltpu.make_async_copy(ref.at[tap], scratch.at[n, columns], sem.at[n]).start()


def wait_taps(scratch, sem, some):
    for n in some:
        pltpu.make_async_copy(scratch.at[n], scratch.at[n], sem.at[n]).wait()


def dilated_products(shape, branch, x, w, first, y):
    dilation, columns = dilations[branch], shape.columns
    for s in range(3):
        for lo, hi, rs in shape.regions(dilation):
            pixels = jnp.concatenate(
                [x[(lo + (r - 1) * dilation) * columns : (hi + (r - 1) * dilation) * columns, :] for r in rs], axis=1
            )
            taps = jnp.concatenate([w[first + 3 * s + r] for r in rs], axis=1)
            y[s, lo * columns : hi * columns, :] = dot(pixels, taps, NT)


def put_dilated(shape, branch, y, kept, low, lane):
    dilation, columns = dilations[branch], shape.columns
    for blk in range(shape.blocks):
        at = slice(blk * shape.block, (blk + 1) * shape.block)
        z = y[1, at, :] + shifted(y[0, at, :], dilation, columns) + shifted(y[2, at, :], -dilation, columns)
        kept[at, lane : lane + shape.out] = z
        low[at, lane : lane + shape.out] = z.astype(jnp.bfloat16)


def taps_of(branch):
    return [9 * branch + 3 * r + s for s in range(3) for r in range(3)]


def branch_sums(shape, info, area, bands, weights):
    nr = shape.nr

    def kernel(info, area, *refs):
        ins, weights = refs[:nr], refs[nr : nr + 2]
        keep, sent, pooled, lifted, x, w, y, kept, low_sums, band_sem, w_sem, out_sem = refs[nr + 2 :]
        start_bands(shape, ins, x, band_sem, info[5])
        start_taps(weights, w, w_sem, taps_of(2) + taps_of(1) + taps_of(0) + [27, 28], info[2])
        wait_bands(shape, ins, x, band_sem)
        wait_taps(w, w_sem, range(29))
        for n, branch in enumerate((2, 1, 0)):
            dilated_products(shape, branch, x, w, 9 * n, y.at[n % 2])
            put_dilated(shape, branch, y.at[n % 2], kept, low_sums, n * shape.out)
        z = dot(x[...], w[27], NT)
        kept[:, 3 * shape.out :] = z
        low_sums[:, 3 * shape.out :] = z.astype(jnp.bfloat16)
        sums = jnp.zeros((1, shape.width), jnp.float32)
        for blk in range(shape.blocks):
            values = x[blk * shape.block : (blk + 1) * shape.block, :]
            sums = sums + jnp.sum(values.astype(jnp.float32), axis=0, keepdims=True)
        low = jnp.broadcast_to(sums / area[0], pooled.shape).astype(jnp.bfloat16)
        first = lax.broadcasted_iota(jnp.int32, pooled.shape, 0) == 0
        pooled[...] = jnp.where(first, low.astype(jnp.float32), 0.0).astype(jnp.bfloat16)
        lifted[...] = dot(pooled[...], w[28], NT)
        send_halves(shape, info[1], kept, low_sums, (keep, sent), out_sem)

    return pl.pallas_call(
        kernel,
        out_shape=half_shapes(shape, 4)
        + [jax.ShapeDtypeStruct((16, shape.width), jnp.bfloat16), jax.ShapeDtypeStruct((16, shape.out), jnp.float32)],
        in_specs=[SMEM, SMEM] + [ANY] * (nr + 2),
        out_specs=[ANY] * 2 + [VMEM] * 2,
        scratch_shapes=[
            pltpu.VMEM((shape.pixels, shape.width), jnp.bfloat16),
            pltpu.VMEM((29, shape.out, shape.width), jnp.bfloat16),
            pltpu.VMEM((2, 3, shape.pixels, shape.out), jnp.float32),
            pltpu.VMEM((shape.pixels, 4 * shape.out), jnp.float32),
            pltpu.VMEM((shape.pixels, 4 * shape.out), jnp.bfloat16),
            pltpu.SemaphoreType.DMA((nr,)),
            pltpu.SemaphoreType.DMA((29,)),
            pltpu.SemaphoreType.DMA((2,)),
        ],
        compiler_params=PARAMS,
        cost_estimate=LIGHT,
        name="branch_sums",
    )(info, area, *bands, *weights)


def band_mask(shape, info):
    pixel = lax.broadcasted_iota(jnp.int32, (shape.band, 1), 0)
    row, column = info[4] * shape.band_rows + pixel // shape.columns, pixel % shape.columns
    return ((row < info[6]) & (column < info[7])).astype(jnp.float32)


def put_moments(values, mask, ref, at_sum, at_square, count):
    total = jnp.sum(values * mask, axis=0, keepdims=True)
    centred = (values - total / jnp.maximum(count, 1.0)) * mask
    ref[at_sum : at_sum + 1, :] = total
    ref[at_square : at_square + 1, :] = jnp.sum(centred * centred, axis=0, keepdims=True)


def merged_rows(refs, k, n):
    count = tree([ref[2 * n : 2 * n + 1, :] for ref in refs])
    mean = tree([ref[k : k + 1, :] for ref in refs]) / jnp.maximum(count, 1.0)
    between = []
    for ref in refs:
        own = ref[2 * n : 2 * n + 1, :]
        gap = ref[k : k + 1, :] / jnp.maximum(own, 1.0) - mean
        between.append(own * gap * gap)
    squares = tree([ref[n + k : n + k + 1, :] for ref in refs]) + tree(between)
    return mean, squares / count, count


def silu(v):
    return v * jax.nn.sigmoid(v)


def call(shape, kernel, name, outs, out_specs, in_specs, scratch=()):
    return pl.pallas_call(
        kernel,
        out_shape=[jax.ShapeDtypeStruct(*o) for o in outs],
        in_specs=in_specs,
        out_specs=out_specs,
        scratch_shapes=list(scratch),
        compiler_params=SMALL,
        cost_estimate=LIGHT,
        name=name,
    )


TABLE = 16


def branch_moments(shape, info, images, mine, others, lifted):
    n = len(others)

    def kernel(info, mine, lifted, *refs):
        others, (z, rows) = refs[:n], refs[n:]
        mask = band_mask(shape, info)
        count = jnp.sum(mask)
        rows[...] = jnp.zeros(rows.shape, jnp.float32)
        for k in range(4):
            lanes = slice((3 - k) * shape.out, (4 - k) * shape.out)
            value = mine[:, lanes]
            for other in others:
                value = value + other[:, lanes].astype(jnp.float32)
            z[:, k * shape.out : (k + 1) * shape.out] = value
            put_moments(value, mask, rows, k, 4 + k, count)
        rows[8:9, :] = jnp.full((1, shape.out), count, jnp.float32)
        rows[pl.ds(TABLE + 2 * info[0] + info[2], 1), :] = lifted[0:1, :]

    return call(
        shape,
        kernel,
        "branch_moments",
        [((shape.band, 4 * shape.out), jnp.float32), ((TABLE + images, shape.out), jnp.float32)],
        [VMEM] * 2,
        [SMEM] + [VMEM] * (2 + n),
    )(info, mine, lifted, *others)


def projected(shape, info, images, rows, z, projection, gain, bias):
    out = shape.out

    def kernel(info, z, projection, gain, bias, *refs):
        n = len(rows)
        rows_in, (concat, pre, moments, stats) = refs[:n], refs[n:]
        mask = band_mask(shape, info)
        pool = tree([ref[TABLE : TABLE + images, :] for ref in rows_in])
        pool = pool - jnp.sum(pool, axis=0, keepdims=True) / images
        pool_inv = lax.rsqrt(jnp.sum(pool * pool, axis=0, keepdims=True) / images + epsilon)
        pool = pool * pool_inv
        stats[9:10, :] = pool_inv
        stats[TABLE : TABLE + images, :] = pool
        stats[TABLE + images :, :] = gain[4:5, :] * pool + bias[4:5, :]
        for k in range(4):
            average, spread, count = merged_rows(rows_in, k, 4)
            inv = lax.rsqrt(spread + epsilon)
            stats[k : k + 1, :] = average
            stats[4 + k : 5 + k, :] = inv
            lanes = slice(k * out, (k + 1) * out)
            lifted = gain[k : k + 1, :] * ((z[:, lanes] - average) * inv) + bias[k : k + 1, :]
            concat[:, lanes] = (silu(lifted) * mask).astype(jnp.bfloat16)
        stats[8:9, :] = count
        line = stats[pl.ds(TABLE + images + 2 * info[0] + info[2], 1), :]
        concat[:, 4 * out :] = (silu(line) * mask).astype(jnp.bfloat16)
        value = dot(concat[...], projection[...], NT)
        pre[...] = value
        local = jnp.sum(mask)
        put_moments(value, mask, moments, 0, 1, local)
        moments[2:, :] = jnp.full((6, out), local, jnp.float32)

    return call(
        shape,
        kernel,
        "projected",
        [
            ((shape.band, 5 * out), jnp.bfloat16),
            ((shape.band, out), jnp.float32),
            ((8, out), jnp.float32),
            ((TABLE + 2 * images, out), jnp.float32),
        ],
        [VMEM] * 4,
        [SMEM] + [VMEM] * (4 + len(rows)),
    )(info, z, projection, gain, bias, *rows)


def branch_gradients(shape, info, images, rows, upstream, normed, inv, z, stats, projection, gain, bias):
    out = shape.out

    def kernel(info, upstream, normed, inv, z, stats, projection, gain, bias, *refs):
        n = len(rows)
        rows_in, (delta, up, sums, totals) = refs[:n], refs[n:]
        mask = band_mask(shape, info)
        whole = tree([ref[...] for ref in rows_in])
        totals[...] = whole
        count, scale = stats[8:9, :], gain[5:6, :]
        low = (
            mask
            * inv[...]
            * (scale * upstream[...] - scale * whole[1:2] / count - normed[...] * scale * whole[0:1] / count)
        ).astype(jnp.bfloat16)
        delta[...] = low
        sums[...] = jnp.zeros(sums.shape, jnp.float32)
        for k in range(4):
            lanes = slice(k * out, (k + 1) * out)
            at = (z[:, lanes] - stats[k : k + 1, :]) * stats[4 + k : 5 + k, :]
            slope = silu_slope(gain[k : k + 1, :] * at + bias[k : k + 1, :])
            value = dot(low, projection[:, lanes], NN) * mask * slope
            up[:, lanes] = value
            sums[k : k + 1, :] = jnp.sum(value * at, axis=0, keepdims=True)
            sums[4 + k : 5 + k, :] = jnp.sum(value, axis=0, keepdims=True)
        line = jnp.sum(dot(low, projection[:, 4 * out :], NN) * mask, axis=0, keepdims=True)
        sums[pl.ds(8 + 2 * info[0] + info[2], 1), :] = line

    return call(
        shape,
        kernel,
        "branch_gradients",
        [
            ((shape.band, out), jnp.bfloat16),
            ((shape.band, 4 * out), jnp.float32),
            ((8 + images, out), jnp.float32),
            ((8, out), jnp.float32),
        ],
        [VMEM] * 4,
        [SMEM] + [VMEM] * (8 + len(rows)),
    )(info, upstream, normed, inv, z, stats, projection, gain, bias, *rows)


def branch_deltas(shape, info, rows, up, z, stats, gain):
    out, half = shape.out, shape.out // 2

    def kernel(info, up, z, stats, gain, *refs):
        n = len(rows)
        rows_in, (delta, crossing, totals) = refs[:n], refs[n:]
        mask = band_mask(shape, info)
        totals[...] = tree([ref[...] for ref in rows_in])
        count = stats[8:9, :]
        for k in range(4):
            lanes = slice(k * out, (k + 1) * out)
            inv, scale = stats[4 + k : 5 + k, :], gain[k : k + 1, :]
            at = (z[:, lanes] - stats[k : k + 1, :]) * inv
            by_gain, by_bias = totals[k : k + 1, :], totals[4 + k : 5 + k, :]
            value = mask * inv * (scale * up[:, lanes] - scale * by_bias / count - at * scale * by_gain / count)
            delta[:, lanes] = value.astype(jnp.bfloat16)
            crossing[:, k * half : (k + 1) * half] = delta[:, lanes_at(k * out + (1 - info[2]) * half, half)]

    return call(
        shape,
        kernel,
        "branch_deltas",
        [
            ((shape.band, 4 * out), jnp.bfloat16),
            ((shape.band, 4 * half), jnp.bfloat16),
            (rows[0].shape, jnp.float32),
        ],
        [VMEM] * 3,
        [SMEM] + [VMEM] * (4 + len(rows)),
    )(info, up, z, stats, gain, *rows)


def moved_columns(shape, delta, lane, lanes, branch, moved):
    for blk in range(shape.blocks):
        at = slice(blk * shape.block, (blk + 1) * shape.block)
        values = delta[at, lanes_at(lane, lanes)].astype(jnp.float32)
        for s in range(3):
            moved[at, s * lanes : (s + 1) * lanes] = shifted(
                values, (s - 1) * dilations[branch], shape.columns
            ).astype(jnp.bfloat16)


def input_gradient(shape, info, area, deltas, pool_delta, weights):
    nr, columns = shape.nr, shape.columns

    def kernel(info, area, *refs):
        ins, pool_delta, weights = refs[:nr], refs[nr], refs[nr + 1 : nr + 3]
        outs = refs[nr + 3 : 2 * nr + 3]
        delta, moved, w, acc, delta_sem, w_sem = refs[2 * nr + 3 :]
        start_bands(shape, ins, delta, delta_sem, info[4])
        start_taps(weights, w, w_sem, range(29), info[2])
        wait_bands(shape, ins, delta, delta_sem)
        wait_taps(w, w_sem, range(29))
        pool = dot(pool_delta[...], w[28], NN)[0:1] / area[0]
        acc[...] = dot(delta[:, : shape.out], w[27], NN) + pool
        for branch in range(3):
            dilation = dilations[branch]
            moved_columns(shape, delta, (branch + 1) * shape.out, shape.out, branch, moved)
            for lo, hi, rs in shape.regions(dilation):
                rows = [2 - r for r in rs]
                cut = lambda r: moved[(lo - (r - 1) * dilation) * columns : (hi - (r - 1) * dilation) * columns, :]
                pixels = jnp.concatenate([cut(r) for r in rows], axis=1)
                taps = jnp.concatenate([w[9 * branch + 3 * r + s] for r in rows for s in range(3)], axis=0)
                acc[lo * columns : hi * columns, :] += dot(pixels, taps, NN)
        pixel = lax.broadcasted_iota(jnp.int32, (shape.band, 1), 0)
        for k in range(nr):
            first = (info[5] ^ k) * shape.band
            inside = ((pixel + first) // columns < info[6]) & (pixel % columns < info[7])
            values = acc[pl.ds(pl.multiple_of(first, shape.band), shape.band), :]
            outs[k][...] = jnp.where(inside, values, 0.0).astype(jnp.bfloat16)

    return pl.pallas_call(
        kernel,
        out_shape=[jax.ShapeDtypeStruct((shape.band, shape.width), jnp.bfloat16)] * nr,
        in_specs=[SMEM, SMEM] + [ANY] * nr + [VMEM] + [ANY] * 2,
        out_specs=[VMEM] * nr,
        scratch_shapes=[
            pltpu.VMEM((shape.pixels, 4 * shape.out), jnp.bfloat16),
            pltpu.VMEM((shape.pixels, 3 * shape.out), jnp.bfloat16),
            pltpu.VMEM((29, shape.out, shape.width), jnp.bfloat16),
            pltpu.VMEM((shape.pixels, shape.width), jnp.float32),
            pltpu.SemaphoreType.DMA((nr,)),
            pltpu.SemaphoreType.DMA((29,)),
        ],
        compiler_params=PARAMS,
        cost_estimate=pl.CostEstimate(
            flops=44 * shape.pixels * shape.width * shape.out, bytes_accessed=2**24, transcendentals=0
        ),
        name="input_gradient",
    )(info, area, *deltas, pool_delta, *weights)


def weight_gradients(shape, info, bands, far_bands, deltas, far_deltas, pool_deltas, pooled):
    nr, columns, half = shape.nr, shape.columns, shape.out // 2
    n_outs = 8 if shape.pieces else 1
    by_rows = lambda v: v.reshape(v.shape[0] // columns, columns, v.shape[1])
    bands = [by_rows(band) for band in [*bands, *far_bands]]

    def kernel(info, *refs):
        ins, delta_ins, far_delta_ins = (refs[n * nr : (n + 1) * nr] for n in range(3))
        far_ins, refs = refs[3 * nr : 4 * nr], refs[4 * nr :]
        pool_deltas, pooled, outs = refs[0], refs[1], refs[2 : 2 + n_outs]
        x, delta, far_delta, moved, grads, sem, out_sem = refs[2 + n_outs :]
        m, c, zh, part, z = info[0], info[1], info[2], info[4], info[5]
        rows = shape.band_rows
        start_bands(shape, delta_ins, delta, sem.at[0], part)
        start_bands(shape, far_delta_ins, far_delta, sem.at[1], part)
        for image, sources in enumerate((ins, far_ins)):
            for k, ref in enumerate(sources):
                pltpu.make_async_copy(ref, x.at[pl.ds((z ^ k) * rows, rows), image], sem.at[2 + image, k]).start()

        def arrive(n):
            for k in range(nr):
                if n < 2:
                    some = (delta, far_delta)[n].at[pl.ds(k * shape.band, shape.band)]
                else:
                    some = x.at[pl.ds(k * rows, rows), n - 2]
                pltpu.make_async_copy(some, some, sem.at[n, k]).wait()

        def move(branch):
            for image, source in enumerate((delta, far_delta)):
                lane = (branch + 1) * half if image else (branch + 1) * shape.out + zh * half
                for blk in range(shape.blocks):
                    at = slice(blk * shape.block, (blk + 1) * shape.block)
                    values = source[at, lanes_at(lane, half)].astype(jnp.float32)
                    for s in range(3):
                        value = shifted(values, (s - 1) * dilations[branch], columns).astype(jnp.bfloat16)
                        moved[blk * BLOCK_ROWS : (blk + 1) * BLOCK_ROWS, image, :, s * half : (s + 1) * half] = (
                            value.reshape(BLOCK_ROWS, columns, half)
                        )

        flat = lambda v: v.reshape(-1, v.shape[-1])

        def put(tap, value):
            value = value.astype(jnp.bfloat16)
            if not shape.pieces:
                grads[tap] = value
                return
            for i in range(4):
                if tap < 27:
                    v = 4 * tap + i
                    chip, slot = v // PER_CHIP, chip_slot(v % PER_CHIP, c)
                else:
                    chip, slot = i, FULL + tap - 27
                for q in range(2):
                    rows = slice(q * shape.quarter, (q + 1) * shape.quarter)
                    grads[2 * (m ^ chip) + q, slot] = value[rows, i * LANES : (i + 1) * LANES]

        arrive(0)
        arrive(1)
        for branch in range(3):
            move(branch)
            if branch == 0:
                arrive(2)
                arrive(3)
            dilation = dilations[branch]
            for r in range(3):
                up, down = max(0, 1 - r) * dilation, max(0, r - 1) * dilation
                to = flat(moved[up : shape.rows - down])
                value = dot(to, flat(x[down : shape.rows - up]), TN)
                for s in range(3):
                    put(9 * branch + 3 * r + s, value[s * half : (s + 1) * half])
        one = jnp.concatenate(
            [
                delta[:, lanes_at(zh * half, half)].reshape(shape.rows, 1, columns, half),
                far_delta[:, :half].reshape(shape.rows, 1, columns, half),
            ],
            axis=1,
        )
        put(27, dot(flat(one), flat(x[...]), TN))
        put(28, dot(pool_deltas[...], pooled[...], TN))
        copies = [pltpu.make_async_copy(grads.at[n] if shape.pieces else grads, outs[n], out_sem.at[n]) for n in range(n_outs)]
        for copy in copies:
            copy.start()
        for copy in copies:
            copy.wait()

    if shape.pieces:
        out_shape = [jax.ShapeDtypeStruct((SLOTS, shape.quarter, LANES), jnp.bfloat16)] * 8
        grads_shape = (8, SLOTS, shape.quarter, LANES)
    else:
        out_shape = [jax.ShapeDtypeStruct((29, half, shape.width), jnp.bfloat16)]
        grads_shape = (29, half, shape.width)
    return pl.pallas_call(
        kernel,
        out_shape=out_shape,
        in_specs=[SMEM] + [ANY] * (4 * nr) + [VMEM] * 2,
        out_specs=[ANY] * n_outs,
        scratch_shapes=[
            pltpu.VMEM((shape.rows, 2, columns, shape.width), jnp.bfloat16),
            pltpu.VMEM((shape.pixels, 4 * shape.out), jnp.bfloat16),
            pltpu.VMEM((shape.pixels, 2 * shape.out), jnp.bfloat16),
            pltpu.VMEM((shape.rows, 2, columns, 3 * half), jnp.bfloat16),
            pltpu.VMEM(grads_shape, jnp.bfloat16),
            pltpu.SemaphoreType.DMA((4, nr)),
            pltpu.SemaphoreType.DMA((n_outs,)),
        ],
        compiler_params=PARAMS,
        cost_estimate=pl.CostEstimate(
            flops=44 * shape.pixels * shape.width * shape.out, bytes_accessed=2**24, transcendentals=0
        ),
        name="weight_gradients",
    )(info, *bands[:nr], *deltas, *far_deltas, *bands[nr:], pool_deltas, pooled)


def valid_pixels(extent, first_row, rows, columns):
    r = first_row + lax.broadcasted_iota(jnp.int32, (rows, columns), 0)
    w = lax.broadcasted_iota(jnp.int32, (rows, columns), 1)
    return ((r < extent[0]) & (w < extent[1])).astype(jnp.float32).reshape(rows * columns, 1)


def to_logical(place, x):
    return jnp.where(place.zh == place.c, x, place.swap(x, c=1, zh=1))


def on_device(
    features, extent, pointwise_weight, pooling_weight, dilated_weight, projection_weight, norm_gain, norm_bias, cotangent
):
    place = Place()
    nr, nzl = place.nr, place.nzl
    _, band_rows, columns, channels = features.shape
    width, out = channels // nr, norm_gain.shape[1]
    band = band_rows * columns
    pieces = nr == 4 and place.nd == 8 and dilated_weight.shape[0] == 2 * PER_CHIP * LANES
    shape = Shape(band_rows, columns, nr, width, out, pieces)
    images = place.nd

    partner = place.swap(extent, c=1)
    extent_here = jnp.where(place.zh == place.c, extent, partner)[0]
    area = (extent_here[0] * extent_here[1]).astype(jnp.float32)
    mask = valid_pixels(extent_here, place.part * band_rows, band_rows, columns)
    own_mask = valid_pixels(extent[0], place.z * band_rows, band_rows, columns)
    here_now = [place.m, place.c, place.zh, place.zl, place.part, place.z, extent_here[0], extent_here[1]]
    info = jnp.stack(here_now).astype(jnp.int32)
    areas = area.reshape(1)

    own_parts, other_parts = split_features(shape, features.reshape(band, channels), own_mask, place.c)
    held = by_xor([own_parts, place.swap(other_parts, c=1)], place.c)
    held = [by_xor([v[q] for q in range(nzl)], place.zl) for v in by_xor(held, place.zh)]

    def sent(image, k, first=()):
        kh, kl = divmod(k, nzl)
        v = held[kh ^ image][kl]
        return place.swap(after(v, first), zh=kh, zl=kl) if k else v

    steps = doubling(place)
    nd_bits = (place.nd // 2).bit_length() - 1
    projection = projection_weight.T
    if pieces:
        sources = line_pieces(place, dilated_weight, pointwise_weight, pooling_weight)
        crossed = place.swap(sources[0][:FIRST], zh=1)
        neighbour = after(place.swap(sources[1], zl=1), crossed, own_parts, other_parts, partner)
        near, rest = packed_near(shape, place.zl, sources[0], neighbour)
        rest = place.swap(rest, zh=1)
        near_x, near_y = plane_direct(place, near)
        near_d = plane_diagonal(place, near_x, near_y)
        far = packed_far(shape, place.zl, crossed, after(rest, near_d, held))
        crossing_band = sent(0, nzl, first=far)
        far_x, far_y = after(plane_direct(place, far), crossing_band)
        far_d = plane_diagonal(place, far_x, far_y)
        bands = [sent(0, k, first=far_x) for k in range(nzl)] + [crossing_band]
        bands += [sent(0, k, first=crossing_band) for k in range(nzl + 1, nr)]
        near = assembled_weights(shape, info, near, near_x, near_y, near_d)
        weights = [near, assembled_weights(shape, info, far, far_x, far_y, after(far_d, near))]
    else:
        bands = [sent(0, k) for k in range(nr)]
        weights = gathered_tiles(place, dilated_weight, pointwise_weight, pooling_weight)
        weights = by_xor([weights[:, : out // 2], weights[:, out // 2 :]], place.zh)

    def given_on(keep, got):
        bands_of = lambda v: v.reshape(nzl, band, v.shape[1])
        at = lambda k: [lax.dynamic_index_in_dim(bands_of(v), place.zl ^ k, 0, keepdims=False) for v in (keep, got)]
        summed = lambda k: at(k)[0] + at(k)[1].astype(jnp.float32)
        return summed(0), [place.swap(summed(k).astype(jnp.bfloat16), zl=k) for k in range(1, nzl)]

    ready = (bands, weights)
    keep, given, pooled, lifted = branch_sums(shape, info, areas, bands, weights)
    far_bands = [sent(1, k, first=ready) for k in range(nzl + 1)]
    projection = after(projection, ready)
    projection = joined(place, projection, steps[-nd_bits - 2])
    given = after(given, far_bands, projection)
    projection = after(projection, given)
    for step in steps[: -nd_bits - 2]:
        projection = joined(place, projection, step)
    got, projection = after((place.swap(given, c=1), projection), projection)
    projection = joined(place, projection, steps[-nd_bits - 1])
    upstream_low = to_logical(place, after(cotangent.reshape(band, out), got))
    plane = [projection] + [place.swap(projection, m=k) for k in range(1, images // 2)]
    mine, others = given_on(keep, got)
    projection = jnp.stack(by_xor(plane, place.m))
    projection = projection.reshape((images // 2, 2, nzl, 2) + projection_weight.shape[::-1])
    projection = jnp.transpose(projection, (3, 2, 4, 0, 1, 5)).reshape(out, -1)
    mine, others = after((mine, others), projection, upstream_low)
    z, rows = branch_moments(shape, info, images, mine, others, lifted)
    rows = exchanged(place, rows, lambda xs: merged(xs, 4))
    concat, proj_pre, rows, stats = projected(shape, info, images, rows, z, projection, norm_gain, norm_bias)
    pooled_far = place.swap(pooled, zh=1)
    rows = merged(exchanged(place, rows, lambda xs: merged(xs, 1)), 1)
    proj_average, proj_spread = rows[0:1] / rows[2:3], rows[1:2] / rows[2:3]
    proj_inv = lax.rsqrt(proj_spread + epsilon)
    proj_normed = (proj_pre - proj_average) * proj_inv
    proj_lift = norm_gain[5:6] * proj_normed + norm_bias[5:6]
    output_here = (jax.nn.silu(proj_lift) * mask).astype(jnp.bfloat16)

    upstream = upstream_low.astype(jnp.float32) * mask * silu_slope(proj_lift)
    sums = [jnp.sum(upstream * proj_normed, axis=0, keepdims=True), jnp.sum(upstream, axis=0, keepdims=True)]
    rows = exchanged(place, jnp.concatenate(sums + [jnp.zeros((6, out), jnp.float32)], axis=0), tree)
    proj_delta, branch_up, rows, proj_totals = branch_gradients(
        shape, info, images, rows, upstream, proj_normed, proj_inv, z, stats, projection, norm_gain, norm_bias
    )
    projection_partial = lambda first: dot(after(proj_delta, first), concat, TN)
    rows = exchanged(place, rows, tree)
    delta, crossing, totals = branch_deltas(shape, info, after(rows, pooled_far), branch_up, z, stats, norm_gain)
    proj_gain_grad, proj_bias_grad = proj_totals[0:1], proj_totals[1:2]
    branch_gain_grad, branch_bias_grad = totals[:4], totals[4:8]
    pool_inv, pool_normed, pool_lift = stats[9:10], stats[TABLE : TABLE + images], stats[TABLE + images :]
    here = lambda rows: lax.dynamic_slice_in_dim(rows, place.image, 1, axis=0)
    pool_up = totals[8:] * silu_slope(pool_lift)
    pool_gain_grad = jnp.sum(pool_up * pool_normed, axis=0, keepdims=True)
    pool_bias_grad = jnp.sum(pool_up, axis=0, keepdims=True)
    pool_deltas = pool_inv * (
        norm_gain[4:5] * pool_up
        - norm_gain[4:5] * pool_bias_grad / images
        - pool_normed * norm_gain[4:5] * pool_gain_grad / images
    )
    low_rows = lambda rows: jnp.pad(rows, ((0, 16 - rows.shape[0]), (0, 0))).astype(jnp.bfloat16)
    pool_pair = lax.dynamic_slice_in_dim(pool_deltas, 2 * place.m, 2, axis=0)
    halves = lambda v, n: by_xor([v[:, n * out : n * out + out // 2], v[:, n * out + out // 2 : (n + 1) * out]], place.zh)
    def over_group(v, first):
        near = [v] + [after(place.swap(v, zl=k), first) for k in range(1, nzl)]
        return near + [place.swap(n, c=1) for n in near]

    crossing = place.swap(crossing, zh=1)
    rows = projection_weight.shape[0]
    part = projection_partial(delta).astype(jnp.bfloat16).reshape(out, images // 2, 2, rows)
    part = jnp.transpose(part, (2, 1, 0, 3)).reshape(2, images // 2, 2, nzl, out // nr, rows)
    part = halved(place, [part[k] for k in range(2)], steps[-nd_bits - 1])
    spread_deltas = over_group(delta, (crossing, part))
    part = m_halved(place, after(part, spread_deltas), steps, 1)
    far_deltas = [crossing] + [place.swap(crossing, zl=k) for k in range(1, nzl)]
    inputs = input_gradient(shape, info, areas, spread_deltas, low_rows(here(pool_deltas)), weights)

    far_bands += [sent(1, k, first=spread_deltas) for k in range(nzl + 1, nr)]
    crossing = after(far_deltas, inputs, far_bands)
    pooled_pair = pooled + jnp.roll(pooled_far, 1, axis=0)
    pool_pair = jnp.concatenate([pool_pair[i : i + 1] for i in range(2)], axis=0)
    pool_pair = jnp.concatenate(by_xor([pool_pair[0:1], pool_pair[1:2]], place.zh), axis=0)
    pool_pair = halves(low_rows(pool_pair), 0)[0]
    far_deltas = crossing + [place.swap(n, c=1) for n in crossing]
    grads = weight_gradients(shape, info, bands, far_bands, spread_deltas, far_deltas, pool_pair, pooled_pair)

    done = (far_deltas, far_bands, part)
    handed = [place.swap(after(inputs[nzl + k], done), zh=1) for k in range(1, nzl)]
    near_handed = [place.swap(after(inputs[k], done), zl=k) for k in range(1, nzl)]
    output = to_logical(place, after(output_here, inputs))
    part = m_halved(place, after(part, inputs), steps, 2)
    crossed = (handed, near_handed, output, part)
    if pieces:
        pairs = [[grads[2 * rel], grads[2 * rel + 1]] for rel in range(4)]
        first_d, second_d = plane_scatter_diagonal(place, pairs)
        first_d, second_d = after((first_d, second_d), crossed, part)
        quarters = plane_scatter(place, pairs, first_d, second_d)
    else:
        quarters = grads
    part, last = after((part, inputs[nzl]), crossed)
    part = part.reshape((2, nzl) + part.shape[-2:])
    part = halved(place, [part[k] for k in range(2)], steps[-nd_bits - 2])
    last = place.swap(last, zh=1)
    handed = [place.swap(after(handed[k - 1], near_handed), zl=k) for k in range(1, nzl)]
    returned = by_xor([[inputs[0]] + near_handed, [last] + handed], place.zh)
    quarters = after(quarters, part, output, returned)
    returned = by_xor(returned, place.c)
    traded = place.swap(jnp.stack(returned[1]), c=1)
    feature_gradient = join_features(shape, returned[0], [traded[k] for k in range(nzl)], place.c, place.zl)
    if pieces:
        dilated_gradient, pointwise_gradient, pooling_gradient = line_back(place, quarters, feature_gradient)
    else:
        dilated_gradient, pointwise_gradient, pooling_gradient = scattered_tiles(place, quarters[0])
    part = after(part, feature_gradient)
    for step in [step for step in steps if "zl" in step[0]]:
        part = part.reshape((-1, 2) + part.shape[-2:])
        part = halved(place, [part[:, k] for k in range(2)], step)
    projection_gradient = part.reshape(out // nr, rows).astype(jnp.float32).T

    return (
        output.reshape(cotangent.shape),
        feature_gradient.reshape(features.shape),
        pointwise_gradient,
        pooling_gradient,
        dilated_gradient,
        projection_gradient,
        jnp.concatenate([branch_gain_grad, pool_gain_grad, proj_gain_grad], axis=0),
        jnp.concatenate([branch_bias_grad, pool_bias_grad, proj_bias_grad], axis=0),
    )


def solution(mesh):
    banded = P("dp", "rows", None, None)
    blocks = P("dp", "rows")
    return jax.shard_map(
        on_device,
        mesh=mesh,
        in_specs=(banded, P("dp", None), blocks, blocks, blocks, blocks, P(), P(), banded),
        out_specs=(banded, banded, blocks, blocks, blocks, blocks, P(), P()),
        check_vma=False,
    )
```

```python
import jax
import jax.numpy as jnp
from jax import lax
from jax.experimental import pallas as pl
from jax.experimental.pallas import tpu as pltpu
from jax.sharding import PartitionSpec as P

epsilon = 1e-05
dilations = (6, 12, 18)
LANES = 128
BLOCK_ROWS = 6
AXES = ("dp", "rows")
FULL, SHORT, PER_CHIP = 14, 13, 27
SLOTS = FULL + 2 + SHORT
FIRST = 16
CUT = 15
NT = (((1,), (1,)), ((), ()))
TN = (((0,), (0,)), ((), ()))
NN = (((1,), (0,)), ((), ()))


def dot(first, second, dims):
    return lax.dot_general(first, second, dims, preferred_element_type=jnp.float32)


def after(x, *first):
    return lax.optimization_barrier((x, first))[0]


def silu_slope(values):
    sigma = jax.nn.sigmoid(values)
    return sigma * (1.0 + values * (1.0 - sigma))


class Place:
    def __init__(self):
        self.nd, self.nr = lax.axis_size("dp"), lax.axis_size("rows")
        self.nzl = self.nr // 2
        d, z = lax.axis_index("dp"), lax.axis_index("rows")
        self.d, self.z = d, z
        self.m, self.c = d // 2, d % 2
        self.zh, self.zl = z // self.nzl, z % self.nzl
        self.part = self.c * self.nzl + self.zl
        self.image = 2 * self.m + self.zh

    def swap(self, x, m=0, c=0, zh=0, zl=0):
        nzl = self.nzl
        pairs = []
        for flat in range(self.nd * self.nr):
            d, z = divmod(flat, self.nr)
            pairs.append((flat, (d ^ (2 * m + c)) * self.nr + (z ^ (zh * nzl + zl))))
        return lax.ppermute(x, AXES, pairs)


def by_xor(items, index):
    items = list(items)
    bit = 1
    while bit < len(items):
        flip = (index & bit) != 0
        pick = lambda a, b: jnp.where(flip, a, b)
        items = [jax.tree.map(pick, items[k ^ bit], items[k]) for k in range(len(items))]
        bit *= 2
    return items


def tree(items):
    items = list(items)
    while len(items) > 1:
        items = [items[i] + items[i + 1] for i in range(0, len(items), 2)]
    return items[0]


def exchange_stages(place):
    return (
        [dict(c=1)],
        [dict(m=k) for k in range(1, place.nd // 2)],
        [dict(zh=k // place.nzl, zl=k % place.nzl) for k in range(1, place.nr)],
    )


def total(place, x):
    for stage in exchange_stages(place):
        x = tree([x] + [place.swap(x, **s) for s in stage])
    return x


def merged(xs, k):
    whole = tree(xs)
    mean = whole[:k] / jnp.maximum(whole[2 * k : 2 * k + 1], 1.0)
    between = []
    for y in xs:
        own = y[2 * k : 2 * k + 1]
        gap = y[:k] / jnp.maximum(own, 1.0) - mean
        between.append(own * gap * gap)
    return jnp.concatenate([whole[:k], whole[k : 2 * k] + tree(between), whole[2 * k :]], axis=0)


def exchanged(place, x, combine):
    *stages, last = exchange_stages(place)
    for stage in stages:
        x = combine([x] + [place.swap(x, **s) for s in stage])
    return [x] + [place.swap(x, **s) for s in last]


def line_pieces(place, dilated, pointwise, pooling):
    tiles = lambda w: jnp.transpose(w.T.reshape(w.shape[1], w.shape[0] // LANES, LANES), (1, 0, 2))
    dil, one, pool = tiles(dilated), tiles(pointwise), tiles(pooling)
    other = [dil[2 + r :: 4][:SHORT] for r in range(2)]
    got = place.swap(jnp.concatenate(other, axis=0), c=1)
    same = [jnp.concatenate([dil[r::4][:FULL], one[r : r + 1], pool[r : r + 1]], axis=0) for r in range(2)]
    whole = [jnp.concatenate([same[r], got[r * SHORT : (r + 1) * SHORT]], axis=0) for r in range(2)]
    return by_xor(whole, place.zl)


def plane_direct(place, half):
    return place.swap(half, m=1), place.swap(half, m=2)


def plane_diagonal(place, by_x, by_y):
    return place.swap(by_x[:CUT], m=2), place.swap(by_y[CUT:], m=1)


def add_low(first, *others):
    out = first.astype(jnp.float32)
    for o in others:
        out = out + o.astype(jnp.float32)
    return out.astype(jnp.bfloat16)


def plane_scatter_diagonal(place, pieces):
    return place.swap(pieces[3][0], m=2), place.swap(pieces[3][1], m=1)


def plane_scatter(place, pieces, first_d, second_d):
    to_x = jnp.stack([add_low(pieces[1][0], first_d), pieces[1][1]])
    to_y = jnp.stack([pieces[2][0], add_low(pieces[2][1], second_d)])
    by_x, by_y = place.swap(to_x, m=1), place.swap(to_y, m=2)
    return [add_low(pieces[0][q], by_x[q], by_y[q]) for q in range(2)]


def line_back(place, quarters, first):
    by_kl = by_xor(quarters, place.zl)
    by_part = by_xor([by_kl[0], after(place.swap(by_kl[1], zl=1), first)], place.zl)
    same = [p[: FULL + 2] for p in by_part]
    got = place.swap(jnp.concatenate([p[FULL + 2 :] for p in by_part], axis=0), c=1)
    other = [got[r * SHORT : (r + 1) * SHORT] for r in range(2)]
    gap = jnp.zeros((FULL - SHORT,) + other[0].shape[1:], other[0].dtype)
    dil = jnp.stack([s[:FULL] for s in same] + [jnp.concatenate([o, gap], axis=0) for o in other], axis=1)
    dil = dil.reshape((4 * FULL,) + dil.shape[2:])[: 2 * PER_CHIP]
    rows = lambda t: jnp.transpose(t, (1, 0, 2)).reshape(t.shape[1], t.shape[0] * LANES).astype(jnp.float32).T
    one = jnp.stack([s[FULL] for s in same])
    pool = jnp.stack([s[FULL + 1] for s in same])
    return rows(dil), rows(one), rows(pool)


def gathered_tiles(place, dilated, pointwise, pooling):
    whole = []
    for w in (dilated, pointwise, pooling):
        w = lax.all_gather(w, "rows", axis=1, tiled=True)
        w = lax.all_gather(w, "dp", axis=0, tiled=True)
        channels = pointwise.shape[0] * place.nd
        taps = w.shape[0] // channels
        w = w.reshape(taps, channels // (LANES * place.nr), place.nr, LANES, w.shape[1])
        w = lax.dynamic_index_in_dim(w, place.part, 2, keepdims=False)
        whole.append(jnp.transpose(w.reshape(taps, channels // place.nr, w.shape[-1]), (0, 2, 1)))
    return jnp.concatenate(whole, axis=0)


def scattered_tiles(place, gradients):
    outs = []
    taps, half, width = gradients.shape
    for g in (gradients[: taps - 2], gradients[taps - 2 : taps - 1], gradients[taps - 1 :]):
        g = jnp.transpose(g, (0, 2, 1)).reshape(g.shape[0], width // LANES, 1, LANES, half)
        spread = jnp.zeros((g.shape[0], width // LANES, place.nr, LANES, 2 * half), g.dtype)
        g = lax.dynamic_update_slice(spread, g, (0, 0, place.part, 0, place.zh * half)).reshape(-1, 2 * half)
        g = lax.psum_scatter(g, "dp", scatter_dimension=0, tiled=True)
        outs.append(lax.psum_scatter(g, "rows", scatter_dimension=1, tiled=True).astype(jnp.float32))
    return outs


def doubling(place):
    steps = []
    for name, index, size in (("zl", place.zl, place.nzl), ("zh", place.zh, 2), ("c", place.c, 2), ("m", place.m, place.nd // 2)):
        bit = 1
        while bit < size:
            steps.append(({name: bit}, (index & bit) != 0))
            bit *= 2
    return steps


def joined(place, x, step):
    swap, upper = step
    return jnp.stack(by_xor([x, place.swap(x, **swap)], upper.astype(jnp.int32)))


def halved(place, x, step):
    swap, upper = step
    mine = by_xor([x[0], x[1]], upper.astype(jnp.int32))
    return add_low(mine[0], place.swap(mine[1], **swap))


def m_halved(place, x, steps, first):
    for step in [step for step in steps if "m" in step[0]]:
        if (step[0]["m"] == 1) == (first == 1):
            x = x.reshape((-1, 2) + x.shape[1:])
            x = halved(place, [x[:, k] for k in range(2)], step)
    return x


class Shape:
    def __init__(self, band_rows, columns, nr, width, out, pieces):
        self.band_rows, self.columns, self.nr, self.width, self.out = band_rows, columns, nr, width, out
        self.rows = band_rows * nr
        self.band, self.pixels = band_rows * columns, band_rows * columns * nr
        self.block = BLOCK_ROWS * columns
        self.blocks = self.rows // BLOCK_ROWS
        self.pieces = pieces
        self.quarter = out // 4

    def regions(self, dilation):
        cuts = sorted({0, min(dilation, self.rows), max(self.rows - dilation, 0), self.rows})
        for lo, hi in zip(cuts, cuts[1:]):
            yield lo, hi, [r for r in range(3) if 0 <= lo + (r - 1) * dilation and hi + (r - 1) * dilation <= self.rows]


ANY = pl.BlockSpec(memory_space=pl.ANY)
SMEM = pl.BlockSpec(memory_space=pltpu.SMEM)
VMEM = pl.BlockSpec(memory_space=pltpu.VMEM)
PARAMS = pltpu.CompilerParams(vmem_limit_bytes=58 * 2**20)
TINY = pltpu.CompilerParams(vmem_limit_bytes=8 * 2**20)
SMALL = pltpu.CompilerParams(vmem_limit_bytes=8 * 2**20)


LIGHT = pl.CostEstimate(flops=0, bytes_accessed=0, transcendentals=0)


def lanes_at(start, size=LANES):
    return pl.ds(pl.multiple_of(start, LANES), size)


def start_bands(shape, refs, scratch, sem, part):
    for k, ref in enumerate(refs):
        pltpu.make_async_copy(ref, scratch.at[pl.ds((part ^ k) * shape.band, shape.band), :], sem.at[k]).start()


def wait_bands(shape, refs, scratch, sem):
    for k, ref in enumerate(refs):
        pltpu.make_async_copy(ref, scratch.at[pl.ds(k * shape.band, shape.band), :], sem.at[k]).wait()


def split_features(shape, features, mask, c):
    tiles, n = shape.width // LANES, shape.nr // 2

    def kernel(info, x, mask_ref, *outs):
        valid = mask_ref[...].astype(jnp.bfloat16)
        for k, out in enumerate(outs):
            for q in range(n):
                for i in range(tiles):
                    at = (i * shape.nr + (info[0] ^ k) * n + q) * LANES
                    out[q, :, i * LANES : (i + 1) * LANES] = x[:, lanes_at(at)] * valid

    return pl.pallas_call(
        kernel,
        out_shape=[jax.ShapeDtypeStruct((n, shape.band, shape.width), jnp.bfloat16)] * 2,
        in_specs=[SMEM, VMEM, VMEM],
        out_specs=[VMEM] * 2,
        compiler_params=SMALL,
        cost_estimate=LIGHT,
        name="split_features",
    )(c.reshape(1), features, mask)


def join_features(shape, own, other, c, zl):
    tiles, n = shape.width // LANES, shape.nr // 2

    def kernel(info, *refs):
        for k, part in enumerate(refs[: 2 * n]):
            core, q = info[0] ^ (k // n), info[1] ^ (k % n)
            for i in range(tiles):
                at = (i * shape.nr + core * n + q) * LANES
                refs[2 * n][:, lanes_at(at)] = part[:, i * LANES : (i + 1) * LANES]

    return pl.pallas_call(
        kernel,
        out_shape=jax.ShapeDtypeStruct((shape.band, shape.width * shape.nr), jnp.bfloat16),
        in_specs=[SMEM] + [VMEM] * shape.nr,
        out_specs=VMEM,
        compiler_params=SMALL,
        cost_estimate=LIGHT,
        name="join_features",
    )(jnp.stack([c, zl]).astype(jnp.int32), *own, *other)


def packed_near(shape, zl, own, neighbour):
    size = shape.quarter

    def kernel(info, own, neighbour, out, rest):
        for kl, ref in enumerate((own, neighbour)):
            out[:, pl.ds(pl.multiple_of((info[0] ^ kl) * size, size), size), :] = ref[...]
        rest[: SLOTS - FIRST] = own[FIRST:]
        rest[SLOTS - FIRST :] = neighbour[...]

    return pl.pallas_call(
        kernel,
        out_shape=[
            jax.ShapeDtypeStruct((SLOTS, 2 * size, LANES), jnp.bfloat16),
            jax.ShapeDtypeStruct((2 * SLOTS - FIRST, size, LANES), jnp.bfloat16),
        ],
        in_specs=[SMEM, VMEM, VMEM],
        out_specs=[VMEM, VMEM],
        compiler_params=SMALL,
        cost_estimate=LIGHT,
        name="packed_near",
    )(zl.reshape(1), own, neighbour)


def packed_far(shape, zl, first, rest):
    size = shape.quarter

    def kernel(info, first, rest, out):
        for kl in range(2):
            columns = pl.ds(pl.multiple_of((info[0] ^ kl) * size, size), size)
            if kl == 0:
                out[:FIRST, columns, :] = first[...]
                out[FIRST:, columns, :] = rest[: SLOTS - FIRST]
            else:
                out[:, columns, :] = rest[SLOTS - FIRST :]

    return pl.pallas_call(
        kernel,
        out_shape=jax.ShapeDtypeStruct((SLOTS, 2 * size, LANES), jnp.bfloat16),
        in_specs=[SMEM, VMEM, VMEM],
        out_specs=VMEM,
        compiler_params=SMALL,
        cost_estimate=LIGHT,
        name="packed_far",
    )(zl.reshape(1), first, rest)


def chip_slot(t, c):
    return jnp.where(jnp.where(c == 0, t < FULL, t >= SHORT), t - SHORT * c, FULL + 2 + t - FULL * (1 - c))


def assembled_weights(shape, info, own, by_x, by_y, diagonal):
    def kernel(info, *refs):
        ins, out, sem = refs[:5], refs[5], refs[6]
        m, c = info[0], info[1]

        def copy(ref, slot, tap, lane):
            pltpu.make_async_copy(ref.at[slot], out.at[tap, :, lanes_at(lane)], sem).start()

        def place(rel, slot, tap, lane):
            if rel < 3:
                copy(ins[rel], slot, tap, lane)
            else:

                @pl.when(slot < CUT)
                def _():
                    copy(ins[3], slot, tap, lane)

                @pl.when(slot >= CUT)
                def _():
                    copy(ins[4], slot - CUT, tap, lane)

        for rel in range(4):
            chip = m ^ rel

            def body(t, carry):
                v = chip * PER_CHIP + t
                place(rel, chip_slot(t, c), v // 4, (v % 4) * LANES)
                return carry

            lax.fori_loop(0, PER_CHIP, body, 0)
            for extra in range(2):
                place(rel, FULL + extra, 27 + extra, chip * LANES)
        pltpu.make_async_copy(out, out, sem).wait()

    return pl.pallas_call(
        kernel,
        out_shape=jax.ShapeDtypeStruct((29, shape.out // 2, shape.width), jnp.bfloat16),
        in_specs=[SMEM] + [ANY] * 5,
        out_specs=VMEM,
        scratch_shapes=[pltpu.SemaphoreType.DMA],
        compiler_params=TINY,
        cost_estimate=LIGHT,
        name="assembled_weights",
    )(info, own, by_x, by_y, *diagonal)


def shifted(values, by, columns):
    if by == 0:
        return values
    pixels = values.shape[0]
    source = lax.broadcasted_iota(jnp.int32, (pixels, 1), 0) % columns - by
    return jnp.where((source >= 0) & (source < columns), pltpu.roll(values, by % pixels, 0), 0.0)


def send_halves(shape, c, kept, low, outs, sem):
    half = shape.pixels // 2
    copies = []
    for n, (source, core) in enumerate(((kept, c), (low, 1 - c))):
        rows = source.at[pl.ds(pl.multiple_of(core * half, half), half)]
        copies.append(pltpu.make_async_copy(rows, outs[n], sem.at[n]))
    for copy in copies:
        copy.start()
    for copy in copies:
        copy.wait()


def half_shapes(shape, n):
    half = shape.pixels // 2
    return [
        jax.ShapeDtypeStruct((half, n * shape.out), jnp.float32),
        jax.ShapeDtypeStruct((half, n * shape.out), jnp.bfloat16),
    ]


def start_taps(weights, scratch, sem, taps, zh):
    half = weights[0].shape[1]
    for n, tap in enumerate(taps):
        for kh, ref in enumerate(weights):
            columns = pl.ds(pl.multiple_of((zh ^ kh) * half, half), half)
            pltpu.make_async_copy(ref.at[tap], scratch.at[n, columns], sem.at[n]).start()


def wait_taps(scratch, sem, some):
    for n in some:
        pltpu.make_async_copy(scratch.at[n], scratch.at[n], sem.at[n]).wait()


def dilated_products(shape, branch, x, w, first, y):
    dilation, columns = dilations[branch], shape.columns
    for s in range(3):
        for lo, hi, rs in shape.regions(dilation):
            pixels = jnp.concatenate(
                [x[(lo + (r - 1) * dilation) * columns : (hi + (r - 1) * dilation) * columns, :] for r in rs], axis=1
            )
            taps = jnp.concatenate([w[first + 3 * s + r] for r in rs], axis=1)
            y[s, lo * columns : hi * columns, :] = dot(pixels, taps, NT)


def put_dilated(shape, branch, y, kept, low, lane):
    dilation, columns = dilations[branch], shape.columns
    for blk in range(shape.blocks):
        at = slice(blk * shape.block, (blk + 1) * shape.block)
        z = y[1, at, :] + shifted(y[0, at, :], dilation, columns) + shifted(y[2, at, :], -dilation, columns)
        kept[at, lane : lane + shape.out] = z
        low[at, lane : lane + shape.out] = z.astype(jnp.bfloat16)


def taps_of(branch):
    return [9 * branch + 3 * r + s for s in range(3) for r in range(3)]


def branch_sums(shape, info, area, bands, weights):
    nr = shape.nr

    def kernel(info, area, *refs):
        ins, weights = refs[:nr], refs[nr : nr + 2]
        keep, sent, pooled, lifted, x, w, y, kept, low_sums, band_sem, w_sem, out_sem = refs[nr + 2 :]
        start_bands(shape, ins, x, band_sem, info[5])
        start_taps(weights, w, w_sem, taps_of(2) + taps_of(1) + taps_of(0) + [27, 28], info[2])
        wait_bands(shape, ins, x, band_sem)
        wait_taps(w, w_sem, range(29))
        for n, branch in enumerate((2, 1, 0)):
            dilated_products(shape, branch, x, w, 9 * n, y.at[n % 2])
            put_dilated(shape, branch, y.at[n % 2], kept, low_sums, n * shape.out)
        z = dot(x[...], w[27], NT)
        kept[:, 3 * shape.out :] = z
        low_sums[:, 3 * shape.out :] = z.astype(jnp.bfloat16)
        sums = jnp.zeros((1, shape.width), jnp.float32)
        for blk in range(shape.blocks):
            values = x[blk * shape.block : (blk + 1) * shape.block, :]
            sums = sums + jnp.sum(values.astype(jnp.float32), axis=0, keepdims=True)
        low = jnp.broadcast_to(sums / area[0], pooled.shape).astype(jnp.bfloat16)
        first = lax.broadcasted_iota(jnp.int32, pooled.shape, 0) == 0
        pooled[...] = jnp.where(first, low.astype(jnp.float32), 0.0).astype(jnp.bfloat16)
        lifted[...] = dot(pooled[...], w[28], NT)
        send_halves(shape, info[1], kept, low_sums, (keep, sent), out_sem)

    return pl.pallas_call(
        kernel,
        out_shape=half_shapes(shape, 4)
        + [jax.ShapeDtypeStruct((16, shape.width), jnp.bfloat16), jax.ShapeDtypeStruct((16, shape.out), jnp.float32)],
        in_specs=[SMEM, SMEM] + [ANY] * (nr + 2),
        out_specs=[ANY] * 2 + [VMEM] * 2,
        scratch_shapes=[
            pltpu.VMEM((shape.pixels, shape.width), jnp.bfloat16),
            pltpu.VMEM((29, shape.out, shape.width), jnp.bfloat16),
            pltpu.VMEM((2, 3, shape.pixels, shape.out), jnp.float32),
            pltpu.VMEM((shape.pixels, 4 * shape.out), jnp.float32),
            pltpu.VMEM((shape.pixels, 4 * shape.out), jnp.bfloat16),
            pltpu.SemaphoreType.DMA((nr,)),
            pltpu.SemaphoreType.DMA((29,)),
            pltpu.SemaphoreType.DMA((2,)),
        ],
        compiler_params=PARAMS,
        cost_estimate=LIGHT,
        name="branch_sums",
    )(info, area, *bands, *weights)


def band_mask(shape, info):
    pixel = lax.broadcasted_iota(jnp.int32, (shape.band, 1), 0)
    row, column = info[4] * shape.band_rows + pixel // shape.columns, pixel % shape.columns
    return ((row < info[6]) & (column < info[7])).astype(jnp.float32)


def put_moments(values, mask, ref, at_sum, at_square, count):
    total = jnp.sum(values * mask, axis=0, keepdims=True)
    centred = (values - total / jnp.maximum(count, 1.0)) * mask
    ref[at_sum : at_sum + 1, :] = total
    ref[at_square : at_square + 1, :] = jnp.sum(centred * centred, axis=0, keepdims=True)


def merged_rows(refs, k, n):
    count = tree([ref[2 * n : 2 * n + 1, :] for ref in refs])
    mean = tree([ref[k : k + 1, :] for ref in refs]) / jnp.maximum(count, 1.0)
    between = []
    for ref in refs:
        own = ref[2 * n : 2 * n + 1, :]
        gap = ref[k : k + 1, :] / jnp.maximum(own, 1.0) - mean
        between.append(own * gap * gap)
    squares = tree([ref[n + k : n + k + 1, :] for ref in refs]) + tree(between)
    return mean, squares / count, count


def silu(v):
    return v * jax.nn.sigmoid(v)


def call(shape, kernel, name, outs, out_specs, in_specs, scratch=()):
    return pl.pallas_call(
        kernel,
        out_shape=[jax.ShapeDtypeStruct(*o) for o in outs],
        in_specs=in_specs,
        out_specs=out_specs,
        scratch_shapes=list(scratch),
        compiler_params=SMALL,
        cost_estimate=LIGHT,
        name=name,
    )


TABLE = 16


def branch_moments(shape, info, images, mine, others, lifted):
    n = len(others)

    def kernel(info, mine, lifted, *refs):
        others, (z, rows) = refs[:n], refs[n:]
        mask = band_mask(shape, info)
        count = jnp.sum(mask)
        rows[...] = jnp.zeros(rows.shape, jnp.float32)
        for k in range(4):
            lanes = slice((3 - k) * shape.out, (4 - k) * shape.out)
            value = mine[:, lanes]
            for other in others:
                value = value + other[:, lanes].astype(jnp.float32)
            z[:, k * shape.out : (k + 1) * shape.out] = value
            put_moments(value, mask, rows, k, 4 + k, count)
        rows[8:9, :] = jnp.full((1, shape.out), count, jnp.float32)
        rows[pl.ds(TABLE + 2 * info[0] + info[2], 1), :] = lifted[0:1, :]

    return call(
        shape,
        kernel,
        "branch_moments",
        [((shape.band, 4 * shape.out), jnp.float32), ((TABLE + images, shape.out), jnp.float32)],
        [VMEM] * 2,
        [SMEM] + [VMEM] * (2 + n),
    )(info, mine, lifted, *others)


def projected(shape, info, images, rows, z, projection, gain, bias):
    out = shape.out

    def kernel(info, z, projection, gain, bias, *refs):
        n = len(rows)
        rows_in, (concat, pre, moments, stats) = refs[:n], refs[n:]
        mask = band_mask(shape, info)
        pool = tree([ref[TABLE : TABLE + images, :] for ref in rows_in])
        pool = pool - jnp.sum(pool, axis=0, keepdims=True) / images
        pool_inv = lax.rsqrt(jnp.sum(pool * pool, axis=0, keepdims=True) / images + epsilon)
        pool = pool * pool_inv
        stats[9:10, :] = pool_inv
        stats[TABLE : TABLE + images, :] = pool
        stats[TABLE + images :, :] = gain[4:5, :] * pool + bias[4:5, :]
        for k in range(4):
            average, spread, count = merged_rows(rows_in, k, 4)
            inv = lax.rsqrt(spread + epsilon)
            stats[k : k + 1, :] = average
            stats[4 + k : 5 + k, :] = inv
            lanes = slice(k * out, (k + 1) * out)
            lifted = gain[k : k + 1, :] * ((z[:, lanes] - average) * inv) + bias[k : k + 1, :]
            concat[:, lanes] = (silu(lifted) * mask).astype(jnp.bfloat16)
        stats[8:9, :] = count
        line = stats[pl.ds(TABLE + images + 2 * info[0] + info[2], 1), :]
        concat[:, 4 * out :] = (silu(line) * mask).astype(jnp.bfloat16)
        value = dot(concat[...], projection[...], NT)
        pre[...] = value
        local = jnp.sum(mask)
        put_moments(value, mask, moments, 0, 1, local)
        moments[2:, :] = jnp.full((6, out), local, jnp.float32)

    return call(
        shape,
        kernel,
        "projected",
        [
            ((shape.band, 5 * out), jnp.bfloat16),
            ((shape.band, out), jnp.float32),
            ((8, out), jnp.float32),
            ((TABLE + 2 * images, out), jnp.float32),
        ],
        [VMEM] * 4,
        [SMEM] + [VMEM] * (4 + len(rows)),
    )(info, z, projection, gain, bias, *rows)


def branch_gradients(shape, info, images, rows, upstream, normed, inv, z, stats, projection, gain, bias):
    out = shape.out

    def kernel(info, upstream, normed, inv, z, stats, projection, gain, bias, *refs):
        n = len(rows)
        rows_in, (delta, up, sums, totals) = refs[:n], refs[n:]
        mask = band_mask(shape, info)
        whole = tree([ref[...] for ref in rows_in])
        totals[...] = whole
        count, scale = stats[8:9, :], gain[5:6, :]
        low = (
            mask
            * inv[...]
            * (scale * upstream[...] - scale * whole[1:2] / count - normed[...] * scale * whole[0:1] / count)
        ).astype(jnp.bfloat16)
        delta[...] = low
        sums[...] = jnp.zeros(sums.shape, jnp.float32)
        for k in range(4):
            lanes = slice(k * out, (k + 1) * out)
            at = (z[:, lanes] - stats[k : k + 1, :]) * stats[4 + k : 5 + k, :]
            slope = silu_slope(gain[k : k + 1, :] * at + bias[k : k + 1, :])
            value = dot(low, projection[:, lanes], NN) * mask * slope
            up[:, lanes] = value
            sums[k : k + 1, :] = jnp.sum(value * at, axis=0, keepdims=True)
            sums[4 + k : 5 + k, :] = jnp.sum(value, axis=0, keepdims=True)
        line = jnp.sum(dot(low, projection[:, 4 * out :], NN) * mask, axis=0, keepdims=True)
        sums[pl.ds(8 + 2 * info[0] + info[2], 1), :] = line

    return call(
        shape,
        kernel,
        "branch_gradients",
        [
            ((shape.band, out), jnp.bfloat16),
            ((shape.band, 4 * out), jnp.float32),
            ((8 + images, out), jnp.float32),
            ((8, out), jnp.float32),
        ],
        [VMEM] * 4,
        [SMEM] + [VMEM] * (8 + len(rows)),
    )(info, upstream, normed, inv, z, stats, projection, gain, bias, *rows)


def branch_deltas(shape, info, rows, up, z, stats, gain):
    out, half = shape.out, shape.out // 2

    def kernel(info, up, z, stats, gain, *refs):
        n = len(rows)
        rows_in, (delta, crossing, totals) = refs[:n], refs[n:]
        mask = band_mask(shape, info)
        totals[...] = tree([ref[...] for ref in rows_in])
        count = stats[8:9, :]
        for k in range(4):
            lanes = slice(k * out, (k + 1) * out)
            inv, scale = stats[4 + k : 5 + k, :], gain[k : k + 1, :]
            at = (z[:, lanes] - stats[k : k + 1, :]) * inv
            by_gain, by_bias = totals[k : k + 1, :], totals[4 + k : 5 + k, :]
            value = mask * inv * (scale * up[:, lanes] - scale * by_bias / count - at * scale * by_gain / count)
            delta[:, lanes] = value.astype(jnp.bfloat16)
            crossing[:, k * half : (k + 1) * half] = delta[:, lanes_at(k * out + (1 - info[2]) * half, half)]

    return call(
        shape,
        kernel,
        "branch_deltas",
        [
            ((shape.band, 4 * out), jnp.bfloat16),
            ((shape.band, 4 * half), jnp.bfloat16),
            (rows[0].shape, jnp.float32),
        ],
        [VMEM] * 3,
        [SMEM] + [VMEM] * (4 + len(rows)),
    )(info, up, z, stats, gain, *rows)


def moved_columns(shape, delta, lane, lanes, branch, moved):
    for blk in range(shape.blocks):
        at = slice(blk * shape.block, (blk + 1) * shape.block)
        values = delta[at, lanes_at(lane, lanes)].astype(jnp.float32)
        for s in range(3):
            moved[at, s * lanes : (s + 1) * lanes] = shifted(
                values, (s - 1) * dilations[branch], shape.columns
            ).astype(jnp.bfloat16)


def input_gradient(shape, info, area, deltas, pool_delta, weights):
    nr, columns = shape.nr, shape.columns

    def kernel(info, area, *refs):
        ins, pool_delta, weights = refs[:nr], refs[nr], refs[nr + 1 : nr + 3]
        outs = refs[nr + 3 : 2 * nr + 3]
        delta, moved, w, acc, delta_sem, w_sem = refs[2 * nr + 3 :]
        start_bands(shape, ins, delta, delta_sem, info[4])
        start_taps(weights, w, w_sem, range(29), info[2])
        wait_bands(shape, ins, delta, delta_sem)
        wait_taps(w, w_sem, range(29))
        pool = dot(pool_delta[...], w[28], NN)[0:1] / area[0]
        acc[...] = dot(delta[:, : shape.out], w[27], NN) + pool
        for branch in range(3):
            dilation = dilations[branch]
            moved_columns(shape, delta, (branch + 1) * shape.out, shape.out, branch, moved)
            for lo, hi, rs in shape.regions(dilation):
                rows = [2 - r for r in rs]
                cut = lambda r: moved[(lo - (r - 1) * dilation) * columns : (hi - (r - 1) * dilation) * columns, :]
                pixels = jnp.concatenate([cut(r) for r in rows], axis=1)
                taps = jnp.concatenate([w[9 * branch + 3 * r + s] for r in rows for s in range(3)], axis=0)
                acc[lo * columns : hi * columns, :] += dot(pixels, taps, NN)
        pixel = lax.broadcasted_iota(jnp.int32, (shape.band, 1), 0)
        for k in range(nr):
            first = (info[5] ^ k) * shape.band
            inside = ((pixel + first) // columns < info[6]) & (pixel % columns < info[7])
            values = acc[pl.ds(pl.multiple_of(first, shape.band), shape.band), :]
            outs[k][...] = jnp.where(inside, values, 0.0).astype(jnp.bfloat16)

    return pl.pallas_call(
        kernel,
        out_shape=[jax.ShapeDtypeStruct((shape.band, shape.width), jnp.bfloat16)] * nr,
        in_specs=[SMEM, SMEM] + [ANY] * nr + [VMEM] + [ANY] * 2,
        out_specs=[VMEM] * nr,
        scratch_shapes=[
            pltpu.VMEM((shape.pixels, 4 * shape.out), jnp.bfloat16),
            pltpu.VMEM((shape.pixels, 3 * shape.out), jnp.bfloat16),
            pltpu.VMEM((29, shape.out, shape.width), jnp.bfloat16),
            pltpu.VMEM((shape.pixels, shape.width), jnp.float32),
            pltpu.SemaphoreType.DMA((nr,)),
            pltpu.SemaphoreType.DMA((29,)),
        ],
        compiler_params=PARAMS,
        cost_estimate=pl.CostEstimate(
            flops=44 * shape.pixels * shape.width * shape.out, bytes_accessed=2**24, transcendentals=0
        ),
        name="input_gradient",
    )(info, area, *deltas, pool_delta, *weights)


def weight_gradients(shape, info, bands, far_bands, deltas, far_deltas, pool_deltas, pooled):
    nr, columns, half = shape.nr, shape.columns, shape.out // 2
    n_outs = 8 if shape.pieces else 1
    by_rows = lambda v: v.reshape(v.shape[0] // columns, columns, v.shape[1])
    bands = [by_rows(band) for band in [*bands, *far_bands]]

    def kernel(info, *refs):
        ins, delta_ins, far_delta_ins = (refs[n * nr : (n + 1) * nr] for n in range(3))
        far_ins, refs = refs[3 * nr : 4 * nr], refs[4 * nr :]
        pool_deltas, pooled, outs = refs[0], refs[1], refs[2 : 2 + n_outs]
        x, delta, far_delta, moved, grads, sem, out_sem = refs[2 + n_outs :]
        m, c, zh, part, z = info[0], info[1], info[2], info[4], info[5]
        rows = shape.band_rows
        start_bands(shape, delta_ins, delta, sem.at[0], part)
        start_bands(shape, far_delta_ins, far_delta, sem.at[1], part)
        for image, sources in enumerate((ins, far_ins)):
            for k, ref in enumerate(sources):
                pltpu.make_async_copy(ref, x.at[pl.ds((z ^ k) * rows, rows), image], sem.at[2 + image, k]).start()

        def arrive(n):
            for k in range(nr):
                if n < 2:
                    some = (delta, far_delta)[n].at[pl.ds(k * shape.band, shape.band)]
                else:
                    some = x.at[pl.ds(k * rows, rows), n - 2]
                pltpu.make_async_copy(some, some, sem.at[n, k]).wait()

        def move(branch):
            for image, source in enumerate((delta, far_delta)):
                lane = (branch + 1) * half if image else (branch + 1) * shape.out + zh * half
                for blk in range(shape.blocks):
                    at = slice(blk * shape.block, (blk + 1) * shape.block)
                    values = source[at, lanes_at(lane, half)].astype(jnp.float32)
                    for s in range(3):
                        value = shifted(values, (s - 1) * dilations[branch], columns).astype(jnp.bfloat16)
                        moved[blk * BLOCK_ROWS : (blk + 1) * BLOCK_ROWS, image, :, s * half : (s + 1) * half] = (
                            value.reshape(BLOCK_ROWS, columns, half)
                        )

        flat = lambda v: v.reshape(-1, v.shape[-1])

        def put(tap, value):
            value = value.astype(jnp.bfloat16)
            if not shape.pieces:
                grads[tap] = value
                return
            for i in range(4):
                if tap < 27:
                    v = 4 * tap + i
                    chip, slot = v // PER_CHIP, chip_slot(v % PER_CHIP, c)
                else:
                    chip, slot = i, FULL + tap - 27
                for q in range(2):
                    rows = slice(q * shape.quarter, (q + 1) * shape.quarter)
                    grads[2 * (m ^ chip) + q, slot] = value[rows, i * LANES : (i + 1) * LANES]

        arrive(0)
        arrive(1)
        for branch in range(3):
            move(branch)
            if branch == 0:
                arrive(2)
                arrive(3)
            dilation = dilations[branch]
            for r in range(3):
                up, down = max(0, 1 - r) * dilation, max(0, r - 1) * dilation
                to = flat(moved[up : shape.rows - down])
                value = dot(to, flat(x[down : shape.rows - up]), TN)
                for s in range(3):
                    put(9 * branch + 3 * r + s, value[s * half : (s + 1) * half])
        one = jnp.concatenate(
            [
                delta[:, lanes_at(zh * half, half)].reshape(shape.rows, 1, columns, half),
                far_delta[:, :half].reshape(shape.rows, 1, columns, half),
            ],
            axis=1,
        )
        put(27, dot(flat(one), flat(x[...]), TN))
        put(28, dot(pool_deltas[...], pooled[...], TN))
        copies = [pltpu.make_async_copy(grads.at[n] if shape.pieces else grads, outs[n], out_sem.at[n]) for n in range(n_outs)]
        for copy in copies:
            copy.start()
        for copy in copies:
            copy.wait()

    if shape.pieces:
        out_shape = [jax.ShapeDtypeStruct((SLOTS, shape.quarter, LANES), jnp.bfloat16)] * 8
        grads_shape = (8, SLOTS, shape.quarter, LANES)
    else:
        out_shape = [jax.ShapeDtypeStruct((29, half, shape.width), jnp.bfloat16)]
        grads_shape = (29, half, shape.width)
    return pl.pallas_call(
        kernel,
        out_shape=out_shape,
        in_specs=[SMEM] + [ANY] * (4 * nr) + [VMEM] * 2,
        out_specs=[ANY] * n_outs,
        scratch_shapes=[
            pltpu.VMEM((shape.rows, 2, columns, shape.width), jnp.bfloat16),
            pltpu.VMEM((shape.pixels, 4 * shape.out), jnp.bfloat16),
            pltpu.VMEM((shape.pixels, 2 * shape.out), jnp.bfloat16),
            pltpu.VMEM((shape.rows, 2, columns, 3 * half), jnp.bfloat16),
            pltpu.VMEM(grads_shape, jnp.bfloat16),
            pltpu.SemaphoreType.DMA((4, nr)),
            pltpu.SemaphoreType.DMA((n_outs,)),
        ],
        compiler_params=PARAMS,
        cost_estimate=pl.CostEstimate(
            flops=44 * shape.pixels * shape.width * shape.out, bytes_accessed=2**24, transcendentals=0
        ),
        name="weight_gradients",
    )(info, *bands[:nr], *deltas, *far_deltas, *bands[nr:], pool_deltas, pooled)


def valid_pixels(extent, first_row, rows, columns):
    r = first_row + lax.broadcasted_iota(jnp.int32, (rows, columns), 0)
    w = lax.broadcasted_iota(jnp.int32, (rows, columns), 1)
    return ((r < extent[0]) & (w < extent[1])).astype(jnp.float32).reshape(rows * columns, 1)


def to_logical(place, x):
    return jnp.where(place.zh == place.c, x, place.swap(x, c=1, zh=1))


def on_device(
    features, extent, pointwise_weight, pooling_weight, dilated_weight, projection_weight, norm_gain, norm_bias, cotangent
):
    place = Place()
    nr, nzl = place.nr, place.nzl
    _, band_rows, columns, channels = features.shape
    width, out = channels // nr, norm_gain.shape[1]
    band = band_rows * columns
    pieces = nr == 4 and place.nd == 8 and dilated_weight.shape[0] == 2 * PER_CHIP * LANES
    shape = Shape(band_rows, columns, nr, width, out, pieces)
    images = place.nd

    partner = place.swap(extent, c=1)
    extent_here = jnp.where(place.zh == place.c, extent, partner)[0]
    area = (extent_here[0] * extent_here[1]).astype(jnp.float32)
    mask = valid_pixels(extent_here, place.part * band_rows, band_rows, columns)
    own_mask = valid_pixels(extent[0], place.z * band_rows, band_rows, columns)
    here_now = [place.m, place.c, place.zh, place.zl, place.part, place.z, extent_here[0], extent_here[1]]
    info = jnp.stack(here_now).astype(jnp.int32)
    areas = area.reshape(1)

    own_parts, other_parts = split_features(shape, features.reshape(band, channels), own_mask, place.c)
    held = by_xor([own_parts, place.swap(other_parts, c=1)], place.c)
    held = [by_xor([v[q] for q in range(nzl)], place.zl) for v in by_xor(held, place.zh)]

    def sent(image, k, first=()):
        kh, kl = divmod(k, nzl)
        v = held[kh ^ image][kl]
        return place.swap(after(v, first), zh=kh, zl=kl) if k else v

    steps = doubling(place)
    nd_bits = (place.nd // 2).bit_length() - 1
    projection = projection_weight.T
    if pieces:
        sources = line_pieces(place, dilated_weight, pointwise_weight, pooling_weight)
        crossed = place.swap(sources[0][:FIRST], zh=1)
        neighbour = after(place.swap(sources[1], zl=1), crossed, own_parts, other_parts, partner)
        near, rest = packed_near(shape, place.zl, sources[0], neighbour)
        rest = place.swap(rest, zh=1)
        near_x, near_y = plane_direct(place, near)
        near_d = plane_diagonal(place, near_x, near_y)
        far = packed_far(shape, place.zl, crossed, after(rest, near_d, held))
        crossing_band = sent(0, nzl, first=far)
        far_x, far_y = after(plane_direct(place, far), crossing_band)
        far_d = plane_diagonal(place, far_x, far_y)
        bands = [sent(0, k, first=far_x) for k in range(nzl)] + [crossing_band]
        bands += [sent(0, k, first=crossing_band) for k in range(nzl + 1, nr)]
        near = assembled_weights(shape, info, near, near_x, near_y, near_d)
        weights = [near, assembled_weights(shape, info, far, far_x, far_y, after(far_d, near))]
    else:
        bands = [sent(0, k) for k in range(nr)]
        weights = gathered_tiles(place, dilated_weight, pointwise_weight, pooling_weight)
        weights = by_xor([weights[:, : out // 2], weights[:, out // 2 :]], place.zh)

    def given_on(keep, got):
        bands_of = lambda v: v.reshape(nzl, band, v.shape[1])
        at = lambda k: [lax.dynamic_index_in_dim(bands_of(v), place.zl ^ k, 0, keepdims=False) for v in (keep, got)]
        summed = lambda k: at(k)[0] + at(k)[1].astype(jnp.float32)
        return summed(0), [place.swap(summed(k).astype(jnp.bfloat16), zl=k) for k in range(1, nzl)]

    ready = (bands, weights)
    keep, given, pooled, lifted = branch_sums(shape, info, areas, bands, weights)
    far_bands = [sent(1, k, first=ready) for k in range(nzl + 1)]
    projection = after(projection, ready)
    projection = joined(place, projection, steps[-nd_bits - 2])
    given = after(given, far_bands, projection)
    projection = after(projection, given)
    for step in steps[: -nd_bits - 2]:
        projection = joined(place, projection, step)
    got, projection = after((place.swap(given, c=1), projection), projection)
    projection = joined(place, projection, steps[-nd_bits - 1])
    upstream_low = to_logical(place, after(cotangent.reshape(band, out), got))
    plane = [projection] + [place.swap(projection, m=k) for k in range(1, images // 2)]
    mine, others = given_on(keep, got)
    projection = jnp.stack(by_xor(plane, place.m))
    projection = projection.reshape((images // 2, 2, nzl, 2) + projection_weight.shape[::-1])
    projection = jnp.transpose(projection, (3, 2, 4, 0, 1, 5)).reshape(out, -1)
    mine, others = after((mine, others), projection, upstream_low)
    z, rows = branch_moments(shape, info, images, mine, others, lifted)
    rows = exchanged(place, rows, lambda xs: merged(xs, 4))
    concat, proj_pre, rows, stats = projected(shape, info, images, rows, z, projection, norm_gain, norm_bias)
    pooled_far = place.swap(pooled, zh=1)
    rows = merged(exchanged(place, rows, lambda xs: merged(xs, 1)), 1)
    proj_average, proj_spread = rows[0:1] / rows[2:3], rows[1:2] / rows[2:3]
    proj_inv = lax.rsqrt(proj_spread + epsilon)
    proj_normed = (proj_pre - proj_average) * proj_inv
    proj_lift = norm_gain[5:6] * proj_normed + norm_bias[5:6]
    output_here = (jax.nn.silu(proj_lift) * mask).astype(jnp.bfloat16)

    upstream = upstream_low.astype(jnp.float32) * mask * silu_slope(proj_lift)
    sums = [jnp.sum(upstream * proj_normed, axis=0, keepdims=True), jnp.sum(upstream, axis=0, keepdims=True)]
    rows = exchanged(place, jnp.concatenate(sums + [jnp.zeros((6, out), jnp.float32)], axis=0), tree)
    proj_delta, branch_up, rows, proj_totals = branch_gradients(
        shape, info, images, rows, upstream, proj_normed, proj_inv, z, stats, projection, norm_gain, norm_bias
    )
    projection_partial = lambda first: dot(after(proj_delta, first), concat, TN)
    rows = exchanged(place, rows, tree)
    delta, crossing, totals = branch_deltas(shape, info, after(rows, pooled_far), branch_up, z, stats, norm_gain)
    proj_gain_grad, proj_bias_grad = proj_totals[0:1], proj_totals[1:2]
    branch_gain_grad, branch_bias_grad = totals[:4], totals[4:8]
    pool_inv, pool_normed, pool_lift = stats[9:10], stats[TABLE : TABLE + images], stats[TABLE + images :]
    here = lambda rows: lax.dynamic_slice_in_dim(rows, place.image, 1, axis=0)
    pool_up = totals[8:] * silu_slope(pool_lift)
    pool_gain_grad = jnp.sum(pool_up * pool_normed, axis=0, keepdims=True)
    pool_bias_grad = jnp.sum(pool_up, axis=0, keepdims=True)
    pool_deltas = pool_inv * (
        norm_gain[4:5] * pool_up
        - norm_gain[4:5] * pool_bias_grad / images
        - pool_normed * norm_gain[4:5] * pool_gain_grad / images
    )
    low_rows = lambda rows: jnp.pad(rows, ((0, 16 - rows.shape[0]), (0, 0))).astype(jnp.bfloat16)
    pool_pair = lax.dynamic_slice_in_dim(pool_deltas, 2 * place.m, 2, axis=0)
    halves = lambda v, n: by_xor([v[:, n * out : n * out + out // 2], v[:, n * out + out // 2 : (n + 1) * out]], place.zh)
    def over_group(v, first):
        near = [v] + [after(place.swap(v, zl=k), first) for k in range(1, nzl)]
        return near + [place.swap(n, c=1) for n in near]

    crossing = place.swap(crossing, zh=1)
    rows = projection_weight.shape[0]
    part = projection_partial(delta).astype(jnp.bfloat16).reshape(out, images // 2, 2, rows)
    part = jnp.transpose(part, (2, 1, 0, 3)).reshape(2, images // 2, 2, nzl, out // nr, rows)
    part = halved(place, [part[k] for k in range(2)], steps[-nd_bits - 1])
    spread_deltas = over_group(delta, (crossing, part))
    part = m_halved(place, after(part, spread_deltas), steps, 1)
    far_deltas = [crossing] + [place.swap(crossing, zl=k) for k in range(1, nzl)]
    inputs = input_gradient(shape, info, areas, spread_deltas, low_rows(here(pool_deltas)), weights)

    far_bands += [sent(1, k, first=spread_deltas) for k in range(nzl + 1, nr)]
    crossing = after(far_deltas, inputs, far_bands)
    pooled_pair = pooled + jnp.roll(pooled_far, 1, axis=0)
    pool_pair = jnp.concatenate([pool_pair[i : i + 1] for i in range(2)], axis=0)
    pool_pair = jnp.concatenate(by_xor([pool_pair[0:1], pool_pair[1:2]], place.zh), axis=0)
    pool_pair = halves(low_rows(pool_pair), 0)[0]
    far_deltas = crossing + [place.swap(n, c=1) for n in crossing]
    grads = weight_gradients(shape, info, bands, far_bands, spread_deltas, far_deltas, pool_pair, pooled_pair)

    done = (far_deltas, far_bands, part)
    handed = [place.swap(after(inputs[nzl + k], done), zh=1) for k in range(1, nzl)]
    near_handed = [place.swap(after(inputs[k], done), zl=k) for k in range(1, nzl)]
    output = to_logical(place, after(output_here, inputs))
    part = m_halved(place, after(part, inputs), steps, 2)
    crossed = (handed, near_handed, output, part)
    if pieces:
        pairs = [[grads[2 * rel], grads[2 * rel + 1]] for rel in range(4)]
        first_d, second_d = plane_scatter_diagonal(place, pairs)
        first_d, second_d = after((first_d, second_d), crossed, part)
        quarters = plane_scatter(place, pairs, first_d, second_d)
    else:
        quarters = grads
    part, last = after((part, inputs[nzl]), crossed)
    part = part.reshape((2, nzl) + part.shape[-2:])
    part = halved(place, [part[k] for k in range(2)], steps[-nd_bits - 2])
    last = place.swap(last, zh=1)
    handed = [place.swap(after(handed[k - 1], near_handed), zl=k) for k in range(1, nzl)]
    returned = by_xor([[inputs[0]] + near_handed, [last] + handed], place.zh)
    quarters = after(quarters, part, output, returned)
    returned = by_xor(returned, place.c)
    traded = place.swap(jnp.stack(returned[1]), c=1)
    feature_gradient = join_features(shape, returned[0], [traded[k] for k in range(nzl)], place.c, place.zl)
    if pieces:
        dilated_gradient, pointwise_gradient, pooling_gradient = line_back(place, quarters, feature_gradient)
    else:
        dilated_gradient, pointwise_gradient, pooling_gradient = scattered_tiles(place, quarters[0])
    part = after(part, feature_gradient)
    for step in [step for step in steps if "zl" in step[0]]:
        part = part.reshape((-1, 2) + part.shape[-2:])
        part = halved(place, [part[:, k] for k in range(2)], step)
    projection_gradient = part.reshape(out // nr, rows).astype(jnp.float32).T

    return (
        output.reshape(cotangent.shape),
        feature_gradient.reshape(features.shape),
        pointwise_gradient,
        pooling_gradient,
        dilated_gradient,
        projection_gradient,
        jnp.concatenate([branch_gain_grad, pool_gain_grad, proj_gain_grad], axis=0),
        jnp.concatenate([branch_bias_grad, pool_bias_grad, proj_bias_grad], axis=0),
    )


def solution(mesh):
    banded = P("dp", "rows", None, None)
    blocks = P("dp", "rows")
    return jax.shard_map(
        on_device,
        mesh=mesh,
        in_specs=(banded, P("dp", None), blocks, blocks, blocks, blocks, P(), P(), banded),
        out_specs=(banded, banded, blocks, blocks, blocks, blocks, P(), P()),
        check_vma=False,
    )
```
